128 devices in a mesh: dom: 32 (over y, x, core), rep: 4 (over z).
Axes of the slice: x: 4, y: 4, z: 4, core: 2. Of those that a mesh axis runs over, the one named last changes fastest.
Arguments:
- features: bfloat16 [4, 65536, 512], P('rep', 'dom'), may hold values from -6 to 6
- w_self: bfloat16 [512, 512], replicated, may hold values from -0.25 to 0.25
- w_neigh: bfloat16 [512, 512], replicated, may hold values from -1 to 1
- out_bias: float32 [512], replicated, may hold values from -3 to 3
- cluster_plan: int32 [512], P('dom'), may hold values from 0 to 511, as said below
- local_source: int32 [512, 3], P('dom'), may hold values from 0 to 15
- halo_owner: int32 [512, 2], P('dom'), may hold values from 0 to 31, all different within a row; in each aligned block of 16 rows (0 to 15, 16 to 31, ...) at most 2 rows name the same one
- halo_local: int32 [512, 2], P('dom'), may hold values from 0 to 15
- adjacency: bfloat16 [512, 5, 128, 128], P('dom'), may hold values from 0 to 1, as said below
- cotangent: bfloat16 [4, 65536, 512], P('rep', 'dom'), may hold values from -6 to 6
Outputs:
- new_features: bfloat16 [4, 65536, 512], P('rep', 'dom')
- feature_grad: bfloat16 [4, 65536, 512], P('rep', 'dom')
- w_self_grad: float32 [512, 512], replicated
- w_neigh_grad: float32 [512, 512], replicated
- bias_grad: float32 [512], replicated
The draws below stay inside these ranges and needn't reach their ends.
Inputs may be any that keep to these rules, and one draw needn't show every extreme that they name: `cluster_plan`: cluster c has home partition c // 16. Every cluster stands in exactly one slot. The first 13 slots of every partition hold its own clusters in home order; its slot 13 + j holds the cluster of the same home index on the partition o_j positions further along dom (cyclically), with o_j nonzero and different for different j and the same for all partitions. `halo_owner`: each row names 2 different partitions; the 16 rows of one partition name one partition at most 2 times. `adjacency`: entries are 0 or 1.
All inputs are finite; a program needn't handle non-finite values.
Results may differ from the reference program's by a relative error of at most 0.0059.
Values may be sent and summed in bfloat16 or wider, within the bound.
A program may use at most 192 MiB of HBM per device.

```python
import math
import jax
import jax.numpy as jnp
import numpy as np
from jax import lax

D = 512
TILE = 128
CL = 16
KL = 3
KH = 2
MIG = 3
HCAP = 2
REPS = 4
SLOTS = 512
NODES = 65536
N_DOM = 32
N_REP = 4


def draw_cluster_plan(key, part):
    key = jax.random.fold_in(key, 11)
    key_pick, key_order = jax.random.split(key)
    extra = jax.random.randint(key_pick, (), 1, N_DOM - 2).astype(jnp.int32)
    extra = jnp.where(extra >= N_DOM // 2, extra + 1, extra).astype(jnp.int32)
    base = jnp.stack([jnp.int32(N_DOM // 2), jnp.int32(N_DOM - 1), extra]).astype(jnp.int32)
    offsets = base[jax.random.permutation(key_order, 3)].astype(jnp.int32)
    device = jnp.arange(N_DOM, dtype=jnp.int32)[:, None]
    column = jnp.arange(CL, dtype=jnp.int32)[None, :]
    moved = column >= CL - MIG
    which = jnp.clip(column - (CL - MIG), 0, MIG - 1)
    source_device = jnp.where(moved, (device + offsets[which]) % N_DOM, device)
    return (source_device * CL + column).reshape(-1).astype(jnp.int32)


def draw_adjacency(key, part):
    key = jax.random.fold_in(key, 23)
    noise = jax.random.uniform(key, (N_DOM * CL, KL + KH, TILE, TILE), jnp.float32)
    density = 0.125
    return jnp.where(noise < density, 1.0, 0.0).astype(jnp.float32).astype(jnp.bfloat16)


def plant(result, own_key, low, top_value):
    extent = result.shape
    spot = [jax.random.randint(jax.random.fold_in(own_key, axis), (), 0, extent[axis]) for axis in range(len(extent))]
    result = result.at[tuple(spot)].set(low)
    longest = extent.index(max(extent))
    spot[longest] = (spot[longest] + 1) % extent[longest]
    return result.at[tuple(spot)].set(top_value)


def level_of(own_key, shape, pieces, least, top_value):
    def one(position, blocks):
        draws = jax.random.uniform(jax.random.fold_in(jax.random.fold_in(own_key, 6), position), (blocks,), jnp.float32, least / len(pieces), top_value / len(pieces))
        return jnp.repeat(jnp.exp(draws), shape[position] // blocks).reshape((-1,) + (1,) * (len(shape) - position - 1))

    gain = one(*pieces[0])
    for cut in pieces[1:]:
        gain = gain * one(*cut)
    return gain


def deal_out(own_key, own, number, rows, number_of, top, reach, skew):
    order = jax.random.permutation(own_key, number_of)
    crowded, ordinary = portions_of(number_of, rows * top, reach, skew, True), portions_of(number_of, rows * top, reach, skew, False)
    places = jnp.arange(number_of)

    def named(tallies, rotation):
        used = int((tallies > 0).sum())
        fixed = max(1, used // 4)
        moved = fixed + (places - fixed + rotation * (used - fixed)) % max(1, number_of - fixed)
        return jnp.zeros((number_of,), jnp.int32).at[order[jnp.where(places < fixed, places, moved)]].set(jnp.asarray(tallies, jnp.int32))

    tallies = jnp.where(number % 4 == 0, named(crowded, number // 4), named(ordinary, number - number // 4 - 1))
    mixed = jax.random.permutation(jax.random.fold_in(own, 3), number_of)
    source_of, taker = mixed[0:number_of // 2 * 2:2], mixed[1:number_of // 2 * 2:2]
    margin = jnp.minimum(tallies[source_of] - 1, reach - tallies[taker]) // 2
    margin = jnp.where((source_of == order[0]) | (taker == order[0]) | (tallies[taker] == 0), 0, jnp.maximum(margin, 0))
    moved = jax.random.randint(jax.random.fold_in(own, 4), (number_of // 2,), 0, 1 << 20) % (margin + 1)
    tallies = tallies.at[source_of].add(-moved).at[taker].add(moved)
    labels = jnp.searchsorted(jnp.cumsum(tallies), jnp.arange(rows * top), side="right").astype(jnp.int32)
    grid = labels.reshape(top, rows).T
    grid = grid[jax.random.permutation(jax.random.fold_in(own, 1), rows)]
    rotation = jax.random.randint(jax.random.fold_in(own, 2), (rows, 1), 0, top)
    return jnp.take_along_axis(grid, (jnp.arange(top)[None, :] + rotation) % top, axis=1)


def portions_of(number_of, total, most, skew, full):
    portions = [(1 << 20) // math.isqrt(standing ** skew) + 1 for standing in range(1, number_of + 1)]
    largest = most if full else min(most, max(-(-total // number_of), total * portions[0] // sum(portions)))
    least = 1 if total - largest >= number_of - 1 else 0
    holding, surplus = [largest] + [least] * (number_of - 1), total - largest - least * (number_of - 1)
    while surplus > 0:
        candidates = [i for i in range(1, number_of) if holding[i] < largest] or [i for i in range(1, number_of) if holding[i] < most]
        pool, remaining = sum([portions[i] for i in candidates]), surplus
        for i in candidates:
            more = min(most - holding[i], max(1, remaining * portions[i] // pool), surplus)
            holding[i] = holding[i] + more
            surplus = surplus - more
    return np.array(holding)


def normal_values(rng, extent, spread, most, cuts=(), held_as=jnp.bfloat16):
    values = jax.random.normal(rng, extent, jnp.float32) * spread
    if len(cuts) > 0:
        values = level_of(rng, extent, cuts, -0.22, 0.18) * values
    return jnp.clip(values, min=-most, max=most).astype(held_as)


def setup_inputs(seed: int = 0) -> dict:
    key_of = jax.random.split(jax.random.key(seed), 11)
    features = normal_values(key_of[0], (REPS, NODES, D), 1.0, 6.0, ((0, 4), (1, 32)))
    w_self = normal_values(key_of[1], (D, D), D ** -0.5, 0.25)
    w_neigh = normal_values(key_of[2], (D, D), (D // 16) ** -0.5, 1.0)
    out_bias = normal_values(key_of[3], (D,), 0.5, 3.0, (), jnp.float32)
    cluster_plan = draw_cluster_plan(jax.random.fold_in(key_of[10], 71), 0)
    local_source = plant(jax.random.randint(key_of[5], (SLOTS, KL), 0, CL), jax.random.fold_in(key_of[5], 1), 0, CL - 1).astype(jnp.int32)
    halo_owner_keys = jax.random.split(jax.random.fold_in(key_of[6], 1), SLOTS // CL)
    halo_owner_turns = jax.random.permutation(jax.random.fold_in(key_of[6], 3), SLOTS // CL)
    halo_owner = jax.vmap(lambda own, number: deal_out(jax.random.fold_in(key_of[6], 2), own, number, CL, N_DOM, KH, HCAP, 2))(halo_owner_keys, halo_owner_turns).reshape((SLOTS, KH))
    halo_local = plant(jax.random.randint(key_of[7], (SLOTS, KH), 0, CL), jax.random.fold_in(key_of[7], 1), 0, CL - 1).astype(jnp.int32)
    adjacency = draw_adjacency(jax.random.fold_in(key_of[10], 71), 0)
    cotangent = normal_values(key_of[9], (REPS, NODES, D), 1.0, 6.0, ((0, 4), (1, 32)))
    return dict(features=features, w_self=w_self, w_neigh=w_neigh, out_bias=out_bias, cluster_plan=cluster_plan, local_source=local_source, halo_owner=halo_owner, halo_local=halo_local, adjacency=adjacency, cotangent=cotangent)


def reference(features, w_self, w_neigh, out_bias, cluster_plan, local_source, halo_owner, halo_local, adjacency, cotangent):
    slot_device = jnp.arange(SLOTS, dtype=jnp.int32) // CL
    source = jnp.concatenate([slot_device[:, None] * CL + local_source, halo_owner * CL + halo_local], axis=1).astype(jnp.int32)
    degree = lax.optimization_barrier(jnp.sum(adjacency.astype(jnp.float32), axis=(1, 3)))
    scale = 1.0 / (1.0 + degree)
    dws_total = jnp.zeros((D, D), jnp.float32)
    dwn_total = jnp.zeros((D, D), jnp.float32)
    bias_total = jnp.zeros((D,), jnp.float32)
    outputs = []
    grads = []
    for replica in range(N_REP):
        clusters_in = features[replica].reshape(SLOTS, TILE, D)
        grad_out = cotangent[replica].reshape(SLOTS, TILE, D)

        def step(carry, block):
            grad_home, dws_sum, dwn_sum, bias_sum = carry
            first = (block * CL).astype(jnp.int32)
            plan_block = lax.dynamic_slice_in_dim(cluster_plan, first, CL)
            source_block = lax.dynamic_slice_in_dim(source, first, CL)
            adj_block = lax.dynamic_slice_in_dim(adjacency, first, CL).astype(jnp.float32)
            scale_block = lax.dynamic_slice_in_dim(scale, first, CL)
            cot_block = lax.dynamic_slice_in_dim(grad_out, first, CL)
            own_rows = clusters_in[plan_block]
            neighbour = clusters_in[source_block]
            aggregate = jnp.einsum('ckij,ckjd->cid', adj_block, neighbour.astype(jnp.float32))
            neigh_mean = ((own_rows.astype(jnp.float32) + aggregate) * scale_block[:, :, None]).astype(jnp.bfloat16)
            own_flat = own_rows.reshape(CL * TILE, D)
            mean_flat = neigh_mean.reshape(CL * TILE, D)
            pre_act = jnp.dot(own_flat, w_self, preferred_element_type=jnp.float32) + jnp.dot(mean_flat, w_neigh, preferred_element_type=jnp.float32) + out_bias.astype(jnp.float32)
            output_rows = jax.nn.silu(pre_act).astype(jnp.bfloat16)
            sig_pre = jax.nn.sigmoid(pre_act)
            grad_pre = (cot_block.reshape(CL * TILE, D).astype(jnp.float32) * sig_pre * (1.0 + pre_act * (1.0 - sig_pre))).astype(jnp.bfloat16)
            grad_pre = lax.optimization_barrier(grad_pre)
            grad_mean = (jnp.dot(grad_pre, w_neigh.T, preferred_element_type=jnp.float32) * scale_block.reshape(-1)[:, None]).astype(jnp.bfloat16)
            grad_mean = lax.optimization_barrier(grad_mean)
            grad_own = (jnp.dot(grad_pre, w_self.T, preferred_element_type=jnp.float32) + grad_mean.astype(jnp.float32)).astype(jnp.bfloat16)
            grad_neighbour = jnp.einsum('ckij,cid->ckjd', adj_block, grad_mean.reshape(CL, TILE, D).astype(jnp.float32)).astype(jnp.bfloat16)
            grad_home = grad_home.at[plan_block].add(grad_own.astype(jnp.float32).reshape(CL, TILE, D))
            grad_home = grad_home.at[source_block].add(grad_neighbour.astype(jnp.float32))
            dws_sum = dws_sum + jnp.dot(own_flat.T, grad_pre, preferred_element_type=jnp.float32)
            dwn_sum = dwn_sum + jnp.dot(mean_flat.T, grad_pre, preferred_element_type=jnp.float32)
            bias_sum = bias_sum + lax.optimization_barrier(jnp.sum(grad_pre.astype(jnp.float32), axis=0))
            return ((grad_home, dws_sum, dwn_sum, bias_sum), output_rows)
        start = (jnp.zeros((SLOTS, TILE, D), jnp.float32), dws_total, dwn_total, bias_total)
        carry, out_blocks = lax.scan(step, start, jnp.arange(N_DOM, dtype=jnp.int32))
        grad_home, dws_total, dwn_total, bias_total = carry
        outputs.append(out_blocks.reshape(NODES, D))
        grads.append(grad_home.astype(jnp.bfloat16).reshape(NODES, D))
    factor = 1.0 / math.sqrt(N_REP * NODES)
    return (jnp.stack(outputs), jnp.stack(grads), dws_total * factor, dwn_total * factor, bias_total * factor)
```

```python
import functools
import math

import jax
import jax.numpy as jnp
from jax import lax
from jax.experimental import pallas as pl
from jax.experimental.pallas import tpu as pltpu
from jax.sharding import PartitionSpec as P

D = 512
TILE = 128
CL = 16
KL = 3
KH = 2
MIG = 3
OWN = CL - MIG
NDOM = 32
NREP = 4
CAP = 2
GROUP = 4
STEPS = CL // GROUP
ROWS = GROUP * TILE
MESH = pl.DeviceIdType.MESH
F32 = jnp.float32
BF16 = jnp.bfloat16

ANY = pl.BlockSpec(memory_space=pl.ANY)
VMEM = pl.BlockSpec(memory_space=pltpu.VMEM)


def dot_tn(a, b):
    return lax.dot_general(a, b, (((0,), (0,)), ((), ())), preferred_element_type=F32)


def dot_nt(a, b):
    return lax.dot_general(a, b, (((1,), (1,)), ((), ())), preferred_element_type=F32)


def dot_nn(a, b):
    return jnp.dot(a, b, preferred_element_type=F32)


def table_kernel(x_ref, o_ref, send_sem, recv_sem):
    me, rep = lax.axis_index("dom"), lax.axis_index("rep")
    barrier = pltpu.get_barrier_semaphore()

    def greet(t, carry):
        pl.semaphore_signal(
            barrier, inc=1, device_id=(lax.rem(me + t, NDOM), rep), device_id_type=MESH
        )
        return carry

    lax.fori_loop(1, NDOM, greet, 0)
    pl.semaphore_wait(barrier, NDOM - 1)

    def copy(t):
        return pltpu.make_async_remote_copy(
            src_ref=x_ref,
            dst_ref=o_ref.at[me],
            send_sem=send_sem.at[t],
            recv_sem=recv_sem.at[t],
            device_id=(lax.rem(me + t, NDOM), rep),
            device_id_type=MESH,
        )

    def start(t, carry):
        copy(t).start()
        return carry

    def finish(t, carry):
        copy(t).wait()
        return carry

    lax.fori_loop(1, NDOM, start, 0)
    o_ref[me] = x_ref[...]
    lax.fori_loop(1, NDOM, finish, 0)


def exchange_tables(row):
    return pl.pallas_call(
        table_kernel,
        out_shape=jax.ShapeDtypeStruct((NDOM, 8, 128), jnp.int32),
        in_specs=[VMEM],
        out_specs=VMEM,
        scratch_shapes=[pltpu.SemaphoreType.DMA((NDOM,)), pltpu.SemaphoreType.DMA((NDOM,))],
        compiler_params=pltpu.CompilerParams(collective_id=0, has_side_effects=True),
    )(row)


def pack_kernel(want_ref, home_ref, out_ref, sem):
    def copy(e):
        return pltpu.make_async_copy(home_ref.at[want_ref[e]], out_ref.at[e], sem.at[e])

    def start(e, carry):
        @pl.when(want_ref[e] >= 0)
        def _():
            copy(e).start()

        return carry

    def finish(e, carry):
        @pl.when(want_ref[e] >= 0)
        def _():
            copy(e).wait()

        return carry

    lax.fori_loop(0, NDOM * CAP, start, 0)
    lax.fori_loop(0, NDOM * CAP, finish, 0)


def pack(want, home):
    return pl.pallas_call(
        pack_kernel,
        out_shape=jax.ShapeDtypeStruct((NDOM * CAP, TILE, D), BF16),
        grid_spec=pltpu.PrefetchScalarGridSpec(
            num_scalar_prefetch=1,
            grid=(),
            in_specs=[VMEM],
            out_specs=ANY,
            scratch_shapes=[pltpu.SemaphoreType.DMA((NDOM * CAP,))],
        ),
        compiler_params=pltpu.CompilerParams(vmem_limit_bytes=16 * 2**20),
    )(want, home)


def local_kernel(src_ref, home_ref, own_ref, adj_ref, w_ref, bias_ref, agg_ref, pre_ref, scale_ref):
    g = pl.program_id(0)
    pre_ref[...] = (
        dot_nn(own_ref[...].reshape(ROWS, D), w_ref[...]) + bias_ref[...]
    ).reshape(GROUP, TILE, D)
    for i in range(GROUP):
        agg = own_ref[i].astype(F32)
        degree = jnp.zeros((TILE, TILE), F32)
        for k in range(KL + KH):
            degree = degree + adj_ref[i, k].astype(F32)
        for k in range(KL):
            agg = agg + dot_nn(adj_ref[i, k], home_ref[src_ref[(g * GROUP + i) * KL + k]])
        scale = 1.0 / (1.0 + jnp.sum(degree, axis=1, keepdims=True))
        agg_ref[i] = agg
        scale_ref[i] = jnp.broadcast_to(scale, (TILE, TILE))


def tile_block(width=D):
    return pl.BlockSpec((GROUP, TILE, width), lambda g, *_: (g, 0, 0))


def whole(*shape):
    return pl.BlockSpec(shape, lambda g, *_: (0,) * len(shape))


def adj_block(k):
    return pl.BlockSpec((GROUP, 1, TILE, TILE), lambda g, *_: (g, k, 0, 0))


def local_forward(src, home, own, adjacency, w_self, bias):
    return pl.pallas_call(
        local_kernel,
        out_shape=[
            jax.ShapeDtypeStruct((CL, TILE, D), F32),
            jax.ShapeDtypeStruct((CL, TILE, D), F32),
            jax.ShapeDtypeStruct((CL, TILE, TILE), F32),
        ],
        grid_spec=pltpu.PrefetchScalarGridSpec(
            num_scalar_prefetch=1,
            grid=(STEPS,),
            in_specs=[
                whole(CL, TILE, D),
                tile_block(),
                pl.BlockSpec((GROUP, KL + KH, TILE, TILE), lambda g, *_: (g, 0, 0, 0)),
                whole(D, D),
                whole(1, D),
            ],
            out_specs=[tile_block(), tile_block(), tile_block(TILE)],
        ),
        cost_estimate=pl.CostEstimate(
            flops=2 * CL * TILE * D * (D + KL * TILE), bytes_accessed=18 * 2**20, transcendentals=0
        ),
        compiler_params=pltpu.CompilerParams(vmem_limit_bytes=32 * 2**20),
    )(src, home, own, adjacency, w_self, bias)


def middle_kernel(pos_ref, *refs):
    halo = refs[: GROUP * KH]
    (a0_ref, a1_ref, agg_ref, pre_ref, scale_ref, cot_ref, w_ref) = refs[GROUP * KH : GROUP * KH + 7]
    (new_ref, gp_ref, mean_ref, gm_ref, back_ref) = refs[GROUP * KH + 7 : GROUP * KH + 12]
    (grads, sem) = refs[GROUP * KH + 12 :]
    g = pl.program_id(0)
    scale = jnp.concatenate([scale_ref[...].reshape(ROWS, TILE)] * (D // TILE), axis=1)
    for i in range(GROUP):
        adj = jnp.concatenate([a0_ref[i, 0], a1_ref[i, 0]], axis=1)
        rows = jnp.concatenate([halo[i * KH][0], halo[i * KH + 1][0]], axis=0)
        agg = agg_ref[i] + dot_nn(adj, rows)
        mean_ref[i] = (agg * scale[i * TILE : (i + 1) * TILE]).astype(BF16)
    pre = pre_ref[...].reshape(ROWS, D) + dot_nn(mean_ref[...].reshape(ROWS, D), w_ref[...])
    sig = 1.0 / (1.0 + jnp.exp(-pre))
    new_ref[...] = (pre * sig).astype(BF16).reshape(GROUP, TILE, D)
    cot = cot_ref[...].reshape(ROWS, D).astype(F32)
    gp = (cot * sig * (1.0 + pre * (1.0 - sig))).astype(BF16)
    gp_ref[...] = gp.reshape(GROUP, TILE, D)
    gm = (dot_nt(gp, w_ref[...]) * scale).astype(BF16)
    gm_ref[...] = gm.reshape(GROUP, TILE, D)

    def copy(e):
        return pltpu.make_async_copy(grads.at[e], back_ref.at[pos_ref[e]], sem.at[e])

    for i in range(GROUP):
        adj = jnp.concatenate([a0_ref[i, 0], a1_ref[i, 0]], axis=1)
        both = dot_tn(adj, gm[i * TILE : (i + 1) * TILE]).astype(BF16)
        for k in range(KH):
            e = (g * GROUP + i) * KH + k
            grads[e] = both[k * TILE : (k + 1) * TILE]
            copy(e).start()

    @pl.when(g == STEPS - 1)
    def _():
        def finish(e, carry):
            copy(e).wait()
            return carry

        lax.fori_loop(0, CL * KH, finish, 0)


def middle(pos, recv, adjacency, agg, pre, scale, cot, w_neigh):
    def halo_block(n):
        return pl.BlockSpec((1, TILE, D), lambda g, pos: (pos[g * GROUP * KH + n], 0, 0))

    tiles = jax.ShapeDtypeStruct((CL, TILE, D), BF16)
    return pl.pallas_call(
        middle_kernel,
        out_shape=[tiles, tiles, tiles, tiles, jax.ShapeDtypeStruct((NDOM * CAP, TILE, D), BF16)],
        grid_spec=pltpu.PrefetchScalarGridSpec(
            num_scalar_prefetch=1,
            grid=(STEPS,),
            in_specs=[halo_block(n) for n in range(GROUP * KH)]
            + [
                adj_block(KL),
                adj_block(KL + 1),
                tile_block(),
                tile_block(),
                tile_block(TILE),
                tile_block(),
                whole(D, D),
            ],
            out_specs=[tile_block(), tile_block(), tile_block(), tile_block(), ANY],
            scratch_shapes=[
                pltpu.VMEM((CL * KH, TILE, D), BF16),
                pltpu.SemaphoreType.DMA((CL * KH,)),
            ],
        ),
        cost_estimate=pl.CostEstimate(
            flops=2 * CL * TILE * D * (2 * D + 4 * TILE),
            bytes_accessed=30 * 2**20,
            transcendentals=CL * TILE * D,
        ),
        compiler_params=pltpu.CompilerParams(vmem_limit_bytes=40 * 2**20),
    )(pos, *([recv] * (GROUP * KH)), adjacency, adjacency, agg, pre, scale, cot, w_neigh)


def rest_kernel(
    src_ref, gp_ref, gm_ref, own_ref, mean_ref, a0_ref, a1_ref, a2_ref, w_ref,
    acc_ref, mig_ref, dw_ref, db_ref,
):
    g = pl.program_id(0)

    @pl.when(g == 0)
    def _():
        acc_ref[...] = jnp.zeros_like(acc_ref)
        dw_ref[...] = jnp.zeros_like(dw_ref)
        db_ref[...] = jnp.zeros_like(db_ref)

    gp = gp_ref[...].reshape(ROWS, D)
    gm = gm_ref[...].reshape(ROWS, D)
    own_grad = (dot_nt(gp, w_ref[...]) + gm.astype(F32)).astype(BF16)
    for i in range(GROUP):
        part = own_grad[i * TILE : (i + 1) * TILE]
        slot = g * GROUP + i

        @pl.when(slot < OWN)
        def _():
            acc_ref[slot] += part.astype(F32)

        if STEPS * GROUP - GROUP + i >= OWN:

            @pl.when(slot >= OWN)
            def _():
                mig_ref[STEPS * GROUP - GROUP + i - OWN] = part

        adj = jnp.concatenate([a0_ref[i, 0], a1_ref[i, 0], a2_ref[i, 0]], axis=1)
        grads = dot_tn(adj, gm[i * TILE : (i + 1) * TILE]).astype(BF16).astype(F32)
        for k in range(KL):
            acc_ref[src_ref[slot * KL + k]] += grads[k * TILE : (k + 1) * TILE]
    dw_ref[0] += dot_tn(own_ref[...].reshape(ROWS, D), gp)
    dw_ref[1] += dot_tn(mean_ref[...].reshape(ROWS, D), gp)
    db_ref[...] += jnp.sum(gp.astype(F32).reshape(ROWS // 8, 8, D), axis=0)


def rest(src, gp, gm, own, mean, adjacency, w_self):
    return pl.pallas_call(
        rest_kernel,
        out_shape=[
            jax.ShapeDtypeStruct((CL, TILE, D), F32),
            jax.ShapeDtypeStruct((MIG, TILE, D), BF16),
            jax.ShapeDtypeStruct((2, D, D), F32),
            jax.ShapeDtypeStruct((8, D), F32),
        ],
        grid_spec=pltpu.PrefetchScalarGridSpec(
            num_scalar_prefetch=1,
            grid=(STEPS,),
            in_specs=[tile_block()] * 4 + [adj_block(0), adj_block(1), adj_block(2), whole(D, D)],
            out_specs=[whole(CL, TILE, D), whole(MIG, TILE, D), whole(2, D, D), whole(8, D)],
        ),
        cost_estimate=pl.CostEstimate(
            flops=2 * CL * TILE * D * (3 * D + 3 * TILE),
            bytes_accessed=20 * 2**20,
            transcendentals=0,
        ),
        compiler_params=pltpu.CompilerParams(vmem_limit_bytes=40 * 2**20),
    )(src, gp, gm, own, mean, adjacency, adjacency, adjacency, w_self)


ZROWS = D // NREP
CHIPS = NDOM // 2
CROWS = ZROWS // CHIPS


def reduce_kernel(
    dw_ref, db_ref, out_ref, bias_ref,
    r1, b1, s1, r2, b2, s2, r3, b3, sems,
):
    me, rep = lax.axis_index("dom"), lax.axis_index("rep")
    core, chip = lax.rem(me, 2), me // 2
    partner = chip * 2 + 1 - core
    barrier = pltpu.get_barrier_semaphore()

    def z_peer(t):
        return lax.rem(rep + t, NREP)

    def chip_peer(t):
        return lax.rem(chip + t, CHIPS)

    def signal(dom, z):
        pl.semaphore_signal(barrier, inc=1, device_id=(dom, z), device_id_type=MESH)

    def loop(n, f):
        def step(t, carry):
            f(t)
            return carry

        lax.fori_loop(1, n, step, 0)

    signal(partner, rep)
    loop(NREP, lambda t: signal(me, z_peer(t)))
    loop(CHIPS, lambda t: signal(chip_peer(t) * 2 + core, rep))
    pl.semaphore_wait(barrier, 1 + (NREP - 1) + (CHIPS - 1))

    def send(src, dst, base, dom, z):
        return pltpu.make_async_remote_copy(
            src_ref=src,
            dst_ref=dst,
            send_sem=sems.at[0, base],
            recv_sem=sems.at[1, base],
            device_id=(dom, z),
            device_id_type=MESH,
        )

    c_dw = send(dw_ref.at[1 - core], r1, 0, partner, rep)
    c_db = send(db_ref, b1, 1, partner, rep)
    c_dw.start()
    c_db.start()
    c_db.wait()
    c_dw.wait()
    s1[...] = dw_ref[core] + r1[...]
    b2[rep] = db_ref[...] + b1[...]

    def z_dw(t):
        z = z_peer(t)
        return send(s1.at[pl.ds(z * ZROWS, ZROWS)], r2.at[rep], 2 + t, me, z)

    def z_db(t):
        return send(b2.at[rep], b2.at[rep], 6 + t, me, z_peer(t))

    loop(NREP, lambda t: z_dw(t).start())
    loop(NREP, lambda t: z_db(t).start())
    r2[rep] = s1[pl.ds(pl.multiple_of(rep * ZROWS, ZROWS), ZROWS)]
    loop(NREP, lambda t: z_db(t).wait())
    loop(NREP, lambda t: z_dw(t).wait())
    s2[...] = (r2[0] + r2[1]) + (r2[2] + r2[3])
    b3[chip] = (b2[0] + b2[1]) + (b2[2] + b2[3])

    def p_dw(t):
        q = chip_peer(t)
        return send(s2.at[pl.ds(q * CROWS, CROWS)], r3.at[chip], 10 + t, q * 2 + core, rep)

    def p_db(t):
        return send(b3.at[chip], b3.at[chip], 26 + t, chip_peer(t) * 2 + core, rep)

    loop(CHIPS, lambda t: p_dw(t).start())
    loop(CHIPS, lambda t: p_db(t).start())
    r3[chip] = s2[pl.ds(pl.multiple_of(chip * CROWS, CROWS), CROWS)]
    loop(CHIPS, lambda t: p_dw(t).wait())
    total = r3[0]
    for q in range(1, CHIPS):
        total = total + r3[q]
    mine = out_ref.at[core, pl.ds(pl.multiple_of(rep * ZROWS + chip * CROWS, CROWS), CROWS)]
    mine[...] = total

    def p_out(t):
        return send(mine, mine, 42 + t, chip_peer(t) * 2 + core, rep)

    loop(CHIPS, lambda t: p_out(t).start())
    loop(CHIPS, lambda t: p_db(t).wait())
    bias = b3[0]
    for q in range(1, CHIPS):
        bias = bias + b3[q]
    bias_ref[...] = bias
    loop(CHIPS, lambda t: p_out(t).wait())
    block = out_ref.at[core, pl.ds(pl.multiple_of(rep * ZROWS, ZROWS), ZROWS)]

    def z_out(t):
        return send(block, block, 58 + t, me, z_peer(t))

    loop(NREP, lambda t: z_out(t).start())
    loop(NREP, lambda t: z_out(t).wait())
    last = send(out_ref.at[core], out_ref.at[core], 62, partner, rep)
    last.start()
    last.wait()


def reduce_all(dw, db):
    return pl.pallas_call(
        reduce_kernel,
        out_shape=[jax.ShapeDtypeStruct((2, D, D), F32), jax.ShapeDtypeStruct((8, D), F32)],
        in_specs=[VMEM, VMEM],
        out_specs=[VMEM, VMEM],
        scratch_shapes=[
            pltpu.VMEM((D, D), F32),
            pltpu.VMEM((8, D), F32),
            pltpu.VMEM((D, D), F32),
            pltpu.VMEM((NREP, ZROWS, D), F32),
            pltpu.VMEM((NREP, 8, D), F32),
            pltpu.VMEM((ZROWS, D), F32),
            pltpu.VMEM((CHIPS, CROWS, D), F32),
            pltpu.VMEM((CHIPS, 8, D), F32),
            pltpu.SemaphoreType.DMA((2, 64)),
        ],
        cost_estimate=pl.CostEstimate(flops=2**20, bytes_accessed=64 * 2**20, transcendentals=0),
        compiler_params=pltpu.CompilerParams(
            collective_id=1, has_side_effects=True, vmem_limit_bytes=24 * 2**20
        ),
    )(dw, db)


def final_kernel(want_ref, acc_in, mig_ref, back_ref, out_ref, acc, tiles, sem):
    def copy(e):
        return pltpu.make_async_copy(back_ref.at[e], tiles.at[e], sem.at[e])

    def start(e, carry):
        @pl.when(want_ref[e] >= 0)
        def _():
            copy(e).start()

        return carry

    lax.fori_loop(0, NDOM * CAP, start, 0)
    acc[...] = acc_in[...]
    for j in range(MIG):
        acc[OWN + j] += mig_ref[j].astype(F32)

    def add(e, carry):
        @pl.when(want_ref[e] >= 0)
        def _():
            copy(e).wait()
            acc[want_ref[e]] += tiles[e].astype(F32)

        return carry

    lax.fori_loop(0, NDOM * CAP, add, 0)
    out_ref[...] = acc[...].astype(BF16)


def finish(want, acc, mig, back):
    return pl.pallas_call(
        final_kernel,
        out_shape=jax.ShapeDtypeStruct((CL, TILE, D), BF16),
        grid_spec=pltpu.PrefetchScalarGridSpec(
            num_scalar_prefetch=1,
            grid=(),
            in_specs=[VMEM, VMEM, ANY],
            out_specs=VMEM,
            scratch_shapes=[
                pltpu.VMEM((CL, TILE, D), F32),
                pltpu.VMEM((NDOM * CAP, TILE, D), BF16),
                pltpu.SemaphoreType.DMA((NDOM * CAP,)),
            ],
        ),
        compiler_params=pltpu.CompilerParams(vmem_limit_bytes=40 * 2**20),
    )(want, acc, mig, back)


def shifted(tile, offset, sign):
    def branch(o):
        pairs = [((i + sign * o) % NDOM, i) for i in range(NDOM)]
        return lambda x: lax.ppermute(x, "dom", pairs)

    return lax.switch(offset - 1, [branch(o) for o in range(1, NDOM)], tile)


def body(
    features, w_self, w_neigh, out_bias, cluster_plan, local_source, halo_owner, halo_local,
    adjacency, cotangent,
):
    me = lax.axis_index("dom")
    home = features[0].reshape(CL, TILE, D)
    cot = cotangent[0].reshape(CL, TILE, D)
    src = local_source.reshape(-1)
    owner, local = halo_owner.reshape(-1), halo_local.reshape(-1)
    onehot = (owner[:, None] == jnp.arange(NDOM, dtype=jnp.int32)[None, :]).astype(jnp.int32)
    before = jnp.cumsum(onehot, axis=0) - 1
    order = jnp.sum(onehot * before, axis=1)
    table = [
        jnp.sum(jnp.where((onehot == 1) & (before == j), local[:, None] + 1, 0), axis=0) - 1
        for j in range(CAP)
    ]
    row = jnp.stack(table, axis=1).reshape(1, NDOM * CAP)
    tables = exchange_tables(jnp.pad(row, ((0, 7), (0, 128 - NDOM * CAP))))
    want = lax.dynamic_slice(tables[:, 0, :], (0, me * CAP), (NDOM, CAP)).reshape(-1)
    pos = owner * CAP + order

    sent = pack(want, home)
    recv = lax.all_to_all(
        sent.reshape(NDOM, CAP, TILE, D), "dom", split_axis=0, concat_axis=0, tiled=True
    ).reshape(NDOM * CAP, TILE, D)
    offsets = [lax.rem(cluster_plan[OWN + j] // CL - me + NDOM, NDOM) for j in range(MIG)]
    moved = [shifted(home[OWN + j], offsets[j], 1) for j in range(MIG)]
    own = jnp.concatenate([home[:OWN], jnp.stack(moved)], axis=0)
    agg, pre, scale = local_forward(src, home, own, adjacency, w_self, out_bias.reshape(1, D))
    new, gp, mean, gm, back = middle(pos, recv, adjacency, agg, pre, scale, cot, w_neigh)
    returned = lax.all_to_all(
        back.reshape(NDOM, CAP, TILE, D), "dom", split_axis=0, concat_axis=0, tiled=True
    ).reshape(NDOM * CAP, TILE, D)
    acc, mig, dw, db = rest(src, gp, gm, own, mean, adjacency, w_self)
    mig_back = jnp.stack([shifted(mig[j], offsets[j], -1) for j in range(MIG)])
    dw_sum, db_sum = reduce_all(dw, db)
    grad = finish(want, acc, mig_back, returned)
    factor = 1.0 / math.sqrt(NDOM * NREP * CL * TILE)
    return (
        new.reshape(1, CL * TILE, D),
        grad.reshape(1, CL * TILE, D),
        dw_sum[0] * factor,
        dw_sum[1] * factor,
        jnp.sum(db_sum, axis=0) * factor,
    )


def solution(mesh):
    return jax.shard_map(
        body,
        mesh=mesh,
        in_specs=(
            P("rep", "dom", None),
            P(),
            P(),
            P(),
            P("dom"),
            P("dom", None),
            P("dom", None),
            P("dom", None),
            P("dom", None, None, None),
            P("rep", "dom", None),
        ),
        out_specs=(P("rep", "dom", None), P("rep", "dom", None), P(), P(), P()),
        check_vma=False,
    )
```

```python
import functools
import math

import jax
import jax.numpy as jnp
from jax import lax
from jax.experimental import pallas as pl
from jax.experimental.pallas import tpu as pltpu
from jax.sharding import PartitionSpec as P

D = 512
TILE = 128
CL = 16
KL = 3
KH = 2
MIG = 3
OWN = CL - MIG
NDOM = 32
NREP = 4
HALF = TILE // 2
WIDE = TILE + HALF
CHUNK = 16
SIDE = 4
GROUP = 4
STEPS = CL // GROUP
ROWS = GROUP * TILE
MESH = pl.DeviceIdType.MESH
F32 = jnp.float32
BF16 = jnp.bfloat16

ANY = pl.BlockSpec(memory_space=pl.ANY)
VMEM = pl.BlockSpec(memory_space=pltpu.VMEM)
SMEM = pl.BlockSpec(memory_space=pltpu.SMEM)


def dot_tn(a, b):
    return lax.dot_general(a, b, (((0,), (0,)), ((), ())), preferred_element_type=F32)


def dot_nt(a, b):
    return lax.dot_general(a, b, (((1,), (1,)), ((), ())), preferred_element_type=F32)


def dot_nn(a, b):
    return jnp.dot(a, b, preferred_element_type=F32)


ZROWS = D // NREP
CHIPS = NDOM // 2
CROWS = ZROWS // CHIPS

ORDER = [
    (1, 0), (3, 0), (0, 1), (0, 3), (1, 1), (3, 3), (1, 3), (3, 1),
    (2, 0), (0, 2), (2, 2), (1, 2), (2, 1), (3, 2), (2, 3),
]
PEERS = [(0, 0, 1)] + [(dx, dy, dc) for dx, dy in ORDER for dc in (0, 1)]
NPEER = len(PEERS)


class Place:
    def __init__(self):
        self.me, self.rep = lax.axis_index("dom"), lax.axis_index("rep")
        self.core, self.chip = lax.rem(self.me, 2), self.me // 2
        self.x, self.y = lax.rem(self.chip, SIDE), self.chip // SIDE
        self.partner = self.chip * 2 + 1 - self.core

    def at(self, dx, dy, dc):
        x, y = lax.rem(self.x + dx, SIDE), lax.rem(self.y + dy, SIDE)
        return (y * SIDE + x) * 2 + lax.rem(self.core + dc, 2)


def loop(low, high, f):
    def step(t, carry):
        f(t)
        return carry

    lax.fori_loop(low, high, step, 0)


def greet_plane(here, barrier):
    def one(t):
        dom = lax.rem(here.me + t, NDOM)
        pl.semaphore_signal(barrier, inc=1, device_id=(dom, here.rep), device_id_type=MESH)

    loop(1, NDOM, one)


def remote(src, dst, send_sem, recv_sem, dom, z):
    return pltpu.make_async_remote_copy(
        src_ref=src,
        dst_ref=dst,
        send_sem=send_sem,
        recv_sem=recv_sem,
        device_id=(dom, z),
        device_id_type=MESH,
    )


class Exchange:
    def __init__(self, here, src, dst, send_sem, recv_sem, first, last):
        self.here, self.src, self.dst = here, src, dst
        self.send_sem, self.recv_sem = send_sem, recv_sem
        self.first, self.last = first, last

    def copy(self, n, rows):
        dom = self.here.at(*PEERS[n])
        return remote(
            self.src.at[dom, rows],
            self.dst.at[self.here.me, rows],
            self.send_sem.at[n],
            self.recv_sem.at[n],
            dom,
            self.here.rep,
        )

    def start(self, low, high):
        def chunk(c):
            rows = pl.ds(pl.multiple_of(self.first + c * CHUNK, CHUNK), CHUNK)
            for n in range(NPEER):
                self.copy(n, rows).start()

        loop(low, high, chunk)

    def every(self, n):
        return self.copy(n, pl.ds(self.first, self.last - self.first))


class Shift:
    def __init__(self, here, pick_ref, along_x, picked, along_y, lanes, sems):
        self.here, self.pick = here, pick_ref
        self.along_x, self.picked, self.along_y, self.lanes = along_x, picked, along_y, lanes
        self.sems = sems

    def sem(self, n):
        return self.sems.at[0, n], self.sems.at[1, n]

    def copy_x(self, t):
        here = self.here
        slot = self.along_x.at[here.x]
        return remote(slot, slot, *self.sem(t), here.at(t, 0, 0), here.rep)

    def copy_y(self, t):
        here = self.here
        return remote(
            self.picked, self.along_y.at[here.y], *self.sem(SIDE + t), here.at(0, t, 0), here.rep
        )

    def copy_lane(self):
        here = self.here
        slot = self.lanes.at[here.core]
        return remote(slot, slot, *self.sem(0), here.partner, here.rep)

    def start_x(self):
        loop(1, SIDE, lambda t: self.copy_x(t).start())

    def start_y(self):
        loop(1, SIDE, lambda t: self.copy_x(t).wait())
        for j in range(MIG):
            self.picked[j] = self.along_x[self.pick[j], j]
        self.along_y[self.here.y] = self.picked[...]
        loop(1, SIDE, lambda t: self.copy_y(t).start())

    def start_lane(self):
        loop(1, SIDE, lambda t: self.copy_y(t).wait())
        for j in range(MIG):
            self.lanes[self.here.core, j] = self.along_y[self.pick[MIG + j], j]
        self.copy_lane().start()

    def finish(self, out_ref):
        self.copy_lane().wait()
        for j in range(MIG):
            out_ref[j] = self.lanes[lax.rem(self.here.core + self.pick[2 * MIG + j], 2), j]


SHIFT_SCRATCH = [
    pltpu.VMEM((SIDE, MIG, TILE, D), BF16),
    pltpu.VMEM((MIG, TILE, D), BF16),
    pltpu.VMEM((SIDE, MIG, TILE, D), BF16),
    pltpu.VMEM((2, MIG, TILE, D), BF16),
    pltpu.SemaphoreType.DMA((2, 2 * SIDE)),
]
EXCHANGE_SEMS = pltpu.SemaphoreType.DMA((2, NPEER))


def forward_kernel(
    pick_ref, row_ref, home_ref,
    recv_ref, table_ref, moved_ref,
    feat, stage, asked, along_x, picked, along_y, lanes, shift_sems,
    table_sems, tile_sems, local_sems,
):
    here = Place()
    me, core, rep = here.me, here.core, here.rep
    barrier = pltpu.get_barrier_semaphore()
    greet_plane(here, barrier)
    own = feat.at[pl.ds(core * CL, CL)]
    take = pltpu.make_async_copy(home_ref, own, local_sems.at[0])
    take.start()
    mine = pltpu.make_async_copy(home_ref.at[pl.ds(OWN, MIG)], along_x.at[here.x], local_sems.at[1])
    mine.start()
    table_ref[me] = row_ref[...]
    pl.semaphore_wait(barrier, NDOM - 1)

    def table(n):
        return remote(
            row_ref, table_ref.at[me], table_sems.at[0, n], table_sems.at[1, n],
            lax.rem(me + n, NDOM), rep,
        )

    loop(1, NDOM, lambda n: table(n).start())
    share = remote(home_ref, own, local_sems.at[2], local_sems.at[3], here.partner, rep)
    share.start()
    shift = Shift(here, pick_ref, along_x, picked, along_y, lanes, shift_sems)
    mine.wait()
    shift.start_x()
    loop(1, NDOM, lambda n: table(n).wait())
    read = pltpu.make_async_copy(table_ref, asked, local_sems.at[4])
    read.start()
    read.wait()
    take.wait()
    share.wait()

    def gather(p):
        first = asked[p, 0, me]
        other = asked[p, 0, NDOM + here.chip]
        stage[p, pl.ds(0, TILE)] = feat[core * CL + jnp.maximum(first, 0)]
        stage[p, pl.ds(TILE, HALF)] = feat[
            jnp.maximum(other, 0), pl.ds(pl.multiple_of(core * HALF, HALF), HALF)
        ]

    loop(0, NDOM, gather)
    keep = pltpu.make_async_copy(stage.at[me], recv_ref.at[me], local_sems.at[5])
    keep.start()
    tiles = Exchange(here, stage, recv_ref, tile_sems.at[0], tile_sems.at[1], 0, WIDE)
    tiles.start(0, 4)
    shift.start_y()
    tiles.start(4, 8)
    shift.start_lane()
    tiles.start(8, WIDE // CHUNK)
    shift.finish(moved_ref)
    keep.wait()
    for n in range(NPEER):
        tiles.every(n).wait()


def exchange_forward(pick, row, home):
    return pl.pallas_call(
        forward_kernel,
        out_shape=[
            jax.ShapeDtypeStruct((NDOM, WIDE, D), BF16),
            jax.ShapeDtypeStruct((NDOM, 1, 128), jnp.int32),
            jax.ShapeDtypeStruct((MIG, TILE, D), BF16),
        ],
        in_specs=[SMEM, VMEM, ANY],
        out_specs=[ANY, VMEM, VMEM],
        scratch_shapes=[
            pltpu.VMEM((2 * CL, TILE, D), BF16),
            pltpu.VMEM((NDOM, WIDE, D), BF16),
            pltpu.SMEM((NDOM, 1, 128), jnp.int32),
        ]
        + SHIFT_SCRATCH
        + [pltpu.SemaphoreType.DMA((2, NDOM)), EXCHANGE_SEMS, pltpu.SemaphoreType.DMA((6,))],
        compiler_params=pltpu.CompilerParams(
            collective_id=0, has_side_effects=True, vmem_limit_bytes=32 * 2**20
        ),
    )(pick, row, home)


def backward_kernel(
    pick_ref, back_ref, tail_ref, dw_ref, db_ref,
    ret_ref, passed_ref, moved_ref, out_ref, bias_ref,
    along_x, picked, along_y, lanes, shift_sems,
    r1, b1, s1, r2, b2, s2, r3, b3, sums, half_sems, tile_sems, pass_sems, local_sems,
):
    here = Place()
    me, core, chip, rep, partner = here.me, here.core, here.chip, here.rep, here.partner
    barrier = pltpu.get_barrier_semaphore()

    def z_peer(t):
        return lax.rem(rep + t, NREP)

    def chip_peer(t):
        return lax.rem(chip + t, CHIPS)

    def greet_z(t):
        pl.semaphore_signal(barrier, inc=1, device_id=(me, z_peer(t)), device_id_type=MESH)

    greet_plane(here, barrier)
    loop(1, NREP, greet_z)
    keep = pltpu.make_async_copy(back_ref.at[me], ret_ref.at[me], local_sems.at[0])
    keep.start()
    along_x[here.x] = tail_ref[...]
    pl.semaphore_wait(barrier, NDOM - 1 + NREP - 1)

    def send(src, dst, n, dom, z):
        return remote(src, dst, sums.at[0, n], sums.at[1, n], dom, z)

    shift = Shift(here, pick_ref, along_x, picked, along_y, lanes, shift_sems)
    halves = Exchange(here, back_ref, ret_ref, half_sems.at[0], half_sems.at[1], TILE, WIDE)
    tiles = Exchange(here, back_ref, ret_ref, tile_sems.at[0], tile_sems.at[1], 0, TILE)

    c_dw = send(dw_ref.at[1 - core], r1, 0, partner, rep)
    c_db = send(db_ref, b1, 1, partner, rep)
    c_dw.start()
    c_db.start()
    shift.start_x()
    halves.start(0, HALF // CHUNK)
    c_db.wait()
    c_dw.wait()
    s1[...] = dw_ref[core] + r1[...]
    b2[rep] = db_ref[...] + b1[...]

    def z_dw(t):
        z = z_peer(t)
        return send(s1.at[pl.ds(z * ZROWS, ZROWS)], r2.at[rep], 2 + t, me, z)

    def z_db(t):
        return send(b2.at[rep], b2.at[rep], 6 + t, me, z_peer(t))

    loop(1, NREP, lambda t: z_dw(t).start())
    loop(1, NREP, lambda t: z_db(t).start())
    r2[rep] = s1[pl.ds(pl.multiple_of(rep * ZROWS, ZROWS), ZROWS)]
    tiles.start(0, 2)
    shift.start_y()
    loop(1, NREP, lambda t: z_db(t).wait())
    loop(1, NREP, lambda t: z_dw(t).wait())
    s2[...] = (r2[0] + r2[1]) + (r2[2] + r2[3])
    b3[chip] = (b2[0] + b2[1]) + (b2[2] + b2[3])

    def p_dw(t):
        q = chip_peer(t)
        return send(s2.at[pl.ds(q * CROWS, CROWS)], r3.at[chip], 10 + t, q * 2 + core, rep)

    def p_db(t):
        return send(b3.at[chip], b3.at[chip], 26 + t, chip_peer(t) * 2 + core, rep)

    loop(1, CHIPS, lambda t: p_dw(t).start())
    loop(1, CHIPS, lambda t: p_db(t).start())
    r3[chip] = s2[pl.ds(pl.multiple_of(chip * CROWS, CROWS), CROWS)]
    tiles.start(2, 4)
    shift.start_lane()
    loop(1, CHIPS, lambda t: p_dw(t).wait())
    total = r3[0]
    for q in range(1, CHIPS):
        total = total + r3[q]
    mine = out_ref.at[core, pl.ds(pl.multiple_of(rep * ZROWS + chip * CROWS, CROWS), CROWS)]
    mine[...] = total

    def p_out(t):
        return send(mine, mine, 42 + t, chip_peer(t) * 2 + core, rep)

    loop(1, CHIPS, lambda t: p_out(t).start())
    tiles.start(4, 6)
    shift.finish(moved_ref)
    loop(1, CHIPS, lambda t: p_db(t).wait())
    bias = b3[0]
    for q in range(1, CHIPS):
        bias = bias + b3[q]
    bias_ref[...] = bias
    loop(1, CHIPS, lambda t: p_out(t).wait())
    block = out_ref.at[core, pl.ds(pl.multiple_of(rep * ZROWS, ZROWS), ZROWS)]

    def z_out(t):
        return send(block, block, 58 + t, me, z_peer(t))

    loop(1, NREP, lambda t: z_out(t).start())
    tiles.start(6, TILE // CHUNK)

    def pass_on(src, n):
        rows = pl.ds(TILE, HALF)
        return remote(
            ret_ref.at[src, rows], passed_ref.at[src], pass_sems.at[0, n], pass_sems.at[1, n],
            partner, rep,
        )

    keep.wait()
    pass_on(me, NPEER).start()
    for n, (dx, dy, dc) in enumerate(PEERS):
        halves.every(n).wait()
        pass_on(here.at(SIDE - dx, SIDE - dy, dc), n).start()
    loop(1, NREP, lambda t: z_out(t).wait())
    last = send(out_ref.at[core], out_ref.at[core], 62, partner, rep)
    last.start()
    pass_on(me, NPEER).wait()
    for n, (dx, dy, dc) in enumerate(PEERS):
        pass_on(here.at(SIDE - dx, SIDE - dy, dc), n).wait()
    for n in range(NPEER):
        tiles.every(n).wait()
    last.wait()


def exchange_backward(pick, back, tail, dw, db):
    return pl.pallas_call(
        backward_kernel,
        out_shape=[
            jax.ShapeDtypeStruct((NDOM, WIDE, D), BF16),
            jax.ShapeDtypeStruct((NDOM, HALF, D), BF16),
            jax.ShapeDtypeStruct((MIG, TILE, D), BF16),
            jax.ShapeDtypeStruct((2, D, D), F32),
            jax.ShapeDtypeStruct((8, D), F32),
        ],
        in_specs=[SMEM, ANY, VMEM, VMEM, VMEM],
        out_specs=[ANY, ANY, VMEM, VMEM, VMEM],
        scratch_shapes=SHIFT_SCRATCH
        + [
            pltpu.VMEM((D, D), F32),
            pltpu.VMEM((8, D), F32),
            pltpu.VMEM((D, D), F32),
            pltpu.VMEM((NREP, ZROWS, D), F32),
            pltpu.VMEM((NREP, 8, D), F32),
            pltpu.VMEM((ZROWS, D), F32),
            pltpu.VMEM((CHIPS, CROWS, D), F32),
            pltpu.VMEM((CHIPS, 8, D), F32),
            pltpu.SemaphoreType.DMA((2, 64)),
            EXCHANGE_SEMS,
            EXCHANGE_SEMS,
            pltpu.SemaphoreType.DMA((2, NDOM)),
            pltpu.SemaphoreType.DMA((1,)),
        ],
        compiler_params=pltpu.CompilerParams(
            collective_id=1, has_side_effects=True, vmem_limit_bytes=32 * 2**20
        ),
    )(pick, back, tail, dw, db)


def tile_block(width=D):
    return pl.BlockSpec((GROUP, TILE, width), lambda g, *_: (g, 0, 0))


def whole(*shape):
    return pl.BlockSpec(shape, lambda g, *_: (0,) * len(shape))


def adj_block(k):
    return pl.BlockSpec((GROUP, 1, TILE, TILE), lambda g, *_: (g, k, 0, 0))


def own_tile(i, g, home_tile, moved_ref):
    j = CL - GROUP + i - OWN
    if j < 0:
        return home_tile
    return jnp.where(g == STEPS - 1, moved_ref[j], home_tile)


PARTS = 2 * GROUP * KH


def middle_kernel(block_ref, src_ref, *refs):
    halo = refs[:PARTS]
    (home_ref, moved_ref, adj_ref, cot_ref, ws_ref, wn_ref, bias_ref) = refs[PARTS : PARTS + 7]
    (new_ref, gp_ref, mean_ref, gm_ref, tail_ref, back_ref) = refs[PARTS + 7 : PARTS + 13]
    (own, scale, grads, sem) = refs[PARTS + 13 :]
    g = pl.program_id(0)
    for i in range(GROUP):
        slot = g * GROUP + i
        rows = pl.ds(i * TILE, TILE)
        mine = own_tile(i, g, home_ref[slot], moved_ref)
        own[rows] = mine
        adj = jnp.concatenate([adj_ref[i, k] for k in range(KL + KH)], axis=1)
        total = jnp.sum(adj.astype(F32), axis=1, keepdims=True)
        scale[rows] = jnp.broadcast_to(1.0 / (1.0 + total), (TILE, D))
        near = [home_ref[src_ref[slot * KL + k]] for k in range(KL)]
        far = [halo[2 * KH * i + n][0] for n in range(2 * KH)]
        agg = mine.astype(F32) + dot_nn(adj, jnp.concatenate(near + far, axis=0))
        mean_ref[i] = (agg * scale[rows]).astype(BF16)
    pre = (
        dot_nn(own[...], ws_ref[...])
        + dot_nn(mean_ref[...].reshape(ROWS, D), wn_ref[...])
        + bias_ref[...]
    )
    sig = 1.0 / (1.0 + jnp.exp(-pre))
    new_ref[...] = (pre * sig).astype(BF16).reshape(GROUP, TILE, D)
    cot = cot_ref[...].reshape(ROWS, D).astype(F32)
    gp = (cot * sig * (1.0 + pre * (1.0 - sig))).astype(BF16)
    gp_ref[...] = gp.reshape(GROUP, TILE, D)
    gm = (dot_nt(gp, wn_ref[...]) * scale[...]).astype(BF16)
    gm_ref[...] = gm.reshape(GROUP, TILE, D)

    def copy(n):
        return pltpu.make_async_copy(grads.at[n], back_ref.at[block_ref[n]], sem.at[n])

    for i in range(GROUP):
        adj = jnp.concatenate([adj_ref[i, KL + k] for k in range(KH)], axis=1)
        both = dot_tn(adj, gm[i * TILE : (i + 1) * TILE]).astype(BF16)
        for part in range(2 * KH):
            n = (g * GROUP + i) * 2 * KH + part
            grads[n] = both[part * HALF : (part + 1) * HALF]
            copy(n).start()

    @pl.when(g == STEPS - 1)
    def _():
        first = TILE * (GROUP - MIG)
        tail = dot_nt(gp[first:], ws_ref[...]) + gm[first:].astype(F32)
        tail_ref[...] = tail.astype(BF16).reshape(MIG, TILE, D)
        loop(0, 2 * CL * KH, lambda n: copy(n).wait())


def middle(blocks, src, recv, home, moved, adjacency, cot, w_self, w_neigh, bias):
    def halo_block(n):
        return pl.BlockSpec((1, HALF, D), lambda g, blocks, src: (blocks[g * PARTS + n], 0, 0))

    tiles = jax.ShapeDtypeStruct((CL, TILE, D), BF16)
    return pl.pallas_call(
        middle_kernel,
        out_shape=[
            tiles, tiles, tiles, tiles,
            jax.ShapeDtypeStruct((MIG, TILE, D), BF16),
            jax.ShapeDtypeStruct(recv.shape, BF16),
        ],
        grid_spec=pltpu.PrefetchScalarGridSpec(
            num_scalar_prefetch=2,
            grid=(STEPS,),
            in_specs=[halo_block(n) for n in range(PARTS)]
            + [
                whole(CL, TILE, D),
                whole(MIG, TILE, D),
                pl.BlockSpec((GROUP, KL + KH, TILE, TILE), lambda g, *_: (g, 0, 0, 0)),
                tile_block(),
                whole(D, D),
                whole(D, D),
                whole(1, D),
            ],
            out_specs=[tile_block()] * 4 + [whole(MIG, TILE, D), ANY],
            scratch_shapes=[
                pltpu.VMEM((ROWS, D), BF16),
                pltpu.VMEM((ROWS, D), F32),
                pltpu.VMEM((2 * CL * KH, HALF, D), BF16),
                pltpu.SemaphoreType.DMA((2 * CL * KH,)),
            ],
        ),
        compiler_params=pltpu.CompilerParams(vmem_limit_bytes=40 * 2**20),
    )(
        blocks, src, *([recv] * PARTS), home, moved, adjacency, cot, w_self, w_neigh, bias
    )


def rest_kernel(
    src_ref, gp_ref, gm_ref, home_ref, moved_ref, mean_ref, a0_ref, a1_ref, a2_ref, w_ref,
    acc_ref, dw_ref, db_ref, own,
):
    g = pl.program_id(0)

    @pl.when(g == 0)
    def _():
        acc_ref[...] = jnp.zeros_like(acc_ref)
        dw_ref[...] = jnp.zeros_like(dw_ref)
        db_ref[...] = jnp.zeros_like(db_ref)

    gp = gp_ref[...].reshape(ROWS, D)
    gm = gm_ref[...].reshape(ROWS, D)
    own_grad = (dot_nt(gp, w_ref[...]) + gm.astype(F32)).astype(BF16)
    for i in range(GROUP):
        part = own_grad[i * TILE : (i + 1) * TILE]
        slot = g * GROUP + i
        own[pl.ds(i * TILE, TILE)] = own_tile(i, g, home_ref[i], moved_ref)

        @pl.when(slot < OWN)
        def _():
            acc_ref[slot] += part.astype(F32)

        adj = jnp.concatenate([a0_ref[i, 0], a1_ref[i, 0], a2_ref[i, 0]], axis=1)
        grads = dot_tn(adj, gm[i * TILE : (i + 1) * TILE]).astype(BF16).astype(F32)
        for k in range(KL):
            acc_ref[src_ref[slot * KL + k]] += grads[k * TILE : (k + 1) * TILE]
    dw_ref[0] += dot_tn(own[...], gp)
    dw_ref[1] += dot_tn(mean_ref[...].reshape(ROWS, D), gp)
    db_ref[...] += jnp.sum(gp.astype(F32).reshape(ROWS // 8, 8, D), axis=0)


def rest(src, gp, gm, home, moved, mean, adjacency, w_self):
    return pl.pallas_call(
        rest_kernel,
        out_shape=[
            jax.ShapeDtypeStruct((CL, TILE, D), F32),
            jax.ShapeDtypeStruct((2, D, D), F32),
            jax.ShapeDtypeStruct((8, D), F32),
        ],
        grid_spec=pltpu.PrefetchScalarGridSpec(
            num_scalar_prefetch=1,
            grid=(STEPS,),
            in_specs=[tile_block()] * 3
            + [whole(MIG, TILE, D), tile_block()]
            + [adj_block(0), adj_block(1), adj_block(2), whole(D, D)],
            out_specs=[whole(CL, TILE, D), whole(2, D, D), whole(8, D)],
            scratch_shapes=[pltpu.VMEM((ROWS, D), BF16)],
        ),
        compiler_params=pltpu.CompilerParams(vmem_limit_bytes=40 * 2**20),
    )(src, gp, gm, home, moved, mean, adjacency, adjacency, adjacency, w_self)


def final_kernel(target_ref, acc_in, moved_ref, back_ref, passed_ref, out_ref, acc, tiles, sem):
    blocks = back_ref.shape[0]

    def copies(n, act):
        @pl.when(jnp.logical_and(target_ref[n] >= 0, n < blocks))
        def _():
            act(pltpu.make_async_copy(back_ref.at[n], tiles.at[n], sem.at[n]))

        @pl.when(jnp.logical_and(target_ref[n] >= 0, n >= blocks))
        def _():
            act(pltpu.make_async_copy(passed_ref.at[n - blocks], tiles.at[n], sem.at[n]))

    count = blocks + passed_ref.shape[0]
    loop(0, count, lambda n: copies(n, lambda c: c.start()))
    acc[...] = acc_in[...]
    for j in range(MIG):
        for h in range(2):
            acc[2 * (OWN + j) + h] += moved_ref[j, h * HALF : (h + 1) * HALF].astype(F32)

    def add(n):
        copies(n, lambda c: c.wait())

        @pl.when(target_ref[n] >= 0)
        def _():
            acc[target_ref[n]] += tiles[n].astype(F32)

    loop(0, count, add)
    out_ref[...] = acc[...].astype(BF16)


def finish(target, acc, moved, back, passed):
    count = back.shape[0] + passed.shape[0]
    return pl.pallas_call(
        final_kernel,
        out_shape=jax.ShapeDtypeStruct((2 * CL, HALF, D), BF16),
        grid_spec=pltpu.PrefetchScalarGridSpec(
            num_scalar_prefetch=1,
            grid=(),
            in_specs=[VMEM, VMEM, ANY, ANY],
            out_specs=VMEM,
            scratch_shapes=[
                pltpu.VMEM((2 * CL, HALF, D), F32),
                pltpu.VMEM((count, HALF, D), BF16),
                pltpu.SemaphoreType.DMA((count,)),
            ],
        ),
        compiler_params=pltpu.CompilerParams(vmem_limit_bytes=40 * 2**20),
    )(target, acc.reshape(2 * CL, HALF, D), moved, back, passed)


def requests(owner, local):
    entries = jnp.arange(owner.shape[0], dtype=jnp.int32)
    same = owner[:, None] == owner[None, :]
    second = jnp.any(same & (entries[None, :] < entries[:, None]), axis=1)
    partner = (owner[:, None] ^ 1) == owner[None, :]
    fourth = second & (owner % 2 == 1) & jnp.any(partner & second[None, :], axis=1)
    chip = owner // 2

    column = jnp.where(second, jnp.where(fourth, NDOM + CHIPS + chip, NDOM + chip), owner)
    value = jnp.where(second & ~fourth, (owner % 2) * CL + local, local)
    hit = column[:, None] == jnp.arange(128, dtype=jnp.int32)[None, :]
    row = jnp.sum(jnp.where(hit, value[:, None] + 1, 0), axis=0) - 1
    low = jnp.where(fourth, 3 * NDOM + 2 * owner, jnp.where(second, 6 * chip + 2, 3 * owner))
    high = jnp.where(second & ~fourth, low + 3, low + 1)
    return row, jnp.stack([low, high], axis=1).reshape(-1)


def picks(offset, me):
    core, chip = me % 2, me // 2
    swap = offset % 2
    shift = offset // 2 + ((core ^ swap) & swap)
    place = (chip + shift) % CHIPS
    return jnp.concatenate([place % SIDE, place // SIDE, swap]).astype(jnp.int32)


def body(
    features, w_self, w_neigh, out_bias, cluster_plan, local_source, halo_owner, halo_local,
    adjacency, cotangent,
):
    me = lax.axis_index("dom")
    core, chip = me % 2, me // 2
    home = features[0].reshape(CL, TILE, D)
    cot = cotangent[0].reshape(CL, TILE, D)
    src = local_source.reshape(-1)
    bias = out_bias.reshape(1, D)
    row, blocks = requests(halo_owner.reshape(-1), halo_local.reshape(-1))
    offset = (cluster_plan[OWN:] // CL - me + NDOM) % NDOM
    recv, tables, moved = exchange_forward(picks(offset, me), row.reshape(1, 128), home)
    asked = tables[:, 0, :]
    first = lax.dynamic_slice(asked, (0, me), (NDOM, 1))
    other = lax.dynamic_slice(asked, (0, NDOM + chip), (NDOM, 1))
    fourth = lax.dynamic_slice(asked, (0, NDOM + CHIPS + chip), (NDOM, 1))
    first = jnp.where(first >= 0, 2 * first, -2)
    other = jnp.where((other >= 0) & (other // CL == core), 2 * (other % CL), -2)
    target = jnp.concatenate([first, first + 1, other + core], axis=1).reshape(-1)
    target = jnp.concatenate([target, (other + 1 - core).reshape(-1)])
    target = jnp.where(target >= 0, target, -1)

    def rest_of(extra, recv, moved):
        recv = recv.reshape(NDOM * 3, HALF, D)
        goal = target
        if extra:
            sent = home[jnp.maximum(fourth[:, 0], 0)]
            more = lax.all_to_all(sent, "dom", split_axis=0, concat_axis=0, tiled=True)
            recv = jnp.concatenate([recv, more.reshape(NDOM * 2, HALF, D)])
            wide = jnp.where((fourth >= 0) & (core == 1), 2 * fourth, -2)
            wide = jnp.concatenate([wide, wide + 1], axis=1).reshape(-1)
            wide = jnp.where(wide >= 0, wide, -1)
            goal = jnp.concatenate([target[: NDOM * 3], wide, target[NDOM * 3 :]])
        new, gp, mean, gm, tail, back = middle(
            blocks, src, recv, home, moved, adjacency, cot, w_self, w_neigh, bias
        )
        acc, dw, db = rest(src, gp, gm, home, moved, mean, adjacency, w_self)
        ret, passed, returned, dw_sum, db_sum = exchange_backward(
            picks(NDOM - offset, me), back[: NDOM * 3].reshape(NDOM, WIDE, D), tail, dw, db
        )
        ret = ret.reshape(NDOM * 3, HALF, D)
        if extra:
            sent = back[NDOM * 3 :].reshape(NDOM, TILE, D)
            more = lax.all_to_all(sent, "dom", split_axis=0, concat_axis=0, tiled=True)
            ret = jnp.concatenate([ret, more.reshape(NDOM * 2, HALF, D)])
        grad = finish(goal, acc, returned, ret, passed)
        return new, grad, dw_sum, db_sum

    new, grad, dw_sum, db_sum = lax.cond(
        jnp.any(asked[:, NDOM + CHIPS : NDOM + 2 * CHIPS] >= 0),
        functools.partial(rest_of, True),
        functools.partial(rest_of, False),
        recv,
        moved,
    )
    factor = 1.0 / math.sqrt(NDOM * NREP * CL * TILE)
    return (
        new.reshape(1, CL * TILE, D),
        grad.reshape(1, CL * TILE, D),
        dw_sum[0] * factor,
        dw_sum[1] * factor,
        jnp.sum(db_sum, axis=0) * factor,
    )


def solution(mesh):
    return jax.shard_map(
        body,
        mesh=mesh,
        in_specs=(
            P("rep", "dom", None),
            P(),
            P(),
            P(),
            P("dom"),
            P("dom", None),
            P("dom", None),
            P("dom", None),
            P("dom", None, None, None),
            P("rep", "dom", None),
        ),
        out_specs=(P("rep", "dom", None), P("rep", "dom", None), P(), P(), P()),
        check_vma=False,
    )
```

```python
import functools
import math

import jax
import jax.numpy as jnp
from jax import lax
from jax.experimental import pallas as pl
from jax.experimental.pallas import tpu as pltpu
from jax.sharding import PartitionSpec as P

D = 512
TILE = 128
CL = 16
KL = 3
KH = 2
MIG = 3
OWN = CL - MIG
NDOM = 32
NREP = 4
HALF = TILE // 2
WIDE = TILE + HALF
CHUNK = 16
SIDE = 4
GROUP = 4
STEPS = CL // GROUP
ROWS = GROUP * TILE
FACTOR = 1.0 / math.sqrt(NDOM * NREP * CL * TILE)
MESH = pl.DeviceIdType.MESH
F32 = jnp.float32
BF16 = jnp.bfloat16

ANY = pl.BlockSpec(memory_space=pl.ANY)
VMEM = pl.BlockSpec(memory_space=pltpu.VMEM)
SMEM = pl.BlockSpec(memory_space=pltpu.SMEM)


def dot_tn(a, b):
    return lax.dot_general(a, b, (((0,), (0,)), ((), ())), preferred_element_type=F32)


def dot_nt(a, b):
    return lax.dot_general(a, b, (((1,), (1,)), ((), ())), preferred_element_type=F32)


def dot_nn(a, b):
    return jnp.dot(a, b, preferred_element_type=F32)


ZROWS = D // NREP
CHIPS = NDOM // 2
CROWS = ZROWS // CHIPS

ORDER = [
    (1, 0), (3, 0), (0, 1), (0, 3), (1, 1), (3, 3), (1, 3), (3, 1),
    (2, 0), (0, 2), (2, 2), (1, 2), (2, 1), (3, 2), (2, 3),
]
PEERS = [(0, 0, 1)] + [(dx, dy, dc) for dx, dy in ORDER for dc in (0, 1)]
NPEER = len(PEERS)


class Place:
    def __init__(self):
        self.me, self.rep = lax.axis_index("dom"), lax.axis_index("rep")
        self.core, self.chip = lax.rem(self.me, 2), self.me // 2
        self.x, self.y = lax.rem(self.chip, SIDE), self.chip // SIDE
        self.partner = self.chip * 2 + 1 - self.core

    def at(self, dx, dy, dc):
        x, y = lax.rem(self.x + dx, SIDE), lax.rem(self.y + dy, SIDE)
        return (y * SIDE + x) * 2 + lax.rem(self.core + dc, 2)


def loop(low, high, f):
    def step(t, carry):
        f(t)
        return carry

    lax.fori_loop(low, high, step, 0)


def greet_plane(here, barrier):
    def one(t):
        dom = lax.rem(here.me + t, NDOM)
        pl.semaphore_signal(barrier, inc=1, device_id=(dom, here.rep), device_id_type=MESH)

    loop(1, NDOM, one)


def remote(src, dst, send_sem, recv_sem, dom, z):
    return pltpu.make_async_remote_copy(
        src_ref=src,
        dst_ref=dst,
        send_sem=send_sem,
        recv_sem=recv_sem,
        device_id=(dom, z),
        device_id_type=MESH,
    )


class Exchange:
    def __init__(self, here, src, dst, send_sem, recv_sem, first, last):
        self.here, self.src, self.dst = here, src, dst
        self.send_sem, self.recv_sem = send_sem, recv_sem
        self.first, self.last = first, last

    def copy(self, n, rows):
        dom = self.here.at(*PEERS[n])
        return remote(
            self.src.at[dom, rows],
            self.dst.at[self.here.me, rows],
            self.send_sem.at[n],
            self.recv_sem.at[n],
            dom,
            self.here.rep,
        )

    def start(self, low, high):
        def chunk(c):
            rows = pl.ds(pl.multiple_of(self.first + c * CHUNK, CHUNK), CHUNK)
            for n in range(NPEER):
                self.copy(n, rows).start()

        loop(low, high, chunk)

    def every(self, n):
        return self.copy(n, pl.ds(self.first, self.last - self.first))


class Shift:
    def __init__(self, here, pick_ref, along_x, picked, along_y, lanes, sems):
        self.here, self.pick = here, pick_ref
        self.along_x, self.picked, self.along_y, self.lanes = along_x, picked, along_y, lanes
        self.sems = sems

    def sem(self, n):
        return self.sems.at[0, n], self.sems.at[1, n]

    def copy_x(self, t):
        here = self.here
        slot = self.along_x.at[here.x]
        return remote(slot, slot, *self.sem(t), here.at(t, 0, 0), here.rep)

    def copy_y(self, t):
        here = self.here
        return remote(
            self.picked, self.along_y.at[here.y], *self.sem(SIDE + t), here.at(0, t, 0), here.rep
        )

    def copy_lane(self):
        here = self.here
        slot = self.lanes.at[here.core]
        return remote(slot, slot, *self.sem(0), here.partner, here.rep)

    def start_x(self):
        loop(1, SIDE, lambda t: self.copy_x(t).start())

    def start_y(self):
        loop(1, SIDE, lambda t: self.copy_x(t).wait())
        for j in range(MIG):
            self.picked[j] = self.along_x[self.pick[j], j]
        self.along_y[self.here.y] = self.picked[...]
        loop(1, SIDE, lambda t: self.copy_y(t).start())

    def start_lane(self):
        loop(1, SIDE, lambda t: self.copy_y(t).wait())
        for j in range(MIG):
            self.lanes[self.here.core, j] = self.along_y[self.pick[MIG + j], j]
        self.copy_lane().start()

    def finish(self, out_ref):
        self.copy_lane().wait()
        for j in range(MIG):
            out_ref[j] = self.lanes[lax.rem(self.here.core + self.pick[2 * MIG + j], 2), j]


SHIFT_SCRATCH = [
    pltpu.VMEM((SIDE, MIG, TILE, D), BF16),
    pltpu.VMEM((MIG, TILE, D), BF16),
    pltpu.VMEM((SIDE, MIG, TILE, D), BF16),
    pltpu.VMEM((2, MIG, TILE, D), BF16),
    pltpu.SemaphoreType.DMA((2, 2 * SIDE)),
]
EXCHANGE_SEMS = pltpu.SemaphoreType.DMA((2, NPEER))


def forward_kernel(
    pick_ref, row_ref, home_ref,
    recv_ref, table_ref, moved_ref,
    feat, stage, asked, along_x, picked, along_y, lanes, shift_sems,
    table_sems, tile_sems, local_sems,
):
    here = Place()
    me, core, rep = here.me, here.core, here.rep
    barrier = pltpu.get_barrier_semaphore()
    greet_plane(here, barrier)
    own = feat.at[pl.ds(core * CL, CL)]
    take = pltpu.make_async_copy(home_ref, own, local_sems.at[0])
    take.start()
    mine = pltpu.make_async_copy(home_ref.at[pl.ds(OWN, MIG)], along_x.at[here.x], local_sems.at[1])
    mine.start()
    table_ref[me] = row_ref[...]
    pl.semaphore_wait(barrier, NDOM - 1)

    def table(n):
        return remote(
            row_ref, table_ref.at[me], table_sems.at[0, n], table_sems.at[1, n],
            lax.rem(me + n, NDOM), rep,
        )

    loop(1, NDOM, lambda n: table(n).start())
    share = remote(home_ref, own, local_sems.at[2], local_sems.at[3], here.partner, rep)
    share.start()
    shift = Shift(here, pick_ref, along_x, picked, along_y, lanes, shift_sems)
    mine.wait()
    shift.start_x()
    loop(1, NDOM, lambda n: table(n).wait())
    read = pltpu.make_async_copy(table_ref, asked, local_sems.at[4])
    read.start()
    read.wait()
    take.wait()
    share.wait()

    def gather(p):
        first = asked[p, 0, me]
        other = asked[p, 0, NDOM + here.chip]
        stage[p, pl.ds(0, TILE)] = feat[core * CL + jnp.maximum(first, 0)]
        stage[p, pl.ds(TILE, HALF)] = feat[
            jnp.maximum(other, 0), pl.ds(pl.multiple_of(core * HALF, HALF), HALF)
        ]

    loop(0, NDOM, gather)
    keep = pltpu.make_async_copy(stage.at[me], recv_ref.at[me], local_sems.at[5])
    keep.start()
    tiles = Exchange(here, stage, recv_ref, tile_sems.at[0], tile_sems.at[1], 0, WIDE)
    tiles.start(0, 4)
    shift.start_y()
    tiles.start(4, 8)
    shift.start_lane()
    tiles.start(8, WIDE // CHUNK)
    shift.finish(moved_ref)
    keep.wait()
    for n in range(NPEER):
        tiles.every(n).wait()


def exchange_forward(pick, row, home):
    return pl.pallas_call(
        forward_kernel,
        out_shape=[
            jax.ShapeDtypeStruct((NDOM, WIDE, D), BF16),
            jax.ShapeDtypeStruct((NDOM, 1, 128), jnp.int32),
            jax.ShapeDtypeStruct((MIG, TILE, D), BF16),
        ],
        in_specs=[SMEM, VMEM, ANY],
        out_specs=[ANY, VMEM, VMEM],
        scratch_shapes=[
            pltpu.VMEM((2 * CL, TILE, D), BF16),
            pltpu.VMEM((NDOM, WIDE, D), BF16),
            pltpu.SMEM((NDOM, 1, 128), jnp.int32),
        ]
        + SHIFT_SCRATCH
        + [pltpu.SemaphoreType.DMA((2, NDOM)), EXCHANGE_SEMS, pltpu.SemaphoreType.DMA((6,))],
        compiler_params=pltpu.CompilerParams(
            collective_id=0, has_side_effects=True, vmem_limit_bytes=32 * 2**20
        ),
    )(pick, row, home)


NEAR = CL * KL


def backward_kernel(
    pick_ref, order_ref, back_ref, tail_ref, gp_ref, gm_ref, mean_ref, home_ref, moved_in, adj_ref, w_ref,
    ret_ref, passed_ref, moved_ref, acc_ref, out_ref, bias_ref,
    along_x, picked, along_y, lanes, shift_sems,
    r1, b1, s1, r2, b2, s2, r3, b3, sums, half_sems, tile_sems, pass_sems, local_sems,
    gp, gm, mean, own, adj, w, dw, db, acc, running,
):
    here = Place()
    me, core, chip, rep, partner = here.me, here.core, here.chip, here.rep, here.partner
    barrier = pltpu.get_barrier_semaphore()

    def z_peer(t):
        return lax.rem(rep + t, NREP)

    def chip_peer(t):
        return lax.rem(chip + t, CHIPS)

    def greet_z(t):
        pl.semaphore_signal(barrier, inc=1, device_id=(me, z_peer(t)), device_id_type=MESH)

    greet_plane(here, barrier)
    loop(1, NREP, greet_z)
    keep = pltpu.make_async_copy(back_ref.at[me], ret_ref.at[me], local_sems.at[0])
    keep.start()
    loads = [
        pltpu.make_async_copy(src, dst, local_sems.at[1 + n])
        for n, (src, dst) in enumerate(
            [
                (gp_ref, gp),
                (home_ref.at[pl.ds(0, OWN)], own.at[pl.ds(0, OWN)]),
                (moved_in, own.at[pl.ds(OWN, MIG)]),
                (mean_ref, mean),
                (gm_ref, gm),
                (w_ref, w),
                (adj_ref, adj),
            ]
        )
    ]
    for copy in loads:
        copy.start()
    along_x[here.x] = tail_ref[...]
    pl.semaphore_wait(barrier, NDOM - 1 + NREP - 1)

    def send(src, dst, n, dom, z):
        return remote(src, dst, sums.at[0, n], sums.at[1, n], dom, z)

    shift = Shift(here, pick_ref, along_x, picked, along_y, lanes, shift_sems)
    halves = Exchange(here, back_ref, ret_ref, half_sems.at[0], half_sems.at[1], TILE, WIDE)
    tiles = Exchange(here, back_ref, ret_ref, tile_sems.at[0], tile_sems.at[1], 0, TILE)
    shift.start_x()
    halves.start(0, HALF // CHUNK)

    dw[...] = jnp.zeros_like(dw)
    db[...] = jnp.zeros_like(db)
    for copy in loads[:4]:
        copy.wait()

    def weights(g):
        rows = pl.ds(g * GROUP, GROUP)
        grad = gp[rows].reshape(ROWS, D)
        dw[0] += dot_tn(own[rows].reshape(ROWS, D), grad)
        dw[1] += dot_tn(mean[rows].reshape(ROWS, D), grad)
        db[...] += jnp.sum(grad.astype(F32).reshape(ROWS // 8, 8, D), axis=0)

    loop(0, STEPS, weights)

    c_dw = send(dw.at[1 - core], r1, 0, partner, rep)
    c_db = send(db, b1, 1, partner, rep)
    c_dw.start()
    c_db.start()
    tiles.start(0, 1)
    c_db.wait()
    c_dw.wait()
    s1[...] = dw[core] + r1[...]
    b2[rep] = db[...] + b1[...]

    def z_dw(t):
        z = z_peer(t)
        return send(s1.at[pl.ds(z * ZROWS, ZROWS)], r2.at[rep], 2 + t, me, z)

    def z_db(t):
        return send(b2.at[rep], b2.at[rep], 6 + t, me, z_peer(t))

    loop(1, NREP, lambda t: z_dw(t).start())
    loop(1, NREP, lambda t: z_db(t).start())
    r2[rep] = s1[pl.ds(pl.multiple_of(rep * ZROWS, ZROWS), ZROWS)]
    tiles.start(1, 2)
    shift.start_y()

    for copy in loads[4:]:
        copy.wait()

    def kept(g):
        rows = pl.ds(g * GROUP, GROUP)
        part = dot_nt(gp[rows].reshape(ROWS, D), w[...]) + gm[rows].reshape(ROWS, D).astype(F32)
        acc[rows] = part.reshape(GROUP, TILE, D)

    loop(0, STEPS, kept)
    acc[pl.ds(OWN, MIG)] = jnp.zeros((MIG, TILE, D), F32)

    loop(1, NREP, lambda t: z_db(t).wait())
    loop(1, NREP, lambda t: z_dw(t).wait())
    s2[...] = (r2[0] + r2[1]) + (r2[2] + r2[3])
    b3[chip] = (b2[0] + b2[1]) + (b2[2] + b2[3])

    def p_dw(t):
        q = chip_peer(t)
        return send(s2.at[pl.ds(q * CROWS, CROWS)], r3.at[chip], 10 + t, q * 2 + core, rep)

    def p_db(t):
        return send(b3.at[chip], b3.at[chip], 26 + t, chip_peer(t) * 2 + core, rep)

    loop(1, CHIPS, lambda t: p_dw(t).start())
    loop(1, CHIPS, lambda t: p_db(t).start())
    r3[chip] = s2[pl.ds(pl.multiple_of(chip * CROWS, CROWS), CROWS)]
    tiles.start(2, 4)
    shift.start_lane()

    running[0] = jnp.zeros((TILE, D), F32)

    def near(n):
        e = order_ref[n]
        running[n + 1] = running[n] + dot_tn(adj[e // KL, e % KL], gm[e // KL])

    loop(0, NEAR, near)

    def settle(h):
        acc[h] += running[order_ref[NEAR + h + 1]] - running[order_ref[NEAR + h]]

    loop(0, CL, settle)
    store = pltpu.make_async_copy(acc, acc_ref, local_sems.at[8])
    store.start()

    loop(1, CHIPS, lambda t: p_dw(t).wait())
    total = r3[0]
    for q in range(1, CHIPS):
        total = total + r3[q]
    mine = out_ref.at[core, pl.ds(pl.multiple_of(rep * ZROWS + chip * CROWS, CROWS), CROWS)]
    mine[...] = total

    def p_out(t):
        return send(mine, mine, 42 + t, chip_peer(t) * 2 + core, rep)

    loop(1, CHIPS, lambda t: p_out(t).start())
    tiles.start(4, 6)
    shift.finish(moved_ref)
    loop(1, CHIPS, lambda t: p_db(t).wait())
    bias = b3[0]
    for q in range(1, CHIPS):
        bias = bias + b3[q]
    bias_ref[...] = bias
    loop(1, CHIPS, lambda t: p_out(t).wait())
    block = out_ref.at[core, pl.ds(pl.multiple_of(rep * ZROWS, ZROWS), ZROWS)]

    def z_out(t):
        return send(block, block, 58 + t, me, z_peer(t))

    loop(1, NREP, lambda t: z_out(t).start())
    tiles.start(6, TILE // CHUNK)

    def pass_on(src, n):
        rows = pl.ds(TILE, HALF)
        return remote(
            ret_ref.at[src, rows], passed_ref.at[src], pass_sems.at[0, n], pass_sems.at[1, n],
            partner, rep,
        )

    keep.wait()
    pass_on(me, NPEER).start()
    for n, (dx, dy, dc) in enumerate(PEERS):
        halves.every(n).wait()
        pass_on(here.at(SIDE - dx, SIDE - dy, dc), n).start()
    loop(1, NREP, lambda t: z_out(t).wait())
    last = send(out_ref.at[core], out_ref.at[core], 62, partner, rep)
    last.start()
    pass_on(me, NPEER).wait()
    for n, (dx, dy, dc) in enumerate(PEERS):
        pass_on(here.at(SIDE - dx, SIDE - dy, dc), n).wait()
    for n in range(NPEER):
        tiles.every(n).wait()
    last.wait()
    store.wait()


def exchange_backward(pick, order, back, tail, gp, gm, mean, home, moved, adjacency, w_self):
    tiles = pltpu.VMEM((CL, TILE, D), BF16)
    return pl.pallas_call(
        backward_kernel,
        out_shape=[
            jax.ShapeDtypeStruct((NDOM, WIDE, D), BF16),
            jax.ShapeDtypeStruct((NDOM, HALF, D), BF16),
            jax.ShapeDtypeStruct((MIG, TILE, D), BF16),
            jax.ShapeDtypeStruct((CL, TILE, D), F32),
            jax.ShapeDtypeStruct((2, D, D), F32),
            jax.ShapeDtypeStruct((8, D), F32),
        ],
        in_specs=[SMEM, SMEM, ANY, VMEM] + [ANY] * 7,
        out_specs=[ANY, ANY, VMEM, ANY, VMEM, VMEM],
        scratch_shapes=SHIFT_SCRATCH
        + [
            pltpu.VMEM((D, D), F32),
            pltpu.VMEM((8, D), F32),
            pltpu.VMEM((D, D), F32),
            pltpu.VMEM((NREP, ZROWS, D), F32),
            pltpu.VMEM((NREP, 8, D), F32),
            pltpu.VMEM((ZROWS, D), F32),
            pltpu.VMEM((CHIPS, CROWS, D), F32),
            pltpu.VMEM((CHIPS, 8, D), F32),
            pltpu.SemaphoreType.DMA((2, 64)),
            EXCHANGE_SEMS,
            EXCHANGE_SEMS,
            pltpu.SemaphoreType.DMA((2, NDOM)),
            pltpu.SemaphoreType.DMA((9,)),
            tiles,
            tiles,
            tiles,
            tiles,
            pltpu.VMEM((CL, KL + KH, TILE, TILE), BF16),
            pltpu.VMEM((D, D), BF16),
            pltpu.VMEM((2, D, D), F32),
            pltpu.VMEM((8, D), F32),
            pltpu.VMEM((CL, TILE, D), F32),
            pltpu.VMEM((NEAR + 1, TILE, D), F32),
        ],
        compiler_params=pltpu.CompilerParams(
            collective_id=1, has_side_effects=True, vmem_limit_bytes=52 * 2**20
        ),
    )(pick, order, back, tail, gp, gm, mean, home, moved, adjacency, w_self)


def tile_block(width=D):
    return pl.BlockSpec((GROUP, TILE, width), lambda g, *_: (g, 0, 0))


def whole(*shape):
    return pl.BlockSpec(shape, lambda g, *_: (0,) * len(shape))


def adj_block(k):
    return pl.BlockSpec((GROUP, 1, TILE, TILE), lambda g, *_: (g, k, 0, 0))


def own_tile(i, g, home_tile, moved_ref):
    j = CL - GROUP + i - OWN
    if j < 0:
        return home_tile
    return jnp.where(g == STEPS - 1, moved_ref[j], home_tile)


PARTS = 2 * GROUP * KH


def middle_kernel(block_ref, src_ref, *refs):
    halo = refs[:PARTS]
    (home_ref, moved_ref, adj_ref, cot_ref, ws_ref, wn_ref, bias_ref) = refs[PARTS : PARTS + 7]
    (new_ref, gp_ref, mean_ref, gm_ref, tail_ref, back_ref) = refs[PARTS + 7 : PARTS + 13]
    (own, scale, grads, sem) = refs[PARTS + 13 :]
    g = pl.program_id(0)
    for i in range(GROUP):
        slot = g * GROUP + i
        rows = pl.ds(i * TILE, TILE)
        mine = own_tile(i, g, home_ref[slot], moved_ref)
        own[rows] = mine
        adj = jnp.concatenate([adj_ref[i, k] for k in range(KL + KH)], axis=1)
        total = jnp.sum(adj.astype(F32), axis=1, keepdims=True)
        scale[rows] = jnp.broadcast_to(1.0 / (1.0 + total), (TILE, D))
        near = [home_ref[src_ref[slot * KL + k]] for k in range(KL)]
        far = [halo[2 * KH * i + n][0] for n in range(2 * KH)]
        agg = mine.astype(F32) + dot_nn(adj, jnp.concatenate(near + far, axis=0))
        mean_ref[i] = (agg * scale[rows]).astype(BF16)
    pre = (
        dot_nn(own[...], ws_ref[...])
        + dot_nn(mean_ref[...].reshape(ROWS, D), wn_ref[...])
        + bias_ref[...]
    )
    sig = 1.0 / (1.0 + jnp.exp(-pre))
    new_ref[...] = (pre * sig).astype(BF16).reshape(GROUP, TILE, D)
    cot = cot_ref[...].reshape(ROWS, D).astype(F32)
    gp = (cot * sig * (1.0 + pre * (1.0 - sig))).astype(BF16)
    gp_ref[...] = gp.reshape(GROUP, TILE, D)
    gm = (dot_nt(gp, wn_ref[...]) * scale[...]).astype(BF16)
    gm_ref[...] = gm.reshape(GROUP, TILE, D)

    def copy(n):
        return pltpu.make_async_copy(grads.at[n], back_ref.at[block_ref[n]], sem.at[n])

    for i in range(GROUP):
        adj = jnp.concatenate([adj_ref[i, KL + k] for k in range(KH)], axis=1)
        both = dot_tn(adj, gm[i * TILE : (i + 1) * TILE]).astype(BF16)
        for part in range(2 * KH):
            n = (g * GROUP + i) * 2 * KH + part
            grads[n] = both[part * HALF : (part + 1) * HALF]
            copy(n).start()

    @pl.when(g == STEPS - 1)
    def _():
        first = TILE * (GROUP - MIG)
        tail = dot_nt(gp[first:], ws_ref[...]) + gm[first:].astype(F32)
        tail_ref[...] = tail.astype(BF16).reshape(MIG, TILE, D)
        loop(0, 2 * CL * KH, lambda n: copy(n).wait())


def middle(blocks, src, recv, home, moved, adjacency, cot, w_self, w_neigh, bias):
    def halo_block(n):
        return pl.BlockSpec((1, HALF, D), lambda g, blocks, src: (blocks[g * PARTS + n], 0, 0))

    tiles = jax.ShapeDtypeStruct((CL, TILE, D), BF16)
    return pl.pallas_call(
        middle_kernel,
        out_shape=[
            tiles, tiles, tiles, tiles,
            jax.ShapeDtypeStruct((MIG, TILE, D), BF16),
            jax.ShapeDtypeStruct(recv.shape, BF16),
        ],
        grid_spec=pltpu.PrefetchScalarGridSpec(
            num_scalar_prefetch=2,
            grid=(STEPS,),
            in_specs=[halo_block(n) for n in range(PARTS)]
            + [
                whole(CL, TILE, D),
                whole(MIG, TILE, D),
                pl.BlockSpec((GROUP, KL + KH, TILE, TILE), lambda g, *_: (g, 0, 0, 0)),
                tile_block(),
                whole(D, D),
                whole(D, D),
                whole(1, D),
            ],
            out_specs=[tile_block()] * 4 + [whole(MIG, TILE, D), ANY],
            scratch_shapes=[
                pltpu.VMEM((ROWS, D), BF16),
                pltpu.VMEM((ROWS, D), F32),
                pltpu.VMEM((2 * CL * KH, HALF, D), BF16),
                pltpu.SemaphoreType.DMA((2 * CL * KH,)),
            ],
        ),
        compiler_params=pltpu.CompilerParams(vmem_limit_bytes=40 * 2**20),
    )(
        blocks, src, *([recv] * PARTS), home, moved, adjacency, cot, w_self, w_neigh, bias
    )


FOUR = 4


def final_kernel(first_ref, other_ref, more_ref, acc_ref, moved_ref, back_ref, passed_ref, *refs):
    extra_ref = refs[0] if len(refs) == 8 else None
    dw_ref, db_ref, out_ref, dws_ref, dwn_ref, bias_ref, acc = refs[-7:]
    g = pl.program_id(0)
    here_half = lax.rem(lax.axis_index("dom"), 2)
    dws_ref[...] = dw_ref[0] * FACTOR
    dwn_ref[...] = dw_ref[1] * FACTOR

    @pl.when(g == 0)
    def _():
        bias_ref[...] = jnp.sum(db_ref[...], axis=0, keepdims=True) * FACTOR
        acc[...] = acc_ref[...]
        for j in range(MIG):
            acc[OWN + j] += moved_ref[j].astype(F32)

    for n in range(FOUR):
        c = g * FOUR + n
        first, other = first_ref[c], other_ref[c]

        @pl.when(first >= 0)
        def _():
            acc[first] += back_ref[n, pl.ds(0, TILE)].astype(F32)

        @pl.when(other >= 0)
        def _():
            rows = pl.ds(pl.multiple_of(here_half * HALF, HALF), HALF)
            acc[other, rows] += back_ref[n, pl.ds(TILE, HALF)].astype(F32)
            rows = pl.ds(pl.multiple_of((1 - here_half) * HALF, HALF), HALF)
            acc[other, rows] += passed_ref[n].astype(F32)

        if extra_ref is not None:
            more = more_ref[c]

            @pl.when(more >= 0)
            def _():
                acc[more] += extra_ref[n].astype(F32)

    @pl.when(g == NDOM // FOUR - 1)
    def _():
        out_ref[...] = acc[...].astype(BF16)


def finish(first, other, more, acc, moved, back, passed, extra, dw, db):
    steps = NDOM // FOUR

    def four(rows):
        return pl.BlockSpec((FOUR, rows, D), lambda g, *_: (g, 0, 0))

    extras = [] if extra is None else [extra]
    return pl.pallas_call(
        final_kernel,
        out_shape=[
            jax.ShapeDtypeStruct((CL, TILE, D), BF16),
            jax.ShapeDtypeStruct((D, D), F32),
            jax.ShapeDtypeStruct((D, D), F32),
            jax.ShapeDtypeStruct((1, D), F32),
        ],
        grid_spec=pltpu.PrefetchScalarGridSpec(
            num_scalar_prefetch=3,
            grid=(steps,),
            in_specs=[whole(CL, TILE, D), whole(MIG, TILE, D), four(WIDE), four(HALF)]
            + [four(TILE)] * len(extras)
            + [pl.BlockSpec((2, D // steps, D), lambda g, *_: (0, g, 0)), whole(8, D)],
            out_specs=[whole(CL, TILE, D)]
            + [pl.BlockSpec((D // steps, D), lambda g, *_: (g, 0))] * 2
            + [whole(1, D)],
            scratch_shapes=[pltpu.VMEM((CL, TILE, D), F32)],
        ),
        compiler_params=pltpu.CompilerParams(vmem_limit_bytes=40 * 2**20),
    )(first, other, more, acc, moved, back, passed, *extras, dw, db)


def requests(owner, local):
    entries = jnp.arange(owner.shape[0], dtype=jnp.int32)
    same = owner[:, None] == owner[None, :]
    second = jnp.any(same & (entries[None, :] < entries[:, None]), axis=1)
    partner = (owner[:, None] ^ 1) == owner[None, :]
    fourth = second & (owner % 2 == 1) & jnp.any(partner & second[None, :], axis=1)
    chip = owner // 2

    column = jnp.where(second, jnp.where(fourth, NDOM + CHIPS + chip, NDOM + chip), owner)
    value = jnp.where(second & ~fourth, (owner % 2) * CL + local, local)
    hit = column[:, None] == jnp.arange(128, dtype=jnp.int32)[None, :]
    row = jnp.sum(jnp.where(hit, value[:, None] + 1, 0), axis=0) - 1
    low = jnp.where(fourth, 3 * NDOM + 2 * owner, jnp.where(second, 6 * chip + 2, 3 * owner))
    high = jnp.where(second & ~fourth, low + 3, low + 1)
    return row, jnp.stack([low, high], axis=1).reshape(-1)


def sorted_near(src):
    entries = jnp.arange(NEAR, dtype=jnp.int32)
    ahead = (src[None, :] < src[:, None]) | (
        (src[None, :] == src[:, None]) & (entries[None, :] < entries[:, None])
    )
    rank = jnp.sum(ahead.astype(jnp.int32), axis=1)
    order = jnp.sum(jnp.where(rank[None, :] == entries[:, None], entries[None, :], 0), axis=1)
    begins = jnp.sum(
        (src[None, :] < jnp.arange(CL + 1, dtype=jnp.int32)[:, None]).astype(jnp.int32), axis=1
    )
    return jnp.concatenate([order, begins])


def picks(offset, me):
    core, chip = me % 2, me // 2
    swap = offset % 2
    shift = offset // 2 + ((core ^ swap) & swap)
    place = (chip + shift) % CHIPS
    return jnp.concatenate([place % SIDE, place // SIDE, swap]).astype(jnp.int32)


def body(
    features, w_self, w_neigh, out_bias, cluster_plan, local_source, halo_owner, halo_local,
    adjacency, cotangent,
):
    me = lax.axis_index("dom")
    core, chip = me % 2, me // 2
    home = features[0].reshape(CL, TILE, D)
    cot = cotangent[0].reshape(CL, TILE, D)
    src = local_source.reshape(-1)
    bias = out_bias.reshape(1, D)
    row, blocks = requests(halo_owner.reshape(-1), halo_local.reshape(-1))
    offset = (cluster_plan[OWN:] // CL - me + NDOM) % NDOM
    recv, tables, moved = exchange_forward(picks(offset, me), row.reshape(1, 128), home)
    asked = tables[:, 0, :]
    first = lax.dynamic_slice(asked, (0, me), (NDOM, 1)).reshape(-1)
    other = lax.dynamic_slice(asked, (0, NDOM + chip), (NDOM, 1)).reshape(-1)
    more = lax.dynamic_slice(asked, (0, NDOM + CHIPS + chip), (NDOM, 1)).reshape(-1)
    other = jnp.where((other >= 0) & (other // CL == core), other % CL, -1)
    more_here = jnp.where(core == 1, more, -1)
    order = sorted_near(src)

    def rest_of(extra, recv, moved):
        recv = recv.reshape(NDOM * 3, HALF, D)
        if extra:
            sent = home[jnp.maximum(more, 0)]
            got = lax.all_to_all(sent, "dom", split_axis=0, concat_axis=0, tiled=True)
            recv = jnp.concatenate([recv, got.reshape(NDOM * 2, HALF, D)])
        new, gp, mean, gm, tail, back = middle(
            blocks, src, recv, home, moved, adjacency, cot, w_self, w_neigh, bias
        )
        ret, passed, returned, acc, dw, db = exchange_backward(
            picks(NDOM - offset, me), order, back[: NDOM * 3].reshape(NDOM, WIDE, D), tail,
            gp, gm, mean, home, moved, adjacency, w_self,
        )
        got = None
        if extra:
            sent = back[NDOM * 3 :].reshape(NDOM, TILE, D)
            got = lax.all_to_all(sent, "dom", split_axis=0, concat_axis=0, tiled=True)
        return new, *finish(first, other, more_here, acc, returned, ret, passed, got, dw, db)

    new, grad, dws, dwn, db = lax.cond(
        jnp.any(asked[:, NDOM + CHIPS : NDOM + 2 * CHIPS] >= 0),
        functools.partial(rest_of, True),
        functools.partial(rest_of, False),
        recv,
        moved,
    )
    return (
        new.reshape(1, CL * TILE, D), grad.reshape(1, CL * TILE, D), dws, dwn, db.reshape(D)
    )


def solution(mesh):
    return jax.shard_map(
        body,
        mesh=mesh,
        in_specs=(
            P("rep", "dom", None),
            P(),
            P(),
            P(),
            P("dom"),
            P("dom", None),
            P("dom", None),
            P("dom", None),
            P("dom", None, None, None),
            P("rep", "dom", None),
        ),
        out_specs=(P("rep", "dom", None), P("rep", "dom", None), P(), P(), P()),
        check_vma=False,
    )
```

```python
import functools
import math

import jax
import jax.numpy as jnp
from jax import lax
from jax.experimental import pallas as pl
from jax.experimental.pallas import tpu as pltpu
from jax.sharding import PartitionSpec as P

D = 512
TILE = 128
CL = 16
KL = 3
KH = 2
MIG = 3
OWN = CL - MIG
NDOM = 32
NREP = 4
HALF = TILE // 2
WIDE = TILE + HALF
CHUNK = 16
SIDE = 4
GROUP = 4
STEPS = CL // GROUP
ROWS = GROUP * TILE
VMEM_LIMIT = 60 * 2**20
FACTOR = 1.0 / math.sqrt(NDOM * NREP * CL * TILE)
MESH = pl.DeviceIdType.MESH
F32 = jnp.float32
BF16 = jnp.bfloat16

ANY = pl.BlockSpec(memory_space=pl.ANY)
VMEM = pl.BlockSpec(memory_space=pltpu.VMEM)
SMEM = pl.BlockSpec(memory_space=pltpu.SMEM)


def dot_tn(a, b):
    return lax.dot_general(a, b, (((0,), (0,)), ((), ())), preferred_element_type=F32)


def dot_nt(a, b):
    return lax.dot_general(a, b, (((1,), (1,)), ((), ())), preferred_element_type=F32)


def dot_nn(a, b):
    return jnp.dot(a, b, preferred_element_type=F32)


ZROWS = D // NREP
CHIPS = NDOM // 2
CROWS = ZROWS // CHIPS

ORDER = [
    (1, 0), (3, 0), (0, 1), (0, 3), (1, 1), (3, 3), (1, 3), (3, 1),
    (2, 0), (0, 2), (2, 2), (1, 2), (2, 1), (3, 2), (2, 3),
]
PEERS = [(0, 0, 1)] + [(dx, dy, dc) for dx, dy in ORDER for dc in (0, 1)]
NPEER = len(PEERS)


class Place:
    def __init__(self):
        self.me, self.rep = lax.axis_index("dom"), lax.axis_index("rep")
        self.core, self.chip = lax.rem(self.me, 2), self.me // 2
        self.x, self.y = lax.rem(self.chip, SIDE), self.chip // SIDE
        self.partner = self.chip * 2 + 1 - self.core

    def at(self, dx, dy, dc):
        x, y = lax.rem(self.x + dx, SIDE), lax.rem(self.y + dy, SIDE)
        return (y * SIDE + x) * 2 + lax.rem(self.core + dc, 2)


def loop(low, high, f):
    def step(t, carry):
        f(t)
        return carry

    lax.fori_loop(low, high, step, 0)


def greet_plane(here, barrier):
    def one(t):
        dom = lax.rem(here.me + t, NDOM)
        pl.semaphore_signal(barrier, inc=1, device_id=(dom, here.rep), device_id_type=MESH)

    loop(1, NDOM, one)


def remote(src, dst, send_sem, recv_sem, dom, z):
    return pltpu.make_async_remote_copy(
        src_ref=src,
        dst_ref=dst,
        send_sem=send_sem,
        recv_sem=recv_sem,
        device_id=(dom, z),
        device_id_type=MESH,
    )


class Exchange:
    def __init__(self, here, src, dst, send_sem, recv_sem, first, last):
        self.here, self.src, self.dst = here, src, dst
        self.send_sem, self.recv_sem = send_sem, recv_sem
        self.first, self.last = first, last

    def copy(self, n, rows):
        dom = self.here.at(*PEERS[n])
        return remote(
            self.src.at[dom, rows],
            self.dst.at[self.here.me, rows],
            self.send_sem.at[n],
            self.recv_sem.at[n],
            dom,
            self.here.rep,
        )

    def start(self, low, high):
        def chunk(c):
            rows = pl.ds(pl.multiple_of(self.first + c * CHUNK, CHUNK), CHUNK)
            for n in range(NPEER):
                self.copy(n, rows).start()

        loop(low, high, chunk)

    def every(self, n):
        return self.copy(n, pl.ds(self.first, self.last - self.first))


def scalar_sum(terms):
    total = jnp.int32(0)
    for term in terms:
        total = total + term
    return total


class Ring:
    def __init__(self, here, steps, axis, room, buffers, sems):
        self.here, self.steps, self.axis, self.room, self.sems = here, steps, axis, room, sems
        self.own, self.out, self.near, self.again, self.far = buffers

    def peer(self, t):
        return self.here.at(t, 0, 0) if self.axis == "x" else self.here.at(0, t, 0)

    def ranked(self, chosen):
        rank = [scalar_sum(chosen[:j]) for j in range(MIG)]
        held = [
            scalar_sum(j * chosen[j] * (rank[j] == k).astype(jnp.int32) for j in range(MIG))
            for k in range(self.room)
        ]
        return rank, held

    def plan(self):
        up = [((s == 1) | (s == 2)).astype(jnp.int32) for s in self.steps]
        down = [(s == 3).astype(jnp.int32) for s in self.steps]
        twice = [(s == 2).astype(jnp.int32) for s in self.steps]
        return self.ranked(up), self.ranked(down), self.ranked(twice), up, down, twice

    def copies(self, n):
        room, rep = self.room, self.here.rep
        if n == 2:
            src, dst, to = self.again, self.far, SIDE - 1
        else:
            src = self.out.at[pl.ds(n * room, room)]
            dst = self.near.at[pl.ds(MIG + n * room, room)]
            to = (SIDE - 1, 1)[n]
        return remote(src, dst, self.sems.at[0, n], self.sems.at[1, n], self.peer(to), rep)

    def first(self):
        (_, up_held), (_, down_held), _, _, _, _ = self.plan()
        for k in range(self.room):
            self.out[k] = self.own[up_held[k]]
            self.out[self.room + k] = self.own[down_held[k]]
        self.near[pl.ds(0, MIG)] = self.own[...]
        self.copies(0).start()
        self.copies(1).start()

    def second(self):
        (up_rank, _), _, (_, twice_held), _, _, _ = self.plan()
        self.copies(0).wait()
        self.copies(1).wait()
        for k in range(self.room):
            slot = scalar_sum(
                up_rank[j] * (twice_held[k] == j).astype(jnp.int32) for j in range(MIG)
            )
            self.again[k] = self.near[MIG + jnp.minimum(slot, self.room - 1)]
        self.copies(2).start()

    def finish(self):
        self.copies(2).wait()

    def result(self, j):
        (up_rank, _), (down_rank, _), (twice_rank, _), up, down, twice = self.plan()
        at = j + up[j] * (MIG + up_rank[j] - j) + down[j] * (MIG + self.room + down_rank[j] - j)
        late = self.far[jnp.minimum(twice_rank[j], self.room - 1)]
        soon = self.near[jnp.minimum(at, MIG + 2 * self.room - 1)]
        return jnp.where(twice[j] == 1, late, soon)


class Shift:
    def __init__(self, here, plan_ref, sign, room, scratch):
        self.here = here
        ring_x, ring_y, self.lanes, self.sems = scratch[:5], scratch[5:10], scratch[10], scratch[11]
        along_x, along_y, self.swaps = [], [], []
        for j in range(MIG):
            offset = lax.rem(plan_ref[OWN + j] // CL - here.me + NDOM, NDOM)
            if sign < 0:
                offset = lax.rem(NDOM - offset, NDOM)
            swap = lax.rem(offset, 2)
            to = lax.rem(here.core + swap, 2)
            shift = offset // 2 + to * swap
            carry = (here.x + lax.rem(shift, SIDE)) // SIDE
            along_x.append(lax.rem(shift, SIDE))
            along_y.append(lax.rem(shift // SIDE + carry, SIDE))
            self.swaps.append(swap)
        self.x = Ring(here, along_x, "x", room, ring_x, self.sems.at[0])
        self.y = Ring(here, along_y, "y", room, ring_y, self.sems.at[1])

    def copy_lane(self):
        slot = self.lanes.at[self.here.core]
        send_sem, recv_sem = self.sems.at[2, 0, 0], self.sems.at[2, 1, 0]
        return remote(slot, slot, send_sem, recv_sem, self.here.partner, self.here.rep)

    def turn(self):
        self.x.finish()
        for j in range(MIG):
            self.y.own[j] = self.x.result(j)
        self.y.first()

    def start_lane(self):
        self.y.finish()
        for j in range(MIG):
            self.lanes[self.here.core, j] = self.y.result(j)
        self.copy_lane().start()

    def finish(self, out_ref):
        self.copy_lane().wait()
        for j in range(MIG):
            out_ref[j] = self.lanes[lax.rem(self.here.core + self.swaps[j], 2), j]


def shift_scratch(room):
    ring = [
        pltpu.VMEM((MIG, TILE, D), BF16),
        pltpu.VMEM((2 * room, TILE, D), BF16),
        pltpu.VMEM((MIG + 2 * room, TILE, D), BF16),
        pltpu.VMEM((room, TILE, D), BF16),
        pltpu.VMEM((room, TILE, D), BF16),
    ]
    return ring + ring + [
        pltpu.VMEM((2, MIG, TILE, D), BF16),
        pltpu.SemaphoreType.DMA((3, 2, 3)),
    ]


SHIFT_REFS = 12


def few_ways(offset):
    fits = jnp.bool_(True)
    for signed in (offset, (NDOM - offset) % NDOM):
        swap = signed % 2
        for core in range(2):
            shift = signed // 2 + ((core + swap) % 2) * swap
            for x in range(SIDE):
                along_x = shift % SIDE
                along_y = (shift // SIDE + (x + along_x) // SIDE) % SIDE
                for steps in (along_x, along_y):
                    up = jnp.sum(((steps == 1) | (steps == 2)).astype(jnp.int32))
                    down = jnp.sum((steps == 3).astype(jnp.int32))
                    fits = fits & (up <= 2) & (down <= 2)
    return fits


EXCHANGE_SEMS = pltpu.SemaphoreType.DMA((2, NPEER))


def forward_kernel(room, plan_ref, row_ref, home_ref, recv_ref, table_ref, moved_ref, *scratch):
    feat, stage, asked, table_sems, tile_sems, local_sems = scratch[:6]
    here = Place()
    me, core, rep = here.me, here.core, here.rep
    barrier = pltpu.get_barrier_semaphore()
    greet_plane(here, barrier)
    own = feat.at[pl.ds(core * CL, CL)]
    take = pltpu.make_async_copy(home_ref, own, local_sems.at[0])
    take.start()
    shift = Shift(here, plan_ref, 1, room, scratch[6:])
    mine = pltpu.make_async_copy(home_ref.at[pl.ds(OWN, MIG)], shift.x.own, local_sems.at[1])
    mine.start()
    table_ref[me] = row_ref[...]
    pl.semaphore_wait(barrier, NDOM - 1)

    def table(n):
        return remote(
            row_ref, table_ref.at[me], table_sems.at[0, n], table_sems.at[1, n],
            lax.rem(me + n, NDOM), rep,
        )

    loop(1, NDOM, lambda n: table(n).start())
    share = remote(home_ref, own, local_sems.at[2], local_sems.at[3], here.partner, rep)
    share.start()
    mine.wait()
    shift.x.first()
    loop(1, NDOM, lambda n: table(n).wait())
    read = pltpu.make_async_copy(table_ref, asked, local_sems.at[4])
    read.start()
    read.wait()
    take.wait()
    share.wait()

    def gather(p):
        first = asked[p, 0, me]
        other = asked[p, 0, NDOM + here.chip]
        stage[p, pl.ds(0, TILE)] = feat[core * CL + jnp.maximum(first, 0)]
        stage[p, pl.ds(TILE, HALF)] = feat[
            jnp.maximum(other, 0), pl.ds(pl.multiple_of(core * HALF, HALF), HALF)
        ]

    loop(0, NDOM, gather)
    keep = pltpu.make_async_copy(stage.at[me], recv_ref.at[me], local_sems.at[5])
    keep.start()
    tiles = Exchange(here, stage, recv_ref, tile_sems.at[0], tile_sems.at[1], 0, WIDE)
    tiles.start(0, 2)
    shift.x.second()
    tiles.start(2, 4)
    shift.turn()
    tiles.start(4, 6)
    shift.y.second()
    tiles.start(6, 9)
    shift.start_lane()
    tiles.start(9, WIDE // CHUNK)
    keep.wait()
    for n in range(NPEER):
        tiles.every(n).wait()
    shift.finish(moved_ref)


def exchange_forward(room, plan, row, home):
    return pl.pallas_call(
        functools.partial(forward_kernel, room),
        out_shape=[
            jax.ShapeDtypeStruct((NDOM, WIDE, D), BF16),
            jax.ShapeDtypeStruct((NDOM, 1, 128), jnp.int32),
            jax.ShapeDtypeStruct((MIG, TILE, D), BF16),
        ],
        in_specs=[SMEM, VMEM, ANY],
        out_specs=[ANY, VMEM, VMEM],
        scratch_shapes=[
            pltpu.VMEM((2 * CL, TILE, D), BF16),
            pltpu.VMEM((NDOM, WIDE, D), BF16),
            pltpu.SMEM((NDOM, 1, 128), jnp.int32),
            pltpu.SemaphoreType.DMA((2, NDOM)),
            EXCHANGE_SEMS,
            pltpu.SemaphoreType.DMA((6,)),
        ]
        + shift_scratch(room),
        compiler_params=pltpu.CompilerParams(
            collective_id=room - 2, has_side_effects=True, vmem_limit_bytes=VMEM_LIMIT
        ),
    )(plan, row, home)


NEAR = CL * KL


def backward_kernel(
    room, plan_ref, order_ref, back_ref, tail_ref, gp_ref, gm_ref, mean_ref, home_ref, moved_in,
    adj_ref, w_ref, ret_ref, passed_ref, moved_ref, acc_ref, out_ref, bias_ref, *scratch
):
    r1, b1, s1, r2, b2, s2, r3, b3, sums, half_sems, tile_sems, pass_sems, local_sems = scratch[:13]
    gp, gm, mean, own, adj, w, dw, db, acc, running = scratch[13:23]
    here = Place()
    me, core, chip, rep, partner = here.me, here.core, here.chip, here.rep, here.partner
    barrier = pltpu.get_barrier_semaphore()

    def z_peer(t):
        return lax.rem(rep + t, NREP)

    def chip_peer(t):
        return lax.rem(chip + t, CHIPS)

    def greet_z(t):
        pl.semaphore_signal(barrier, inc=1, device_id=(me, z_peer(t)), device_id_type=MESH)

    greet_plane(here, barrier)
    loop(1, NREP, greet_z)
    keep = pltpu.make_async_copy(back_ref.at[me], ret_ref.at[me], local_sems.at[0])
    keep.start()
    loads = [
        pltpu.make_async_copy(src, dst, local_sems.at[1 + n])
        for n, (src, dst) in enumerate(
            [
                (gp_ref, gp),
                (home_ref.at[pl.ds(0, OWN)], own.at[pl.ds(0, OWN)]),
                (moved_in, own.at[pl.ds(OWN, MIG)]),
                (mean_ref, mean),
                (gm_ref, gm),
                (w_ref, w),
                (adj_ref, adj),
            ]
        )
    ]
    for copy in loads:
        copy.start()
    shift = Shift(here, plan_ref, -1, room, scratch[23:])
    shift.x.own[...] = tail_ref[...]
    pl.semaphore_wait(barrier, NDOM - 1 + NREP - 1)

    def send(src, dst, n, dom, z):
        return remote(src, dst, sums.at[0, n], sums.at[1, n], dom, z)

    halves = Exchange(here, back_ref, ret_ref, half_sems.at[0], half_sems.at[1], TILE, WIDE)
    tiles = Exchange(here, back_ref, ret_ref, tile_sems.at[0], tile_sems.at[1], 0, TILE)
    shift.x.first()
    halves.start(0, HALF // CHUNK)

    dw[...] = jnp.zeros_like(dw)
    db[...] = jnp.zeros_like(db)
    for copy in loads[:4]:
        copy.wait()

    def weights(g):
        rows = pl.ds(g * GROUP, GROUP)
        grad = gp[rows].reshape(ROWS, D)
        dw[0] += dot_tn(own[rows].reshape(ROWS, D), grad)
        dw[1] += dot_tn(mean[rows].reshape(ROWS, D), grad)
        db[...] += jnp.sum(grad.astype(F32).reshape(ROWS // 8, 8, D), axis=0)

    loop(0, STEPS, weights)

    c_dw = send(dw.at[1 - core], r1, 0, partner, rep)
    c_db = send(db, b1, 1, partner, rep)
    c_dw.start()
    c_db.start()
    tiles.start(0, 1)
    c_db.wait()
    c_dw.wait()
    s1[...] = dw[core] + r1[...]
    b2[rep] = db[...] + b1[...]

    def z_dw(t):
        z = z_peer(t)
        return send(s1.at[pl.ds(z * ZROWS, ZROWS)], r2.at[rep], 2 + t, me, z)

    def z_db(t):
        return send(b2.at[rep], b2.at[rep], 6 + t, me, z_peer(t))

    loop(1, NREP, lambda t: z_dw(t).start())
    loop(1, NREP, lambda t: z_db(t).start())
    r2[rep] = s1[pl.ds(pl.multiple_of(rep * ZROWS, ZROWS), ZROWS)]
    shift.x.second()
    tiles.start(1, 2)

    for copy in loads[4:]:
        copy.wait()

    def kept(g):
        rows = pl.ds(g * GROUP, GROUP)
        part = dot_nt(gp[rows].reshape(ROWS, D), w[...]) + gm[rows].reshape(ROWS, D).astype(F32)
        acc[rows] = part.astype(BF16).astype(F32).reshape(GROUP, TILE, D)

    loop(0, STEPS, kept)
    acc[pl.ds(OWN, MIG)] = jnp.zeros((MIG, TILE, D), F32)
    shift.turn()

    loop(1, NREP, lambda t: z_db(t).wait())
    loop(1, NREP, lambda t: z_dw(t).wait())
    s2[...] = (r2[0] + r2[1]) + (r2[2] + r2[3])
    b3[chip] = (b2[0] + b2[1]) + (b2[2] + b2[3])

    def p_dw(t):
        q = chip_peer(t)
        return send(s2.at[pl.ds(q * CROWS, CROWS)], r3.at[chip], 10 + t, q * 2 + core, rep)

    def p_db(t):
        return send(b3.at[chip], b3.at[chip], 26 + t, chip_peer(t) * 2 + core, rep)

    loop(1, CHIPS, lambda t: p_dw(t).start())
    loop(1, CHIPS, lambda t: p_db(t).start())
    r3[chip] = s2[pl.ds(pl.multiple_of(chip * CROWS, CROWS), CROWS)]
    tiles.start(2, 4)
    shift.y.second()

    running[0] = jnp.zeros((TILE, D), F32)

    def near(n):
        e = order_ref[n]
        part = dot_tn(adj[e // KL, e % KL], gm[e // KL]).astype(BF16)
        running[n + 1] = running[n] + part.astype(F32)

    loop(0, NEAR, near)

    def settle(h):
        acc[h] += running[order_ref[NEAR + h + 1]] - running[order_ref[NEAR + h]]

    loop(0, CL, settle)
    store = pltpu.make_async_copy(acc, acc_ref, local_sems.at[8])
    store.start()

    loop(1, CHIPS, lambda t: p_dw(t).wait())
    total = r3[0]
    for q in range(1, CHIPS):
        total = total + r3[q]
    mine = out_ref.at[core, pl.ds(pl.multiple_of(rep * ZROWS + chip * CROWS, CROWS), CROWS)]
    mine[...] = total

    def p_out(t):
        return send(mine, mine, 42 + t, chip_peer(t) * 2 + core, rep)

    loop(1, CHIPS, lambda t: p_out(t).start())
    tiles.start(4, 6)
    shift.start_lane()
    loop(1, CHIPS, lambda t: p_db(t).wait())
    bias = b3[0]
    for q in range(1, CHIPS):
        bias = bias + b3[q]
    bias_ref[...] = bias
    loop(1, CHIPS, lambda t: p_out(t).wait())
    block = out_ref.at[core, pl.ds(pl.multiple_of(rep * ZROWS, ZROWS), ZROWS)]

    def z_out(t):
        return send(block, block, 58 + t, me, z_peer(t))

    loop(1, NREP, lambda t: z_out(t).start())
    tiles.start(6, TILE // CHUNK)

    def pass_on(src, n):
        rows = pl.ds(TILE, HALF)
        return remote(
            ret_ref.at[src, rows], passed_ref.at[src], pass_sems.at[0, n], pass_sems.at[1, n],
            partner, rep,
        )

    keep.wait()
    pass_on(me, NPEER).start()
    for n, (dx, dy, dc) in enumerate(PEERS):
        halves.every(n).wait()
        pass_on(here.at(SIDE - dx, SIDE - dy, dc), n).start()
    loop(1, NREP, lambda t: z_out(t).wait())
    last = send(out_ref.at[core], out_ref.at[core], 62, partner, rep)
    last.start()
    pass_on(me, NPEER).wait()
    for n, (dx, dy, dc) in enumerate(PEERS):
        pass_on(here.at(SIDE - dx, SIDE - dy, dc), n).wait()
    for n in range(NPEER):
        tiles.every(n).wait()
    last.wait()
    store.wait()
    shift.finish(moved_ref)


def exchange_backward(room, plan, order, back, tail, gp, gm, mean, home, moved, adjacency, w_self):
    tiles = pltpu.VMEM((CL, TILE, D), BF16)
    return pl.pallas_call(
        functools.partial(backward_kernel, room),
        out_shape=[
            jax.ShapeDtypeStruct((NDOM, WIDE, D), BF16),
            jax.ShapeDtypeStruct((NDOM, HALF, D), BF16),
            jax.ShapeDtypeStruct((MIG, TILE, D), BF16),
            jax.ShapeDtypeStruct((CL, TILE, D), F32),
            jax.ShapeDtypeStruct((2, D, D), F32),
            jax.ShapeDtypeStruct((8, D), F32),
        ],
        in_specs=[SMEM, SMEM, ANY, VMEM] + [ANY] * 7,
        out_specs=[ANY, ANY, VMEM, ANY, VMEM, VMEM],
        scratch_shapes=[
            pltpu.VMEM((D, D), F32),
            pltpu.VMEM((8, D), F32),
            pltpu.VMEM((D, D), F32),
            pltpu.VMEM((NREP, ZROWS, D), F32),
            pltpu.VMEM((NREP, 8, D), F32),
            pltpu.VMEM((ZROWS, D), F32),
            pltpu.VMEM((CHIPS, CROWS, D), F32),
            pltpu.VMEM((CHIPS, 8, D), F32),
            pltpu.SemaphoreType.DMA((2, 64)),
            EXCHANGE_SEMS,
            EXCHANGE_SEMS,
            pltpu.SemaphoreType.DMA((2, NDOM)),
            pltpu.SemaphoreType.DMA((9,)),
            tiles,
            tiles,
            tiles,
            tiles,
            pltpu.VMEM((CL, KL + KH, TILE, TILE), BF16),
            pltpu.VMEM((D, D), BF16),
            pltpu.VMEM((2, D, D), F32),
            pltpu.VMEM((8, D), F32),
            pltpu.VMEM((CL, TILE, D), F32),
            pltpu.VMEM((NEAR + 1, TILE, D), F32),
        ]
        + shift_scratch(room),
        compiler_params=pltpu.CompilerParams(
            collective_id=room, has_side_effects=True, vmem_limit_bytes=VMEM_LIMIT
        ),
    )(plan, order, back, tail, gp, gm, mean, home, moved, adjacency, w_self)


def tile_block(width=D):
    return pl.BlockSpec((GROUP, TILE, width), lambda g, *_: (g, 0, 0))


def whole(*shape):
    return pl.BlockSpec(shape, lambda g, *_: (0,) * len(shape))


def adj_block(k):
    return pl.BlockSpec((GROUP, 1, TILE, TILE), lambda g, *_: (g, k, 0, 0))


def own_tile(i, g, home_tile, moved_ref):
    j = CL - GROUP + i - OWN
    if j < 0:
        return home_tile
    return jnp.where(g == STEPS - 1, moved_ref[j], home_tile)


PARTS = 2 * GROUP * KH


def middle_kernel(block_ref, src_ref, *refs):
    halo = refs[:PARTS]
    (home_ref, moved_ref, adj_ref, cot_ref, ws_ref, wn_ref, bias_ref) = refs[PARTS : PARTS + 7]
    (new_ref, gp_ref, mean_ref, gm_ref, tail_ref, back_ref) = refs[PARTS + 7 : PARTS + 13]
    (own, scale, grads, sem) = refs[PARTS + 13 :]
    g = pl.program_id(0)
    for i in range(GROUP):
        slot = g * GROUP + i
        rows = pl.ds(i * TILE, TILE)
        mine = own_tile(i, g, home_ref[slot], moved_ref)
        own[rows] = mine
        adj = jnp.concatenate([adj_ref[i, k] for k in range(KL + KH)], axis=1)
        total = jnp.sum(adj.astype(F32), axis=1, keepdims=True)
        scale[rows] = jnp.broadcast_to(1.0 / (1.0 + total), (TILE, D))
        near = [home_ref[src_ref[slot * KL + k]] for k in range(KL)]
        far = [halo[2 * KH * i + n][0] for n in range(2 * KH)]
        agg = mine.astype(F32) + dot_nn(adj, jnp.concatenate(near + far, axis=0))
        mean_ref[i] = (agg * scale[rows]).astype(BF16)
    pre = (
        dot_nn(own[...], ws_ref[...])
        + dot_nn(mean_ref[...].reshape(ROWS, D), wn_ref[...])
        + bias_ref[...]
    )
    sig = 1.0 / (1.0 + jnp.exp(-pre))
    new_ref[...] = (pre * sig).astype(BF16).reshape(GROUP, TILE, D)
    cot = cot_ref[...].reshape(ROWS, D).astype(F32)
    gp = (cot * sig * (1.0 + pre * (1.0 - sig))).astype(BF16)
    gp_ref[...] = gp.reshape(GROUP, TILE, D)
    gm = (dot_nt(gp, wn_ref[...]) * scale[...]).astype(BF16)
    gm_ref[...] = gm.reshape(GROUP, TILE, D)

    def copy(n):
        return pltpu.make_async_copy(grads.at[n], back_ref.at[block_ref[n]], sem.at[n])

    for i in range(GROUP):
        adj = jnp.concatenate([adj_ref[i, KL + k] for k in range(KH)], axis=1)
        both = dot_tn(adj, gm[i * TILE : (i + 1) * TILE]).astype(BF16)
        for part in range(2 * KH):
            n = (g * GROUP + i) * 2 * KH + part
            grads[n] = both[part * HALF : (part + 1) * HALF]
            copy(n).start()

    @pl.when(g == STEPS - 1)
    def _():
        first = TILE * (GROUP - MIG)
        tail = dot_nt(gp[first:], ws_ref[...]) + gm[first:].astype(F32)
        tail_ref[...] = tail.astype(BF16).reshape(MIG, TILE, D)
        loop(0, 2 * CL * KH, lambda n: copy(n).wait())


def middle(blocks, src, recv, home, moved, adjacency, cot, w_self, w_neigh, bias):
    def halo_block(n):
        return pl.BlockSpec((1, HALF, D), lambda g, blocks, src: (blocks[g * PARTS + n], 0, 0))

    tiles = jax.ShapeDtypeStruct((CL, TILE, D), BF16)
    return pl.pallas_call(
        middle_kernel,
        out_shape=[
            tiles, tiles, tiles, tiles,
            jax.ShapeDtypeStruct((MIG, TILE, D), BF16),
            jax.ShapeDtypeStruct(recv.shape, BF16),
        ],
        grid_spec=pltpu.PrefetchScalarGridSpec(
            num_scalar_prefetch=2,
            grid=(STEPS,),
            in_specs=[halo_block(n) for n in range(PARTS)]
            + [
                whole(CL, TILE, D),
                whole(MIG, TILE, D),
                pl.BlockSpec((GROUP, KL + KH, TILE, TILE), lambda g, *_: (g, 0, 0, 0)),
                tile_block(),
                whole(D, D),
                whole(D, D),
                whole(1, D),
            ],
            out_specs=[tile_block()] * 4 + [whole(MIG, TILE, D), ANY],
            scratch_shapes=[
                pltpu.VMEM((ROWS, D), BF16),
                pltpu.VMEM((ROWS, D), F32),
                pltpu.VMEM((2 * CL * KH, HALF, D), BF16),
                pltpu.SemaphoreType.DMA((2 * CL * KH,)),
            ],
        ),
        compiler_params=pltpu.CompilerParams(vmem_limit_bytes=VMEM_LIMIT),
    )(
        blocks, src, *([recv] * PARTS), home, moved, adjacency, cot, w_self, w_neigh, bias
    )


FOUR = 4


def final_kernel(first_ref, other_ref, more_ref, acc_ref, moved_ref, back_ref, passed_ref, *refs):
    extra_ref = refs[0] if len(refs) == 8 else None
    dw_ref, db_ref, out_ref, dws_ref, dwn_ref, bias_ref, acc = refs[-7:]
    g = pl.program_id(0)
    here_half = lax.rem(lax.axis_index("dom"), 2)
    dws_ref[...] = dw_ref[0] * FACTOR
    dwn_ref[...] = dw_ref[1] * FACTOR

    @pl.when(g == 0)
    def _():
        bias_ref[...] = jnp.sum(db_ref[...], axis=0, keepdims=True) * FACTOR
        acc[...] = acc_ref[...]
        for j in range(MIG):
            acc[OWN + j] += moved_ref[j].astype(F32)

    for n in range(FOUR):
        c = g * FOUR + n
        first, other = first_ref[c], other_ref[c]

        @pl.when(first >= 0)
        def _():
            acc[first] += back_ref[n, pl.ds(0, TILE)].astype(F32)

        @pl.when(other >= 0)
        def _():
            rows = pl.ds(pl.multiple_of(here_half * HALF, HALF), HALF)
            acc[other, rows] += back_ref[n, pl.ds(TILE, HALF)].astype(F32)
            rows = pl.ds(pl.multiple_of((1 - here_half) * HALF, HALF), HALF)
            acc[other, rows] += passed_ref[n].astype(F32)

        if extra_ref is not None:
            more = more_ref[c]

            @pl.when(more >= 0)
            def _():
                acc[more] += extra_ref[n].astype(F32)

    @pl.when(g == NDOM // FOUR - 1)
    def _():
        out_ref[...] = acc[...].astype(BF16)


def finish(first, other, more, acc, moved, back, passed, extra, dw, db):
    steps = NDOM // FOUR

    def four(rows):
        return pl.BlockSpec((FOUR, rows, D), lambda g, *_: (g, 0, 0))

    extras = [] if extra is None else [extra]
    return pl.pallas_call(
        final_kernel,
        out_shape=[
            jax.ShapeDtypeStruct((CL, TILE, D), BF16),
            jax.ShapeDtypeStruct((D, D), F32),
            jax.ShapeDtypeStruct((D, D), F32),
            jax.ShapeDtypeStruct((1, D), F32),
        ],
        grid_spec=pltpu.PrefetchScalarGridSpec(
            num_scalar_prefetch=3,
            grid=(steps,),
            in_specs=[whole(CL, TILE, D), whole(MIG, TILE, D), four(WIDE), four(HALF)]
            + [four(TILE)] * len(extras)
            + [pl.BlockSpec((2, D // steps, D), lambda g, *_: (0, g, 0)), whole(8, D)],
            out_specs=[whole(CL, TILE, D)]
            + [pl.BlockSpec((D // steps, D), lambda g, *_: (g, 0))] * 2
            + [whole(1, D)],
            scratch_shapes=[pltpu.VMEM((CL, TILE, D), F32)],
        ),
        compiler_params=pltpu.CompilerParams(vmem_limit_bytes=VMEM_LIMIT),
    )(first, other, more, acc, moved, back, passed, *extras, dw, db)


def requests(owner, local):
    entries = jnp.arange(owner.shape[0], dtype=jnp.int32)
    same = owner[:, None] == owner[None, :]
    second = jnp.any(same & (entries[None, :] < entries[:, None]), axis=1)
    partner = (owner[:, None] ^ 1) == owner[None, :]
    fourth = second & (owner % 2 == 1) & jnp.any(partner & second[None, :], axis=1)
    chip = owner // 2

    column = jnp.where(second, jnp.where(fourth, NDOM + CHIPS + chip, NDOM + chip), owner)
    value = jnp.where(second & ~fourth, (owner % 2) * CL + local, local)
    hit = column[:, None] == jnp.arange(128, dtype=jnp.int32)[None, :]
    row = jnp.sum(jnp.where(hit, value[:, None] + 1, 0), axis=0) - 1
    low = jnp.where(fourth, 3 * NDOM + 2 * owner, jnp.where(second, 6 * chip + 2, 3 * owner))
    high = jnp.where(second & ~fourth, low + 3, low + 1)
    return row, jnp.stack([low, high], axis=1).reshape(-1)


def sorted_near(src):
    entries = jnp.arange(NEAR, dtype=jnp.int32)
    ahead = (src[None, :] < src[:, None]) | (
        (src[None, :] == src[:, None]) & (entries[None, :] < entries[:, None])
    )
    rank = jnp.sum(ahead.astype(jnp.int32), axis=1)
    order = jnp.sum(jnp.where(rank[None, :] == entries[:, None], entries[None, :], 0), axis=1)
    begins = jnp.sum(
        (src[None, :] < jnp.arange(CL + 1, dtype=jnp.int32)[:, None]).astype(jnp.int32), axis=1
    )
    return jnp.concatenate([order, begins])


def body(
    features, w_self, w_neigh, out_bias, cluster_plan, local_source, halo_owner, halo_local,
    adjacency, cotangent,
):
    me = lax.axis_index("dom")
    core, chip = me % 2, me // 2
    home = features[0].reshape(CL, TILE, D)
    cot = cotangent[0].reshape(CL, TILE, D)
    src = local_source.reshape(-1)
    bias = out_bias.reshape(1, D)
    row, blocks = requests(halo_owner.reshape(-1), halo_local.reshape(-1))
    offset = (cluster_plan[OWN:] // CL - me + NDOM) % NDOM
    few = few_ways(offset)
    recv, tables, moved = lax.cond(
        few,
        functools.partial(exchange_forward, 2),
        functools.partial(exchange_forward, 3),
        cluster_plan,
        row.reshape(1, 128),
        home,
    )
    asked = tables[:, 0, :]
    first = lax.dynamic_slice(asked, (0, me), (NDOM, 1)).reshape(-1)
    other = lax.dynamic_slice(asked, (0, NDOM + chip), (NDOM, 1)).reshape(-1)
    more = lax.dynamic_slice(asked, (0, NDOM + CHIPS + chip), (NDOM, 1)).reshape(-1)
    other = jnp.where((other >= 0) & (other // CL == core), other % CL, -1)
    more_here = jnp.where(core == 1, more, -1)
    order = sorted_near(src)

    def rest_of(extra, room, recv, moved):
        recv = recv.reshape(NDOM * 3, HALF, D)
        if extra:
            sent = home[jnp.maximum(more, 0)]
            got = lax.all_to_all(sent, "dom", split_axis=0, concat_axis=0, tiled=True)
            recv = jnp.concatenate([recv, got.reshape(NDOM * 2, HALF, D)])
        new, gp, mean, gm, tail, back = middle(
            blocks, src, recv, home, moved, adjacency, cot, w_self, w_neigh, bias
        )
        ret, passed, returned, acc, dw, db = exchange_backward(
            room, cluster_plan, order, back[: NDOM * 3].reshape(NDOM, WIDE, D), tail,
            gp, gm, mean, home, moved, adjacency, w_self,
        )
        got = None
        if extra:
            sent = back[NDOM * 3 :].reshape(NDOM, TILE, D)
            got = lax.all_to_all(sent, "dom", split_axis=0, concat_axis=0, tiled=True)
        return new, *finish(first, other, more_here, acc, returned, ret, passed, got, dw, db)

    extra = jnp.any(asked[:, NDOM + CHIPS : NDOM + 2 * CHIPS] >= 0)
    new, grad, dws, dwn, db = lax.switch(
        2 * extra.astype(jnp.int32) + 1 - few.astype(jnp.int32),
        [functools.partial(rest_of, more, room) for more in (False, True) for room in (2, 3)],
        recv,
        moved,
    )
    return (
        new.reshape(1, CL * TILE, D), grad.reshape(1, CL * TILE, D), dws, dwn, db.reshape(D)
    )


def solution(mesh):
    return jax.shard_map(
        body,
        mesh=mesh,
        in_specs=(
            P("rep", "dom", None),
            P(),
            P(),
            P(),
            P("dom"),
            P("dom", None),
            P("dom", None),
            P("dom", None),
            P("dom", None, None, None),
            P("rep", "dom", None),
        ),
        out_specs=(P("rep", "dom", None), P("rep", "dom", None), P(), P(), P()),
        check_vma=False,
    )
```

```python
import functools
import math

import jax
import jax.numpy as jnp
from jax import lax
from jax.experimental import pallas as pl
from jax.experimental.pallas import tpu as pltpu
from jax.sharding import PartitionSpec as P

D = 512
TILE = 128
CL = 16
KL = 3
KH = 2
MIG = 3
OWN = CL - MIG
NDOM = 32
NREP = 4
HALF = TILE // 2
WIDE = TILE + HALF
FULL = WIDE + TILE
UNITS = FULL // HALF
CHUNK = 16
SIDE = 4
GROUP = 4
STEPS = CL // GROUP
ROWS = GROUP * TILE
VMEM_LIMIT = 60 * 2**20
FACTOR = 1.0 / math.sqrt(NDOM * NREP * CL * TILE)
MESH = pl.DeviceIdType.MESH
F32 = jnp.float32
BF16 = jnp.bfloat16

ANY = pl.BlockSpec(memory_space=pl.ANY)
VMEM = pl.BlockSpec(memory_space=pltpu.VMEM)
SMEM = pl.BlockSpec(memory_space=pltpu.SMEM)


def dot_tn(a, b):
    return lax.dot_general(a, b, (((0,), (0,)), ((), ())), preferred_element_type=F32)


def dot_nt(a, b):
    return lax.dot_general(a, b, (((1,), (1,)), ((), ())), preferred_element_type=F32)


def dot_nn(a, b):
    return jnp.dot(a, b, preferred_element_type=F32)


ZROWS = D // NREP
CHIPS = NDOM // 2
CROWS = ZROWS // CHIPS

ORDER = [
    (1, 0), (3, 0), (0, 1), (0, 3), (1, 1), (3, 3), (1, 3), (3, 1),
    (2, 0), (0, 2), (2, 2), (1, 2), (2, 1), (3, 2), (2, 3),
]
PEERS = [(0, 0, 1)] + [(dx, dy, dc) for dx, dy in ORDER for dc in (0, 1)]
NPEER = len(PEERS)


class Place:
    def __init__(self):
        self.me, self.rep = lax.axis_index("dom"), lax.axis_index("rep")
        self.core, self.chip = lax.rem(self.me, 2), self.me // 2
        self.x, self.y = lax.rem(self.chip, SIDE), self.chip // SIDE
        self.partner = self.chip * 2 + 1 - self.core

    def at(self, dx, dy, dc):
        x, y = lax.rem(self.x + dx, SIDE), lax.rem(self.y + dy, SIDE)
        return (y * SIDE + x) * 2 + lax.rem(self.core + dc, 2)


def loop(low, high, f):
    def step(t, carry):
        f(t)
        return carry

    lax.fori_loop(low, high, step, 0)


def greet_plane(here, barrier):
    def one(t):
        dom = lax.rem(here.me + t, NDOM)
        pl.semaphore_signal(barrier, inc=1, device_id=(dom, here.rep), device_id_type=MESH)

    loop(1, NDOM, one)


def remote(src, dst, send_sem, recv_sem, dom, z):
    return pltpu.make_async_remote_copy(
        src_ref=src,
        dst_ref=dst,
        send_sem=send_sem,
        recv_sem=recv_sem,
        device_id=(dom, z),
        device_id_type=MESH,
    )


class Exchange:
    def __init__(self, here, src, dst, send_sem, recv_sem, first, last):
        self.here, self.src, self.dst = here, src, dst
        self.send_sem, self.recv_sem = send_sem, recv_sem
        self.first, self.last = first, last

    def copy(self, n, rows):
        dom = self.here.at(*PEERS[n])
        return remote(
            self.src.at[dom, rows],
            self.dst.at[self.here.me, rows],
            self.send_sem.at[n],
            self.recv_sem.at[n],
            dom,
            self.here.rep,
        )

    def start(self, low, high):
        def chunk(c):
            rows = pl.ds(pl.multiple_of(self.first + c * CHUNK, CHUNK), CHUNK)
            for n in range(NPEER):
                self.copy(n, rows).start()

        loop(low, high, chunk)

    def every(self, n):
        return self.copy(n, pl.ds(self.first, self.last - self.first))


def scalar_sum(terms):
    total = jnp.int32(0)
    for term in terms:
        total = total + term
    return total


class Ring:
    def __init__(self, here, steps, axis, sign, room, buffers, sems):
        self.here, self.axis, self.room, self.sems = here, axis, room, sems
        self.steps = steps if sign > 0 else [lax.rem(SIDE - s, SIDE) for s in steps]
        self.up_to, self.down_to = (SIDE - 1, 1) if sign > 0 else (1, SIDE - 1)
        self.own, self.out, self.near, self.again, self.far = buffers

    def peer(self, t):
        return self.here.at(t, 0, 0) if self.axis == "x" else self.here.at(0, t, 0)

    def ranked(self, chosen):
        rank = [scalar_sum(chosen[:j]) for j in range(MIG)]
        held = [
            scalar_sum(j * chosen[j] * (rank[j] == k).astype(jnp.int32) for j in range(MIG))
            for k in range(self.room)
        ]
        return rank, held

    def plan(self):
        up = [((s == 1) | (s == 2)).astype(jnp.int32) for s in self.steps]
        down = [(s == 3).astype(jnp.int32) for s in self.steps]
        twice = [(s == 2).astype(jnp.int32) for s in self.steps]
        return self.ranked(up), self.ranked(down), self.ranked(twice), up, down, twice

    def copies(self, n):
        room, rep = self.room, self.here.rep
        if n == 2:
            src, dst, to = self.again, self.far, self.up_to
        else:
            src = self.out.at[pl.ds(n * room, room)]
            dst = self.near.at[pl.ds(MIG + n * room, room)]
            to = (self.up_to, self.down_to)[n]
        return remote(src, dst, self.sems.at[0, n], self.sems.at[1, n], self.peer(to), rep)

    def first(self):
        (_, up_held), (_, down_held), _, _, _, _ = self.plan()
        for k in range(self.room):
            self.out[k] = self.own[up_held[k]]
            self.out[self.room + k] = self.own[down_held[k]]
        self.near[pl.ds(0, MIG)] = self.own[...]
        self.copies(0).start()
        self.copies(1).start()

    def second(self):
        (up_rank, _), _, (_, twice_held), _, _, _ = self.plan()
        self.copies(0).wait()
        self.copies(1).wait()
        for k in range(self.room):
            slot = scalar_sum(
                up_rank[j] * (twice_held[k] == j).astype(jnp.int32) for j in range(MIG)
            )
            self.again[k] = self.near[MIG + jnp.minimum(slot, self.room - 1)]
        self.copies(2).start()

    def finish(self):
        self.copies(2).wait()

    def result(self, j):
        (up_rank, _), (down_rank, _), (twice_rank, _), up, down, twice = self.plan()
        at = j + up[j] * (MIG + up_rank[j] - j) + down[j] * (MIG + self.room + down_rank[j] - j)
        late = self.far[jnp.minimum(twice_rank[j], self.room - 1)]
        soon = self.near[jnp.minimum(at, MIG + 2 * self.room - 1)]
        return jnp.where(twice[j] == 1, late, soon)


class Shift:
    def __init__(self, here, plan_ref, sign, room, scratch):
        self.here = here
        ring_x, ring_y, self.lanes, self.sems = scratch[:5], scratch[5:10], scratch[10], scratch[11]
        along_x, along_y, self.swaps = [], [], []
        for j in range(MIG):
            offset = lax.rem(plan_ref[OWN + j] // CL - here.me + NDOM, NDOM)
            if sign < 0:
                offset = lax.rem(NDOM - offset, NDOM)
            swap = lax.rem(offset, 2)
            to = lax.rem(here.core + swap, 2)
            shift = offset // 2 + to * swap
            carry = (here.x + lax.rem(shift, SIDE)) // SIDE
            along_x.append(lax.rem(shift, SIDE))
            along_y.append(lax.rem(shift // SIDE + carry, SIDE))
            self.swaps.append(swap)
        self.x = Ring(here, along_x, "x", sign, room, ring_x, self.sems.at[0])
        self.y = Ring(here, along_y, "y", sign, room, ring_y, self.sems.at[1])

    def copy_lane(self):
        slot = self.lanes.at[self.here.core]
        send_sem, recv_sem = self.sems.at[2, 0, 0], self.sems.at[2, 1, 0]
        return remote(slot, slot, send_sem, recv_sem, self.here.partner, self.here.rep)

    def turn(self):
        self.x.finish()
        for j in range(MIG):
            self.y.own[j] = self.x.result(j)
        self.y.first()

    def start_lane(self):
        self.y.finish()
        for j in range(MIG):
            self.lanes[self.here.core, j] = self.y.result(j)
        self.copy_lane().start()

    def finish(self, out_ref):
        self.copy_lane().wait()
        for j in range(MIG):
            out_ref[j] = self.lanes[lax.rem(self.here.core + self.swaps[j], 2), j]


def shift_scratch(room):
    ring = [
        pltpu.VMEM((MIG, TILE, D), BF16),
        pltpu.VMEM((2 * room, TILE, D), BF16),
        pltpu.VMEM((MIG + 2 * room, TILE, D), BF16),
        pltpu.VMEM((room, TILE, D), BF16),
        pltpu.VMEM((room, TILE, D), BF16),
    ]
    return ring + ring + [
        pltpu.VMEM((2, MIG, TILE, D), BF16),
        pltpu.SemaphoreType.DMA((3, 2, 3)),
    ]


SHIFT_REFS = 12


def few_ways(offset):
    fits = jnp.bool_(True)
    for sign, signed in ((1, offset), (-1, (NDOM - offset) % NDOM)):
        swap = signed % 2
        for core in range(2):
            shift = signed // 2 + ((core + swap) % 2) * swap
            for x in range(SIDE):
                along_x = shift % SIDE
                along_y = (shift // SIDE + (x + along_x) // SIDE) % SIDE
                for steps in (along_x, along_y):
                    steps = steps if sign > 0 else (SIDE - steps) % SIDE
                    up = jnp.sum(((steps == 1) | (steps == 2)).astype(jnp.int32))
                    down = jnp.sum((steps == 3).astype(jnp.int32))
                    fits = fits & (up <= 2) & (down <= 2)
    return fits


EXCHANGE_SEMS = pltpu.SemaphoreType.DMA((2, NPEER))


def forward_kernel(room, plan_ref, row_ref, home_ref, recv_ref, table_ref, moved_ref, *scratch):
    feat, stage, asked, table_sems, tile_sems, local_sems = scratch[:6]
    here = Place()
    me, core, rep = here.me, here.core, here.rep
    barrier = pltpu.get_barrier_semaphore()
    greet_plane(here, barrier)
    own = feat.at[pl.ds(core * CL, CL)]
    take = pltpu.make_async_copy(home_ref, own, local_sems.at[0])
    take.start()
    shift = Shift(here, plan_ref, 1, room, scratch[6:])
    mine = pltpu.make_async_copy(home_ref.at[pl.ds(OWN, MIG)], shift.x.own, local_sems.at[1])
    mine.start()
    table_ref[me] = row_ref[...]
    pl.semaphore_wait(barrier, NDOM - 1)

    def table(n):
        return remote(
            row_ref, table_ref.at[me], table_sems.at[0, n], table_sems.at[1, n],
            lax.rem(me + n, NDOM), rep,
        )

    loop(1, NDOM, lambda n: table(n).start())
    share = remote(home_ref, own, local_sems.at[2], local_sems.at[3], here.partner, rep)
    share.start()
    mine.wait()
    shift.x.first()
    loop(1, NDOM, lambda n: table(n).wait())
    read = pltpu.make_async_copy(table_ref, asked, local_sems.at[4])
    read.start()
    read.wait()
    take.wait()
    share.wait()

    def gather(p):
        first = asked[p, 0, me]
        other = asked[p, 0, NDOM + here.chip]
        stage[p, pl.ds(0, TILE)] = feat[core * CL + jnp.maximum(first, 0)]
        stage[p, pl.ds(TILE, HALF)] = feat[
            jnp.maximum(other, 0), pl.ds(pl.multiple_of(core * HALF, HALF), HALF)
        ]

    loop(0, NDOM, gather)
    keep = pltpu.make_async_copy(
        stage.at[me], recv_ref.at[me, pl.ds(0, WIDE)], local_sems.at[5]
    )
    keep.start()
    tiles = Exchange(here, stage, recv_ref, tile_sems.at[0], tile_sems.at[1], 0, WIDE)
    tiles.start(0, 2)
    shift.x.second()
    tiles.start(2, 4)
    shift.turn()
    tiles.start(4, 6)
    shift.y.second()
    tiles.start(6, 9)
    shift.start_lane()
    tiles.start(9, WIDE // CHUNK)
    keep.wait()
    for n in range(NPEER):
        tiles.every(n).wait()
    shift.finish(moved_ref)


def exchange_forward(room, plan, row, home):
    return pl.pallas_call(
        functools.partial(forward_kernel, room),
        out_shape=[
            jax.ShapeDtypeStruct((NDOM, FULL, D), BF16),
            jax.ShapeDtypeStruct((NDOM, 1, 128), jnp.int32),
            jax.ShapeDtypeStruct((MIG, TILE, D), BF16),
        ],
        in_specs=[SMEM, VMEM, ANY],
        out_specs=[ANY, VMEM, VMEM],
        scratch_shapes=[
            pltpu.VMEM((2 * CL, TILE, D), BF16),
            pltpu.VMEM((NDOM, WIDE, D), BF16),
            pltpu.SMEM((NDOM, 1, 128), jnp.int32),
            pltpu.SemaphoreType.DMA((2, NDOM)),
            EXCHANGE_SEMS,
            pltpu.SemaphoreType.DMA((6,)),
        ]
        + shift_scratch(room),
        compiler_params=pltpu.CompilerParams(
            collective_id=room - 2, has_side_effects=True, vmem_limit_bytes=VMEM_LIMIT
        ),
    )(plan, row, home)


NEAR = CL * KL


def backward_kernel(
    room, plan_ref, order_ref, back_ref, tail_ref, gp_ref, gm_ref, mean_ref, home_ref, moved_in,
    adj_ref, w_ref, ret_ref, passed_ref, moved_ref, acc_ref, out_ref, bias_ref, *scratch
):
    r1, b1, s1, r2, b2, s2, r3, b3, sums, half_sems, tile_sems, pass_sems, local_sems = scratch[:13]
    gp, gm, mean, own, adj, w, dw, db, acc, running = scratch[13:23]
    here = Place()
    me, core, chip, rep, partner = here.me, here.core, here.chip, here.rep, here.partner
    barrier = pltpu.get_barrier_semaphore()

    def z_peer(t):
        return lax.rem(rep + t, NREP)

    def chip_peer(t):
        return lax.rem(chip + t, CHIPS)

    def greet_z(t):
        pl.semaphore_signal(barrier, inc=1, device_id=(me, z_peer(t)), device_id_type=MESH)

    greet_plane(here, barrier)
    loop(1, NREP, greet_z)
    keep = pltpu.make_async_copy(
        back_ref.at[me, pl.ds(0, WIDE)], ret_ref.at[me], local_sems.at[0]
    )
    keep.start()
    loads = [
        pltpu.make_async_copy(src, dst, local_sems.at[1 + n])
        for n, (src, dst) in enumerate(
            [
                (gp_ref, gp),
                (home_ref.at[pl.ds(0, OWN)], own.at[pl.ds(0, OWN)]),
                (moved_in, own.at[pl.ds(OWN, MIG)]),
                (mean_ref, mean),
                (gm_ref, gm),
                (w_ref, w),
                (adj_ref, adj),
            ]
        )
    ]
    for copy in loads:
        copy.start()
    shift = Shift(here, plan_ref, -1, room, scratch[23:])
    shift.x.own[...] = tail_ref[...]
    pl.semaphore_wait(barrier, NDOM - 1 + NREP - 1)

    def send(src, dst, n, dom, z):
        return remote(src, dst, sums.at[0, n], sums.at[1, n], dom, z)

    halves = Exchange(here, back_ref, ret_ref, half_sems.at[0], half_sems.at[1], TILE, WIDE)
    tiles = Exchange(here, back_ref, ret_ref, tile_sems.at[0], tile_sems.at[1], 0, TILE)
    shift.x.first()
    halves.start(0, 2)

    dw[...] = jnp.zeros_like(dw)
    db[...] = jnp.zeros_like(db)
    for copy in loads[:4]:
        copy.wait()

    def weights(g):
        rows = pl.ds(g * GROUP, GROUP)
        grad = gp[rows].reshape(ROWS, D)
        dw[0] += dot_tn(own[rows].reshape(ROWS, D), grad)
        dw[1] += dot_tn(mean[rows].reshape(ROWS, D), grad)
        db[...] += jnp.sum(grad.astype(F32).reshape(ROWS // 8, 8, D), axis=0)

    loop(0, STEPS, weights)

    c_dw = send(dw.at[1 - core], r1, 0, partner, rep)
    c_db = send(db, b1, 1, partner, rep)
    c_dw.start()
    c_db.start()
    halves.start(2, 3)
    shift.x.second()
    halves.start(3, 4)
    c_db.wait()
    c_dw.wait()
    s1[...] = dw[core] + r1[...]
    b2[rep] = db[...] + b1[...]

    def z_dw(t):
        z = z_peer(t)
        return send(s1.at[pl.ds(z * ZROWS, ZROWS)], r2.at[rep], 2 + t, me, z)

    def z_db(t):
        return send(b2.at[rep], b2.at[rep], 6 + t, me, z_peer(t))

    loop(1, NREP, lambda t: z_dw(t).start())
    loop(1, NREP, lambda t: z_db(t).start())
    r2[rep] = s1[pl.ds(pl.multiple_of(rep * ZROWS, ZROWS), ZROWS)]
    shift.turn()
    tiles.start(0, 2)

    for copy in loads[4:]:
        copy.wait()

    def kept(g):
        rows = pl.ds(g * GROUP, GROUP)
        part = dot_nt(gp[rows].reshape(ROWS, D), w[...]) + gm[rows].reshape(ROWS, D).astype(F32)
        acc[rows] = part.astype(BF16).astype(F32).reshape(GROUP, TILE, D)

    loop(0, STEPS, kept)
    acc[pl.ds(OWN, MIG)] = jnp.zeros((MIG, TILE, D), F32)

    loop(1, NREP, lambda t: z_db(t).wait())
    loop(1, NREP, lambda t: z_dw(t).wait())
    s2[...] = (r2[0] + r2[1]) + (r2[2] + r2[3])
    b3[chip] = (b2[0] + b2[1]) + (b2[2] + b2[3])

    def p_dw(t):
        q = chip_peer(t)
        return send(s2.at[pl.ds(q * CROWS, CROWS)], r3.at[chip], 10 + t, q * 2 + core, rep)

    def p_db(t):
        return send(b3.at[chip], b3.at[chip], 26 + t, chip_peer(t) * 2 + core, rep)

    loop(1, CHIPS, lambda t: p_dw(t).start())
    loop(1, CHIPS, lambda t: p_db(t).start())
    r3[chip] = s2[pl.ds(pl.multiple_of(chip * CROWS, CROWS), CROWS)]
    shift.y.second()
    tiles.start(2, 4)

    running[0] = jnp.zeros((TILE, D), F32)

    def near(n):
        e = order_ref[n]
        part = dot_tn(adj[e // KL, e % KL], gm[e // KL]).astype(BF16)
        running[n + 1] = running[n] + part.astype(F32)

    loop(0, NEAR // 2, near)
    loop(1, CHIPS, lambda t: p_dw(t).wait())
    total = r3[0]
    for q in range(1, CHIPS):
        total = total + r3[q]
    mine = out_ref.at[core, pl.ds(pl.multiple_of(rep * ZROWS + chip * CROWS, CROWS), CROWS)]
    mine[...] = total

    def p_out(t):
        return send(mine, mine, 42 + t, chip_peer(t) * 2 + core, rep)

    loop(1, CHIPS, lambda t: p_out(t).start())
    shift.start_lane()
    tiles.start(4, 6)
    loop(NEAR // 2, NEAR, near)
    loop(1, CHIPS, lambda t: p_db(t).wait())
    bias = b3[0]
    for q in range(1, CHIPS):
        bias = bias + b3[q]
    bias_ref[...] = bias
    loop(1, CHIPS, lambda t: p_out(t).wait())
    block = out_ref.at[core, pl.ds(pl.multiple_of(rep * ZROWS, ZROWS), ZROWS)]

    def z_out(t):
        return send(block, block, 58 + t, me, z_peer(t))

    loop(1, NREP, lambda t: z_out(t).start())

    def pass_on(src, n):
        rows = pl.ds(TILE, HALF)
        return remote(
            ret_ref.at[src, rows], passed_ref.at[src], pass_sems.at[0, n], pass_sems.at[1, n],
            partner, rep,
        )

    keep.wait()
    pass_on(me, NPEER).start()
    for n, (dx, dy, dc) in enumerate(PEERS):
        halves.every(n).wait()
        pass_on(here.at(SIDE - dx, SIDE - dy, dc), n).start()
    tiles.start(6, TILE // CHUNK)

    def settle(h):
        acc[h] += running[order_ref[NEAR + h + 1]] - running[order_ref[NEAR + h]]

    loop(0, CL, settle)
    store = pltpu.make_async_copy(acc, acc_ref, local_sems.at[8])
    store.start()
    shift.finish(moved_ref)
    loop(1, NREP, lambda t: z_out(t).wait())
    last = send(out_ref.at[core], out_ref.at[core], 62, partner, rep)
    last.start()
    pass_on(me, NPEER).wait()
    for n, (dx, dy, dc) in enumerate(PEERS):
        pass_on(here.at(SIDE - dx, SIDE - dy, dc), n).wait()
    for n in range(NPEER):
        tiles.every(n).wait()
    last.wait()
    store.wait()


def exchange_backward(room, plan, order, back, tail, gp, gm, mean, home, moved, adjacency, w_self):
    tiles = pltpu.VMEM((CL, TILE, D), BF16)
    return pl.pallas_call(
        functools.partial(backward_kernel, room),
        out_shape=[
            jax.ShapeDtypeStruct((NDOM, WIDE, D), BF16),
            jax.ShapeDtypeStruct((NDOM, HALF, D), BF16),
            jax.ShapeDtypeStruct((MIG, TILE, D), BF16),
            jax.ShapeDtypeStruct((CL, TILE, D), F32),
            jax.ShapeDtypeStruct((2, D, D), F32),
            jax.ShapeDtypeStruct((8, D), F32),
        ],
        in_specs=[SMEM, SMEM, ANY, VMEM] + [ANY] * 7,
        out_specs=[ANY, ANY, VMEM, ANY, VMEM, VMEM],
        scratch_shapes=[
            pltpu.VMEM((D, D), F32),
            pltpu.VMEM((8, D), F32),
            pltpu.VMEM((D, D), F32),
            pltpu.VMEM((NREP, ZROWS, D), F32),
            pltpu.VMEM((NREP, 8, D), F32),
            pltpu.VMEM((ZROWS, D), F32),
            pltpu.VMEM((CHIPS, CROWS, D), F32),
            pltpu.VMEM((CHIPS, 8, D), F32),
            pltpu.SemaphoreType.DMA((2, 64)),
            EXCHANGE_SEMS,
            EXCHANGE_SEMS,
            pltpu.SemaphoreType.DMA((2, NDOM)),
            pltpu.SemaphoreType.DMA((9,)),
            tiles,
            tiles,
            tiles,
            tiles,
            pltpu.VMEM((CL, KL + KH, TILE, TILE), BF16),
            pltpu.VMEM((D, D), BF16),
            pltpu.VMEM((2, D, D), F32),
            pltpu.VMEM((8, D), F32),
            pltpu.VMEM((CL, TILE, D), F32),
            pltpu.VMEM((NEAR + 1, TILE, D), F32),
        ]
        + shift_scratch(room),
        compiler_params=pltpu.CompilerParams(
            collective_id=room, has_side_effects=True, vmem_limit_bytes=VMEM_LIMIT
        ),
    )(plan, order, back, tail, gp, gm, mean, home, moved, adjacency, w_self)


def fourth_pass(back, want_ref, home_ref, buffer_ref, out_ref, stage, sems, local_sem):
    here = Place()
    me, core = here.me, here.core
    barrier = pltpu.get_barrier_semaphore()

    def peers(which):
        return [n for n in range(NPEER) if (which + PEERS[n][2]) % 2 == 1]

    every = list(range(NPEER))
    roles = []
    for which in range(2):
        served, near = every if which == 1 else [], peers(which)
        roles.append((near, served) if back else (served, near))

    for which, (_, receives) in enumerate(roles):

        @pl.when(core == which)
        def _():
            for n in receives:
                dom = here.at(SIDE - PEERS[n][0], SIDE - PEERS[n][1], PEERS[n][2])
                pl.semaphore_signal(
                    barrier, inc=1, device_id=(dom, here.rep), device_id_type=MESH
                )

    rows = pl.ds(WIDE, TILE)
    if back:
        keep = pltpu.make_async_copy(buffer_ref.at[me, rows], out_ref.at[me], local_sem.at[0])
    else:

        def gather(p):
            stage[p] = home_ref[jnp.maximum(want_ref[p], 0)]

        loop(0, NDOM, gather)
        keep = pltpu.make_async_copy(stage.at[me], out_ref.at[me, rows], local_sem.at[0])
    keep.start()

    def copy(n, low, count):
        dom = here.at(*PEERS[n])
        if back:
            src = buffer_ref.at[dom, pl.ds(WIDE + low, count)]
            dst = out_ref.at[me, pl.ds(low, count)]
        else:
            src = stage.at[dom, pl.ds(low, count)]
            dst = out_ref.at[me, pl.ds(WIDE + low, count)]
        return remote(src, dst, sems.at[0, n], sems.at[1, n], dom, here.rep)

    def run(sends, receives):
        def chunk(c):
            for n in sends:
                copy(n, pl.multiple_of(c * CHUNK, CHUNK), CHUNK).start()

        if sends:
            pl.semaphore_wait(barrier, len(sends))
            loop(0, TILE // CHUNK, chunk)
        for n in sends:
            copy(n, 0, TILE).wait_send()
        for n in receives:
            copy(n, 0, TILE).wait_recv()

    for which, (sends, receives) in enumerate(roles):

        @pl.when(core == which)
        def _():
            run(sends, receives)

    keep.wait()


def fourth_forward(want, home, recv):
    return pl.pallas_call(
        functools.partial(fourth_pass, False),
        out_shape=jax.ShapeDtypeStruct((NDOM, FULL, D), BF16),
        in_specs=[SMEM, VMEM, ANY],
        out_specs=ANY,
        input_output_aliases={2: 0},
        scratch_shapes=[
            pltpu.VMEM((NDOM, TILE, D), BF16),
            pltpu.SemaphoreType.DMA((2, NPEER)),
            pltpu.SemaphoreType.DMA((1,)),
        ],
        compiler_params=pltpu.CompilerParams(
            collective_id=4, has_side_effects=True, vmem_limit_bytes=VMEM_LIMIT
        ),
    )(want, home, recv)


def fourth_backward(back):
    def kernel(back_ref, out_ref, sems, local_sem):
        fourth_pass(True, None, None, back_ref, out_ref, None, sems, local_sem)

    return pl.pallas_call(
        kernel,
        out_shape=jax.ShapeDtypeStruct((NDOM, TILE, D), BF16),
        in_specs=[ANY],
        out_specs=ANY,
        scratch_shapes=[pltpu.SemaphoreType.DMA((2, NPEER)), pltpu.SemaphoreType.DMA((1,))],
        compiler_params=pltpu.CompilerParams(
            collective_id=5, has_side_effects=True, vmem_limit_bytes=VMEM_LIMIT
        ),
    )(back)


def tile_block(width=D):
    return pl.BlockSpec((GROUP, TILE, width), lambda g, *_: (g, 0, 0))


def whole(*shape):
    return pl.BlockSpec(shape, lambda g, *_: (0,) * len(shape))


def adj_block(k):
    return pl.BlockSpec((GROUP, 1, TILE, TILE), lambda g, *_: (g, k, 0, 0))


def own_tile(i, g, home_tile, moved_ref):
    j = CL - GROUP + i - OWN
    if j < 0:
        return home_tile
    return jnp.where(g == STEPS - 1, moved_ref[j], home_tile)


PARTS = 2 * GROUP * KH


def middle_kernel(block_ref, src_ref, *refs):
    halo = refs[:PARTS]
    (home_ref, moved_ref, adj_ref, cot_ref, ws_ref, wn_ref, bias_ref) = refs[PARTS : PARTS + 7]
    (new_ref, gp_ref, mean_ref, gm_ref, tail_ref, back_ref) = refs[PARTS + 7 : PARTS + 13]
    (own, scale, grads, sem) = refs[PARTS + 13 :]
    g = pl.program_id(0)
    for i in range(GROUP):
        slot = g * GROUP + i
        rows = pl.ds(i * TILE, TILE)
        mine = own_tile(i, g, home_ref[slot], moved_ref)
        own[rows] = mine
        adj = jnp.concatenate([adj_ref[i, k] for k in range(KL + KH)], axis=1)
        total = jnp.sum(adj.astype(F32), axis=1, keepdims=True)
        scale[rows] = jnp.broadcast_to(1.0 / (1.0 + total), (TILE, D))
        near = [home_ref[src_ref[slot * KL + k]] for k in range(KL)]
        far = [halo[2 * KH * i + n][0] for n in range(2 * KH)]
        agg = mine.astype(F32) + dot_nn(adj, jnp.concatenate(near + far, axis=0))
        mean_ref[i] = (agg * scale[rows]).astype(BF16)
    pre = (
        dot_nn(own[...], ws_ref[...])
        + dot_nn(mean_ref[...].reshape(ROWS, D), wn_ref[...])
        + bias_ref[...]
    )
    sig = 1.0 / (1.0 + jnp.exp(-pre))
    new_ref[...] = (pre * sig).astype(BF16).reshape(GROUP, TILE, D)
    cot = cot_ref[...].reshape(ROWS, D).astype(F32)
    gp = (cot * sig * (1.0 + pre * (1.0 - sig))).astype(BF16)
    gp_ref[...] = gp.reshape(GROUP, TILE, D)
    gm = (dot_nt(gp, wn_ref[...]) * scale[...]).astype(BF16)
    gm_ref[...] = gm.reshape(GROUP, TILE, D)

    def copy(n):
        return pltpu.make_async_copy(grads.at[n], back_ref.at[block_ref[n]], sem.at[n])

    for i in range(GROUP):
        adj = jnp.concatenate([adj_ref[i, KL + k] for k in range(KH)], axis=1)
        both = dot_tn(adj, gm[i * TILE : (i + 1) * TILE]).astype(BF16)
        for part in range(2 * KH):
            n = (g * GROUP + i) * 2 * KH + part
            grads[n] = both[part * HALF : (part + 1) * HALF]
            copy(n).start()

    @pl.when(g == STEPS - 1)
    def _():
        first = TILE * (GROUP - MIG)
        tail = dot_nt(gp[first:], ws_ref[...]) + gm[first:].astype(F32)
        tail_ref[...] = tail.astype(BF16).reshape(MIG, TILE, D)
        loop(0, 2 * CL * KH, lambda n: copy(n).wait())


def middle(blocks, src, recv, home, moved, adjacency, cot, w_self, w_neigh, bias):
    def halo_block(n):
        return pl.BlockSpec((1, HALF, D), lambda g, blocks, src: (blocks[g * PARTS + n], 0, 0))

    tiles = jax.ShapeDtypeStruct((CL, TILE, D), BF16)
    return pl.pallas_call(
        middle_kernel,
        out_shape=[
            tiles, tiles, tiles, tiles,
            jax.ShapeDtypeStruct((MIG, TILE, D), BF16),
            jax.ShapeDtypeStruct(recv.shape, BF16),
        ],
        grid_spec=pltpu.PrefetchScalarGridSpec(
            num_scalar_prefetch=2,
            grid=(STEPS,),
            in_specs=[halo_block(n) for n in range(PARTS)]
            + [
                whole(CL, TILE, D),
                whole(MIG, TILE, D),
                pl.BlockSpec((GROUP, KL + KH, TILE, TILE), lambda g, *_: (g, 0, 0, 0)),
                tile_block(),
                whole(D, D),
                whole(D, D),
                whole(1, D),
            ],
            out_specs=[tile_block()] * 4 + [whole(MIG, TILE, D), ANY],
            scratch_shapes=[
                pltpu.VMEM((ROWS, D), BF16),
                pltpu.VMEM((ROWS, D), F32),
                pltpu.VMEM((2 * CL * KH, HALF, D), BF16),
                pltpu.SemaphoreType.DMA((2 * CL * KH,)),
            ],
        ),
        compiler_params=pltpu.CompilerParams(vmem_limit_bytes=VMEM_LIMIT),
    )(
        blocks, src, *([recv] * PARTS), home, moved, adjacency, cot, w_self, w_neigh, bias
    )


FOUR = 4


def final_kernel(first_ref, other_ref, more_ref, acc_ref, moved_ref, back_ref, passed_ref, *refs):
    extra_ref = refs[0] if len(refs) == 8 else None
    dw_ref, db_ref, out_ref, dws_ref, dwn_ref, bias_ref, acc = refs[-7:]
    g = pl.program_id(0)
    here_half = lax.rem(lax.axis_index("dom"), 2)
    dws_ref[...] = dw_ref[0] * FACTOR
    dwn_ref[...] = dw_ref[1] * FACTOR

    @pl.when(g == 0)
    def _():
        bias_ref[...] = jnp.sum(db_ref[...], axis=0, keepdims=True) * FACTOR
        acc[...] = acc_ref[...]
        for j in range(MIG):
            acc[OWN + j] += moved_ref[j].astype(F32)

    for n in range(FOUR):
        c = g * FOUR + n
        first, other = first_ref[c], other_ref[c]

        @pl.when(first >= 0)
        def _():
            acc[first] += back_ref[n, pl.ds(0, TILE)].astype(F32)

        @pl.when(other >= 0)
        def _():
            rows = pl.ds(pl.multiple_of(here_half * HALF, HALF), HALF)
            acc[other, rows] += back_ref[n, pl.ds(TILE, HALF)].astype(F32)
            rows = pl.ds(pl.multiple_of((1 - here_half) * HALF, HALF), HALF)
            acc[other, rows] += passed_ref[n].astype(F32)

        if extra_ref is not None:
            more = more_ref[c]

            @pl.when(more >= 0)
            def _():
                acc[more] += extra_ref[n].astype(F32)

    @pl.when(g == NDOM // FOUR - 1)
    def _():
        out_ref[...] = acc[...].astype(BF16)


def finish(first, other, more, acc, moved, back, passed, extra, dw, db):
    steps = NDOM // FOUR

    def four(rows):
        return pl.BlockSpec((FOUR, rows, D), lambda g, *_: (g, 0, 0))

    extras = [] if extra is None else [extra]
    return pl.pallas_call(
        final_kernel,
        out_shape=[
            jax.ShapeDtypeStruct((CL, TILE, D), BF16),
            jax.ShapeDtypeStruct((D, D), F32),
            jax.ShapeDtypeStruct((D, D), F32),
            jax.ShapeDtypeStruct((1, D), F32),
        ],
        grid_spec=pltpu.PrefetchScalarGridSpec(
            num_scalar_prefetch=3,
            grid=(steps,),
            in_specs=[whole(CL, TILE, D), whole(MIG, TILE, D), four(WIDE), four(HALF)]
            + [four(TILE)] * len(extras)
            + [pl.BlockSpec((2, D // steps, D), lambda g, *_: (0, g, 0)), whole(8, D)],
            out_specs=[whole(CL, TILE, D)]
            + [pl.BlockSpec((D // steps, D), lambda g, *_: (g, 0))] * 2
            + [whole(1, D)],
            scratch_shapes=[pltpu.VMEM((CL, TILE, D), F32)],
        ),
        compiler_params=pltpu.CompilerParams(vmem_limit_bytes=VMEM_LIMIT),
    )(first, other, more, acc, moved, back, passed, *extras, dw, db)


def requests(owner, local):
    entries = jnp.arange(owner.shape[0], dtype=jnp.int32)
    same = owner[:, None] == owner[None, :]
    second = jnp.any(same & (entries[None, :] < entries[:, None]), axis=1)
    partner = (owner[:, None] ^ 1) == owner[None, :]
    fourth = second & (owner % 2 == 1) & jnp.any(partner & second[None, :], axis=1)
    chip = owner // 2

    column = jnp.where(second, jnp.where(fourth, NDOM + CHIPS + chip, NDOM + chip), owner)
    value = jnp.where(second & ~fourth, (owner % 2) * CL + local, local)
    hit = column[:, None] == jnp.arange(128, dtype=jnp.int32)[None, :]
    row = jnp.sum(jnp.where(hit, value[:, None] + 1, 0), axis=0) - 1
    low = jnp.where(
        fourth, UNITS * owner + 3, jnp.where(second, 2 * UNITS * chip + 2, UNITS * owner)
    )
    high = jnp.where(second & ~fourth, low + UNITS, low + 1)
    return row, jnp.stack([low, high], axis=1).reshape(-1)


def sorted_near(src):
    entries = jnp.arange(NEAR, dtype=jnp.int32)
    ahead = (src[None, :] < src[:, None]) | (
        (src[None, :] == src[:, None]) & (entries[None, :] < entries[:, None])
    )
    rank = jnp.sum(ahead.astype(jnp.int32), axis=1)
    order = jnp.sum(jnp.where(rank[None, :] == entries[:, None], entries[None, :], 0), axis=1)
    begins = jnp.sum(
        (src[None, :] < jnp.arange(CL + 1, dtype=jnp.int32)[:, None]).astype(jnp.int32), axis=1
    )
    return jnp.concatenate([order, begins])


def body(
    features, w_self, w_neigh, out_bias, cluster_plan, local_source, halo_owner, halo_local,
    adjacency, cotangent,
):
    me = lax.axis_index("dom")
    core, chip = me % 2, me // 2
    home = features[0].reshape(CL, TILE, D)
    cot = cotangent[0].reshape(CL, TILE, D)
    src = local_source.reshape(-1)
    bias = out_bias.reshape(1, D)
    row, blocks = requests(halo_owner.reshape(-1), halo_local.reshape(-1))
    offset = (cluster_plan[OWN:] // CL - me + NDOM) % NDOM
    few = few_ways(offset)
    recv, tables, moved = lax.cond(
        few,
        functools.partial(exchange_forward, 2),
        functools.partial(exchange_forward, 3),
        cluster_plan,
        row.reshape(1, 128),
        home,
    )
    asked = tables[:, 0, :]
    first = lax.dynamic_slice(asked, (0, me), (NDOM, 1)).reshape(-1)
    other = lax.dynamic_slice(asked, (0, NDOM + chip), (NDOM, 1)).reshape(-1)
    more = lax.dynamic_slice(asked, (0, NDOM + CHIPS + chip), (NDOM, 1)).reshape(-1)
    other = jnp.where((other >= 0) & (other // CL == core), other % CL, -1)
    more_here = jnp.where(core == 1, more, -1)
    order = sorted_near(src)

    def rest_of(extra, room, recv, moved):
        if extra:
            recv = fourth_forward(more, home, recv)
        new, gp, mean, gm, tail, back = middle(
            blocks, src, recv.reshape(NDOM * UNITS, HALF, D), home, moved, adjacency, cot,
            w_self, w_neigh, bias,
        )
        back = back.reshape(NDOM, FULL, D)
        ret, passed, returned, acc, dw, db = exchange_backward(
            room, cluster_plan, order, back, tail, gp, gm, mean, home, moved, adjacency, w_self
        )
        got = fourth_backward(back) if extra else None
        return new, *finish(first, other, more_here, acc, returned, ret, passed, got, dw, db)

    extra = jnp.any(asked[:, NDOM + CHIPS : NDOM + 2 * CHIPS] >= 0)
    new, grad, dws, dwn, db = lax.switch(
        2 * extra.astype(jnp.int32) + 1 - few.astype(jnp.int32),
        [functools.partial(rest_of, more, room) for more in (False, True) for room in (2, 3)],
        recv,
        moved,
    )
    return (
        new.reshape(1, CL * TILE, D), grad.reshape(1, CL * TILE, D), dws, dwn, db.reshape(D)
    )


def solution(mesh):
    return jax.shard_map(
        body,
        mesh=mesh,
        in_specs=(
            P("rep", "dom", None),
            P(),
            P(),
            P(),
            P("dom"),
            P("dom", None),
            P("dom", None),
            P("dom", None),
            P("dom", None, None, None),
            P("rep", "dom", None),
        ),
        out_specs=(P("rep", "dom", None), P("rep", "dom", None), P(), P(), P()),
        check_vma=False,
    )
```

```python
import functools
import math

import jax
import jax.numpy as jnp
from jax import lax
from jax.experimental import pallas as pl
from jax.experimental.pallas import tpu as pltpu
from jax.sharding import PartitionSpec as P

D = 512
TILE = 128
CL = 16
KL = 3
KH = 2
MIG = 3
OWN = CL - MIG
NDOM = 32
NREP = 4
HALF = TILE // 2
WIDE = TILE + HALF
FULL = WIDE + TILE
UNITS = FULL // HALF
CHUNK = 16
SIDE = 4
GROUP = 4
STEPS = CL // GROUP
ROWS = GROUP * TILE
VMEM_LIMIT = 60 * 2**20
FACTOR = 1.0 / math.sqrt(NDOM * NREP * CL * TILE)
MESH = pl.DeviceIdType.MESH
F32 = jnp.float32
BF16 = jnp.bfloat16

ANY = pl.BlockSpec(memory_space=pl.ANY)
VMEM = pl.BlockSpec(memory_space=pltpu.VMEM)
SMEM = pl.BlockSpec(memory_space=pltpu.SMEM)


def dot_tn(a, b):
    return lax.dot_general(a, b, (((0,), (0,)), ((), ())), preferred_element_type=F32)


def dot_nt(a, b):
    return lax.dot_general(a, b, (((1,), (1,)), ((), ())), preferred_element_type=F32)


def dot_nn(a, b):
    return jnp.dot(a, b, preferred_element_type=F32)


ZROWS = D // NREP
CHIPS = NDOM // 2
CROWS = ZROWS // CHIPS

ORDER = [
    (1, 0), (3, 0), (0, 1), (0, 3), (1, 1), (3, 3), (1, 3), (3, 1),
    (2, 0), (0, 2), (2, 2), (1, 2), (2, 1), (3, 2), (2, 3),
]
PEERS = [(0, 0, 1)] + [(dx, dy, dc) for dx, dy in ORDER for dc in (0, 1)]
NPEER = len(PEERS)


class Place:
    def __init__(self):
        self.me, self.rep = lax.axis_index("dom"), lax.axis_index("rep")
        self.core, self.chip = lax.rem(self.me, 2), self.me // 2
        self.x, self.y = lax.rem(self.chip, SIDE), self.chip // SIDE
        self.partner = self.chip * 2 + 1 - self.core

    def at(self, dx, dy, dc):
        x, y = lax.rem(self.x + dx, SIDE), lax.rem(self.y + dy, SIDE)
        return (y * SIDE + x) * 2 + lax.rem(self.core + dc, 2)


def loop(low, high, f):
    def step(t, carry):
        f(t)
        return carry

    lax.fori_loop(low, high, step, 0)


def greet_plane(here, barrier):
    def one(t):
        dom = lax.rem(here.me + t, NDOM)
        pl.semaphore_signal(barrier, inc=1, device_id=(dom, here.rep), device_id_type=MESH)

    loop(1, NDOM, one)


def remote(src, dst, send_sem, recv_sem, dom, z):
    return pltpu.make_async_remote_copy(
        src_ref=src,
        dst_ref=dst,
        send_sem=send_sem,
        recv_sem=recv_sem,
        device_id=(dom, z),
        device_id_type=MESH,
    )


class Exchange:
    def __init__(self, here, src, dst, send_sem, recv_sem, first, last):
        self.here, self.src, self.dst = here, src, dst
        self.send_sem, self.recv_sem = send_sem, recv_sem
        self.first, self.last = first, last

    def copy(self, n, rows):
        dom = self.here.at(*PEERS[n])
        return remote(
            self.src.at[dom, rows],
            self.dst.at[self.here.me, rows],
            self.send_sem.at[n],
            self.recv_sem.at[n],
            dom,
            self.here.rep,
        )

    def start(self, low, high):
        def chunk(c):
            rows = pl.ds(pl.multiple_of(self.first + c * CHUNK, CHUNK), CHUNK)
            for n in range(NPEER):
                self.copy(n, rows).start()

        loop(low, high, chunk)

    def every(self, n):
        return self.copy(n, pl.ds(self.first, self.last - self.first))


def scalar_sum(terms):
    total = jnp.int32(0)
    for term in terms:
        total = total + term
    return total


class Ring:
    def __init__(self, here, steps, axis, sign, room, buffers, sems):
        self.here, self.axis, self.room, self.sems = here, axis, room, sems
        self.steps = steps if sign > 0 else [lax.rem(SIDE - s, SIDE) for s in steps]
        self.to = (SIDE - 1, 1, 2) if sign > 0 else (1, SIDE - 1, 2)
        self.own, self.out, self.near = buffers

    def peer(self, t):
        return self.here.at(t, 0, 0) if self.axis == "x" else self.here.at(0, t, 0)

    def ways(self):
        first = 0
        for way, step in enumerate((1, SIDE - 1, 2)):
            chosen = [(s == step).astype(jnp.int32) for s in self.steps]
            rank = [scalar_sum(chosen[:j]) for j in range(MIG)]
            yield way, first, chosen, rank
            first += self.room[way]

    def copy(self, way, first):
        room = self.room[way]
        return remote(
            self.out.at[pl.ds(first, room)],
            self.near.at[pl.ds(MIG + first, room)],
            self.sems.at[0, way],
            self.sems.at[1, way],
            self.peer(self.to[way]),
            self.here.rep,
        )

    def start(self):
        for way, first, chosen, rank in self.ways():
            for k in range(self.room[way]):
                held = scalar_sum(
                    j * chosen[j] * (rank[j] == k).astype(jnp.int32) for j in range(MIG)
                )
                self.out[first + k] = self.own[held]
            self.copy(way, first).start()
        self.near[pl.ds(0, MIG)] = self.own[...]

    def finish(self):
        for way, first, _, _ in self.ways():
            self.copy(way, first).wait()

    def result(self, j):
        at = jnp.int32(j)
        for way, first, chosen, rank in self.ways():
            slot = MIG + first + jnp.minimum(rank[j], self.room[way] - 1)
            at = at + chosen[j] * (slot - j)
        return self.near[at]


class Shift:
    def __init__(self, here, plan_ref, sign, room, scratch):
        self.here = here
        ring_x, ring_y, self.lanes, self.sems = scratch[:3], scratch[3:6], scratch[6], scratch[7]
        along_x, along_y, self.swaps = [], [], []
        for j in range(MIG):
            offset = lax.rem(plan_ref[OWN + j] // CL - here.me + NDOM, NDOM)
            if sign < 0:
                offset = lax.rem(NDOM - offset, NDOM)
            swap = lax.rem(offset, 2)
            to = lax.rem(here.core + swap, 2)
            shift = offset // 2 + to * swap
            carry = (here.x + lax.rem(shift, SIDE)) // SIDE
            along_x.append(lax.rem(shift, SIDE))
            along_y.append(lax.rem(shift // SIDE + carry, SIDE))
            self.swaps.append(swap)
        self.x = Ring(here, along_x, "x", sign, room, ring_x, self.sems.at[0])
        self.y = Ring(here, along_y, "y", sign, room, ring_y, self.sems.at[1])

    def copy_lane(self):
        slot = self.lanes.at[self.here.core]
        send_sem, recv_sem = self.sems.at[2, 0, 0], self.sems.at[2, 1, 0]
        return remote(slot, slot, send_sem, recv_sem, self.here.partner, self.here.rep)

    def turn(self):
        self.x.finish()
        for j in range(MIG):
            self.y.own[j] = self.x.result(j)
        self.y.start()

    def start_lane(self):
        self.y.finish()
        for j in range(MIG):
            self.lanes[self.here.core, j] = self.y.result(j)
        self.copy_lane().start()

    def finish(self, out_ref):
        self.copy_lane().wait()
        for j in range(MIG):
            out_ref[j] = self.lanes[lax.rem(self.here.core + self.swaps[j], 2), j]


ROOMS = [(1, 2, 2), (MIG, MIG, MIG)]


def shift_scratch(room):
    ring = [
        pltpu.VMEM((MIG, TILE, D), BF16),
        pltpu.VMEM((sum(room), TILE, D), BF16),
        pltpu.VMEM((MIG + sum(room), TILE, D), BF16),
    ]
    return ring + ring + [
        pltpu.VMEM((2, MIG, TILE, D), BF16),
        pltpu.SemaphoreType.DMA((3, 2, 3)),
    ]


def few_ways(offset):
    back = jnp.arange(2, dtype=jnp.int32)[:, None, None, None]
    core = jnp.arange(2, dtype=jnp.int32)[None, :, None, None]
    x = jnp.arange(SIDE, dtype=jnp.int32)[None, None, :, None]
    signed = jnp.where(back == 1, NDOM - offset, offset)
    swap = signed & 1
    shift = (signed >> 1) + ((core + swap) & 1) * swap
    along_x = shift & (SIDE - 1)
    along_y = ((shift >> 2) + ((x + along_x) >> 2)) & (SIDE - 1)
    fits = jnp.bool_(True)
    for steps in (jnp.broadcast_to(along_x, along_y.shape), along_y):
        steps = jnp.where(back == 1, (SIDE - steps) & (SIDE - 1), steps)
        for way, step in enumerate((1, SIDE - 1, 2)):
            count = jnp.sum((steps == step).astype(jnp.int32), axis=-1)
            fits = fits & jnp.all(count <= ROOMS[0][way])
    return fits


EXCHANGE_SEMS = pltpu.SemaphoreType.DMA((2, NPEER))


def forward_kernel(room, plan_ref, row_ref, home_ref, recv_ref, table_ref, moved_ref, *scratch):
    feat, stage, asked, table_sems, tile_sems, local_sems = scratch[:6]
    here = Place()
    me, core, rep = here.me, here.core, here.rep
    barrier = pltpu.get_barrier_semaphore()
    greet_plane(here, barrier)
    own = feat.at[pl.ds(core * CL, CL)]
    take = pltpu.make_async_copy(home_ref, own, local_sems.at[0])
    take.start()
    shift = Shift(here, plan_ref, 1, room, scratch[6:])
    mine = pltpu.make_async_copy(home_ref.at[pl.ds(OWN, MIG)], shift.x.own, local_sems.at[1])
    mine.start()
    table_ref[me] = row_ref[...]
    pl.semaphore_wait(barrier, NDOM - 1)

    def table(n):
        return remote(
            row_ref, table_ref.at[me], table_sems.at[0, n], table_sems.at[1, n],
            lax.rem(me + n, NDOM), rep,
        )

    loop(1, NDOM, lambda n: table(n).start())
    share = remote(home_ref, own, local_sems.at[2], local_sems.at[3], here.partner, rep)
    share.start()
    mine.wait()
    shift.x.start()
    loop(1, NDOM, lambda n: table(n).wait())
    read = pltpu.make_async_copy(table_ref, asked, local_sems.at[4])
    read.start()
    read.wait()
    take.wait()
    share.wait()

    def gather(p):
        first = asked[p, 0, me]
        other = asked[p, 0, NDOM + here.chip]
        stage[p, pl.ds(0, TILE)] = feat[core * CL + jnp.maximum(first, 0)]
        stage[p, pl.ds(TILE, HALF)] = feat[
            jnp.maximum(other, 0), pl.ds(pl.multiple_of(core * HALF, HALF), HALF)
        ]

    loop(0, NDOM, gather)
    keep = pltpu.make_async_copy(
        stage.at[me], recv_ref.at[me, pl.ds(0, WIDE)], local_sems.at[5]
    )
    keep.start()
    tiles = Exchange(here, stage, recv_ref, tile_sems.at[0], tile_sems.at[1], 0, WIDE)
    tiles.start(0, 3)
    shift.turn()
    tiles.start(3, 7)
    shift.start_lane()
    tiles.start(7, WIDE // CHUNK)
    keep.wait()
    for n in range(NPEER):
        tiles.every(n).wait()
    shift.finish(moved_ref)


def exchange_forward(room, plan, row, home):
    return pl.pallas_call(
        functools.partial(forward_kernel, room),
        out_shape=[
            jax.ShapeDtypeStruct((NDOM, FULL, D), BF16),
            jax.ShapeDtypeStruct((NDOM, 1, 128), jnp.int32),
            jax.ShapeDtypeStruct((MIG, TILE, D), BF16),
        ],
        in_specs=[SMEM, VMEM, ANY],
        out_specs=[ANY, VMEM, VMEM],
        scratch_shapes=[
            pltpu.VMEM((2 * CL, TILE, D), BF16),
            pltpu.VMEM((NDOM, WIDE, D), BF16),
            pltpu.SMEM((NDOM, 1, 128), jnp.int32),
            pltpu.SemaphoreType.DMA((2, NDOM)),
            EXCHANGE_SEMS,
            pltpu.SemaphoreType.DMA((6,)),
        ]
        + shift_scratch(room),
        compiler_params=pltpu.CompilerParams(
            collective_id=ROOMS.index(room), has_side_effects=True, vmem_limit_bytes=VMEM_LIMIT
        ),
    )(plan, row, home)


NEAR = CL * KL


def backward_kernel(
    room, plan_ref, order_ref, back_ref, tail_ref, gp_ref, gm_ref, mean_ref, home_ref, moved_in,
    adj_ref, w_ref, ret_ref, passed_ref, moved_ref, acc_ref, out_ref, bias_ref, *scratch
):
    r1, b1, s1, r2, b2, s2, r3, b3, sums, half_sems, tile_sems, pass_sems, local_sems = scratch[:13]
    gp, gm, mean, own, adj, w, dw, db, acc, running = scratch[13:23]
    here = Place()
    me, core, chip, rep, partner = here.me, here.core, here.chip, here.rep, here.partner
    barrier = pltpu.get_barrier_semaphore()

    def z_peer(t):
        return lax.rem(rep + t, NREP)

    def chip_peer(t):
        return lax.rem(chip + t, CHIPS)

    def greet_z(t):
        pl.semaphore_signal(barrier, inc=1, device_id=(me, z_peer(t)), device_id_type=MESH)

    greet_plane(here, barrier)
    loop(1, NREP, greet_z)
    keep = pltpu.make_async_copy(
        back_ref.at[me, pl.ds(0, WIDE)], ret_ref.at[me], local_sems.at[0]
    )
    keep.start()
    loads = [
        pltpu.make_async_copy(src, dst, local_sems.at[1 + n])
        for n, (src, dst) in enumerate(
            [
                (gp_ref, gp),
                (home_ref.at[pl.ds(0, OWN)], own.at[pl.ds(0, OWN)]),
                (moved_in, own.at[pl.ds(OWN, MIG)]),
                (mean_ref, mean),
                (gm_ref, gm),
                (w_ref, w),
                (adj_ref, adj),
            ]
        )
    ]
    for copy in loads:
        copy.start()
    shift = Shift(here, plan_ref, -1, room, scratch[23:])
    shift.x.own[...] = tail_ref[...]
    pl.semaphore_wait(barrier, NDOM - 1 + NREP - 1)

    def send(src, dst, n, dom, z):
        return remote(src, dst, sums.at[0, n], sums.at[1, n], dom, z)

    halves = Exchange(here, back_ref, ret_ref, half_sems.at[0], half_sems.at[1], TILE, WIDE)
    tiles = Exchange(here, back_ref, ret_ref, tile_sems.at[0], tile_sems.at[1], 0, TILE)
    shift.x.start()
    halves.start(0, 2)

    dw[...] = jnp.zeros_like(dw)
    db[...] = jnp.zeros_like(db)
    for copy in loads[:4]:
        copy.wait()

    def weights(g):
        rows = pl.ds(g * GROUP, GROUP)
        grad = gp[rows].reshape(ROWS, D)
        dw[0] += dot_tn(own[rows].reshape(ROWS, D), grad)
        dw[1] += dot_tn(mean[rows].reshape(ROWS, D), grad)
        db[...] += jnp.sum(grad.astype(F32), axis=0, keepdims=True)

    loop(0, STEPS, weights)

    c_dw = send(dw.at[1 - core], r1, 0, partner, rep)
    c_db = send(db, b1, 1, partner, rep)
    c_dw.start()
    c_db.start()
    halves.start(2, 4)
    c_db.wait()
    c_dw.wait()
    s1[...] = dw[core] + r1[...]
    b2[rep] = db[...] + b1[...]

    def z_dw(t):
        z = z_peer(t)
        return send(s1.at[pl.ds(z * ZROWS, ZROWS)], r2.at[rep], 2 + t, me, z)

    def z_db(t):
        return send(b2.at[rep], b2.at[rep], 6 + t, me, z_peer(t))

    loop(1, NREP, lambda t: z_dw(t).start())
    loop(1, NREP, lambda t: z_db(t).start())
    r2[rep] = s1[pl.ds(pl.multiple_of(rep * ZROWS, ZROWS), ZROWS)]
    tiles.start(0, 2)
    shift.turn()

    for copy in loads[4:]:
        copy.wait()

    def kept(g):
        rows = pl.ds(g * GROUP, GROUP)
        part = dot_nt(gp[rows].reshape(ROWS, D), w[...]) + gm[rows].reshape(ROWS, D).astype(F32)
        acc[rows] = part.astype(BF16).astype(F32).reshape(GROUP, TILE, D)

    loop(0, STEPS, kept)
    acc[pl.ds(OWN, MIG)] = jnp.zeros((MIG, TILE, D), F32)

    loop(1, NREP, lambda t: z_db(t).wait())
    loop(1, NREP, lambda t: z_dw(t).wait())
    s2[...] = (r2[0] + r2[1]) + (r2[2] + r2[3])
    b3[chip] = (b2[0] + b2[1]) + (b2[2] + b2[3])

    def p_dw(t):
        q = chip_peer(t)
        return send(s2.at[pl.ds(q * CROWS, CROWS)], r3.at[chip], 10 + t, q * 2 + core, rep)

    def p_db(t):
        return send(b3.at[chip], b3.at[chip], 26 + t, chip_peer(t) * 2 + core, rep)

    loop(1, CHIPS, lambda t: p_dw(t).start())
    loop(1, CHIPS, lambda t: p_db(t).start())
    r3[chip] = s2[pl.ds(pl.multiple_of(chip * CROWS, CROWS), CROWS)]
    tiles.start(2, 4)

    running[0] = jnp.zeros((TILE, D), F32)

    def near(n):
        e = order_ref[n]
        part = dot_tn(adj[e // KL, e % KL], gm[e // KL]).astype(BF16)
        running[n + 1] = running[n] + part.astype(F32)

    loop(0, NEAR // 2, near)
    loop(1, CHIPS, lambda t: p_dw(t).wait())
    total = r3[0]
    for q in range(1, CHIPS):
        total = total + r3[q]
    mine = out_ref.at[core, pl.ds(pl.multiple_of(rep * ZROWS + chip * CROWS, CROWS), CROWS)]
    mine[...] = total

    def p_out(t):
        return send(mine, mine, 42 + t, chip_peer(t) * 2 + core, rep)

    loop(1, CHIPS, lambda t: p_out(t).start())
    shift.start_lane()
    tiles.start(4, 6)
    loop(NEAR // 2, NEAR, near)
    loop(1, CHIPS, lambda t: p_db(t).wait())
    bias = b3[0]
    for q in range(1, CHIPS):
        bias = bias + b3[q]
    bias_ref[...] = bias
    loop(1, CHIPS, lambda t: p_out(t).wait())
    block = out_ref.at[core, pl.ds(pl.multiple_of(rep * ZROWS, ZROWS), ZROWS)]

    def z_out(t):
        return send(block, block, 58 + t, me, z_peer(t))

    loop(1, NREP, lambda t: z_out(t).start())

    def pass_on(src, n):
        rows = pl.ds(TILE, HALF)
        return remote(
            ret_ref.at[src, rows], passed_ref.at[src], pass_sems.at[0, n], pass_sems.at[1, n],
            partner, rep,
        )

    keep.wait()
    pass_on(me, NPEER).start()
    for n, (dx, dy, dc) in enumerate(PEERS):
        halves.every(n).wait()
        pass_on(here.at(SIDE - dx, SIDE - dy, dc), n).start()
    tiles.start(6, TILE // CHUNK)

    def settle(h):
        acc[h] += running[order_ref[NEAR + h + 1]] - running[order_ref[NEAR + h]]

    loop(0, CL, settle)
    store = pltpu.make_async_copy(acc, acc_ref, local_sems.at[8])
    store.start()
    shift.finish(moved_ref)
    loop(1, NREP, lambda t: z_out(t).wait())
    last = send(out_ref.at[core], out_ref.at[core], 62, partner, rep)
    last.start()
    pass_on(me, NPEER).wait()
    for n, (dx, dy, dc) in enumerate(PEERS):
        pass_on(here.at(SIDE - dx, SIDE - dy, dc), n).wait()
    for n in range(NPEER):
        tiles.every(n).wait()
    last.wait()
    store.wait()


def exchange_backward(room, plan, order, back, tail, gp, gm, mean, home, moved, adjacency, w_self):
    tiles = pltpu.VMEM((CL, TILE, D), BF16)
    return pl.pallas_call(
        functools.partial(backward_kernel, room),
        out_shape=[
            jax.ShapeDtypeStruct((NDOM, WIDE, D), BF16),
            jax.ShapeDtypeStruct((NDOM, HALF, D), BF16),
            jax.ShapeDtypeStruct((MIG, TILE, D), BF16),
            jax.ShapeDtypeStruct((CL, TILE, D), F32),
            jax.ShapeDtypeStruct((2, D, D), F32),
            jax.ShapeDtypeStruct((1, D), F32),
        ],
        in_specs=[SMEM, SMEM, ANY, VMEM] + [ANY] * 7,
        out_specs=[ANY, ANY, VMEM, ANY, VMEM, VMEM],
        scratch_shapes=[
            pltpu.VMEM((D, D), F32),
            pltpu.VMEM((1, D), F32),
            pltpu.VMEM((D, D), F32),
            pltpu.VMEM((NREP, ZROWS, D), F32),
            pltpu.VMEM((NREP, 1, D), F32),
            pltpu.VMEM((ZROWS, D), F32),
            pltpu.VMEM((CHIPS, CROWS, D), F32),
            pltpu.VMEM((CHIPS, 1, D), F32),
            pltpu.SemaphoreType.DMA((2, 64)),
            EXCHANGE_SEMS,
            EXCHANGE_SEMS,
            pltpu.SemaphoreType.DMA((2, NDOM)),
            pltpu.SemaphoreType.DMA((9,)),
            tiles,
            tiles,
            tiles,
            tiles,
            pltpu.VMEM((CL, KL + KH, TILE, TILE), BF16),
            pltpu.VMEM((D, D), BF16),
            pltpu.VMEM((2, D, D), F32),
            pltpu.VMEM((1, D), F32),
            pltpu.VMEM((CL, TILE, D), F32),
            pltpu.VMEM((NEAR + 1, TILE, D), F32),
        ]
        + shift_scratch(room),
        compiler_params=pltpu.CompilerParams(
            collective_id=2 + ROOMS.index(room), has_side_effects=True, vmem_limit_bytes=VMEM_LIMIT
        ),
    )(plan, order, back, tail, gp, gm, mean, home, moved, adjacency, w_self)


def fourth_pass(back, want_ref, home_ref, buffer_ref, out_ref, stage, sems, local_sem):
    here = Place()
    me, core = here.me, here.core
    barrier = pltpu.get_barrier_semaphore()

    def peers(which):
        return [n for n in range(NPEER) if (which + PEERS[n][2]) % 2 == 1]

    every = list(range(NPEER))
    roles = []
    for which in range(2):
        served, near = every if which == 1 else [], peers(which)
        roles.append((near, served) if back else (served, near))

    for which, (_, receives) in enumerate(roles):

        @pl.when(core == which)
        def _():
            for n in receives:
                dom = here.at(SIDE - PEERS[n][0], SIDE - PEERS[n][1], PEERS[n][2])
                pl.semaphore_signal(
                    barrier, inc=1, device_id=(dom, here.rep), device_id_type=MESH
                )

    rows = pl.ds(WIDE, TILE)
    if back:
        keep = pltpu.make_async_copy(buffer_ref.at[me, rows], out_ref.at[me], local_sem.at[0])
    else:

        def gather(p):
            stage[p] = home_ref[jnp.maximum(want_ref[p], 0)]

        loop(0, NDOM, gather)
        keep = pltpu.make_async_copy(stage.at[me], out_ref.at[me, rows], local_sem.at[0])
    keep.start()

    def copy(n, low, count):
        dom = here.at(*PEERS[n])
        if back:
            src = buffer_ref.at[dom, pl.ds(WIDE + low, count)]
            dst = out_ref.at[me, pl.ds(low, count)]
        else:
            src = stage.at[dom, pl.ds(low, count)]
            dst = out_ref.at[me, pl.ds(WIDE + low, count)]
        return remote(src, dst, sems.at[0, n], sems.at[1, n], dom, here.rep)

    def run(sends, receives):
        def chunk(c):
            for n in sends:
                copy(n, pl.multiple_of(c * CHUNK, CHUNK), CHUNK).start()

        if sends:
            pl.semaphore_wait(barrier, len(sends))
            loop(0, TILE // CHUNK, chunk)
        for n in sends:
            copy(n, 0, TILE).wait_send()
        for n in receives:
            copy(n, 0, TILE).wait_recv()

    for which, (sends, receives) in enumerate(roles):

        @pl.when(core == which)
        def _():
            run(sends, receives)

    keep.wait()


def fourth_forward(want, home, recv):
    return pl.pallas_call(
        functools.partial(fourth_pass, False),
        out_shape=jax.ShapeDtypeStruct((NDOM, FULL, D), BF16),
        in_specs=[SMEM, VMEM, ANY],
        out_specs=ANY,
        input_output_aliases={2: 0},
        scratch_shapes=[
            pltpu.VMEM((NDOM, TILE, D), BF16),
            pltpu.SemaphoreType.DMA((2, NPEER)),
            pltpu.SemaphoreType.DMA((1,)),
        ],
        compiler_params=pltpu.CompilerParams(
            collective_id=4, has_side_effects=True, vmem_limit_bytes=VMEM_LIMIT
        ),
    )(want, home, recv)


def fourth_backward(back):
    def kernel(back_ref, out_ref, sems, local_sem):
        fourth_pass(True, None, None, back_ref, out_ref, None, sems, local_sem)

    return pl.pallas_call(
        kernel,
        out_shape=jax.ShapeDtypeStruct((NDOM, TILE, D), BF16),
        in_specs=[ANY],
        out_specs=ANY,
        scratch_shapes=[pltpu.SemaphoreType.DMA((2, NPEER)), pltpu.SemaphoreType.DMA((1,))],
        compiler_params=pltpu.CompilerParams(
            collective_id=5, has_side_effects=True, vmem_limit_bytes=VMEM_LIMIT
        ),
    )(back)


def tile_block(width=D):
    return pl.BlockSpec((GROUP, TILE, width), lambda g, *_: (g, 0, 0))


def whole(*shape):
    return pl.BlockSpec(shape, lambda g, *_: (0,) * len(shape))


def adj_block(k):
    return pl.BlockSpec((GROUP, 1, TILE, TILE), lambda g, *_: (g, k, 0, 0))


def own_tile(i, g, home_tile, moved_ref):
    j = CL - GROUP + i - OWN
    if j < 0:
        return home_tile
    return jnp.where(g == STEPS - 1, moved_ref[j], home_tile)


PARTS = 2 * GROUP * KH


def middle_kernel(block_ref, src_ref, *refs):
    halo = refs[:PARTS]
    (home_ref, moved_ref, adj_ref, cot_ref, ws_ref, wn_ref, bias_ref) = refs[PARTS : PARTS + 7]
    (new_ref, gp_ref, mean_ref, gm_ref, tail_ref, back_ref) = refs[PARTS + 7 : PARTS + 13]
    (own, scale, grads, sem) = refs[PARTS + 13 :]
    g = pl.program_id(0)
    for i in range(GROUP):
        slot = g * GROUP + i
        rows = pl.ds(i * TILE, TILE)
        mine = own_tile(i, g, home_ref[slot], moved_ref)
        own[rows] = mine
        adj = jnp.concatenate([adj_ref[i, k] for k in range(KL + KH)], axis=1)
        total = jnp.sum(adj.astype(F32), axis=1, keepdims=True)
        scale[rows] = jnp.broadcast_to(1.0 / (1.0 + total), (TILE, D))
        near = [home_ref[src_ref[slot * KL + k]] for k in range(KL)]
        far = [halo[2 * KH * i + n][0] for n in range(2 * KH)]
        agg = mine.astype(F32) + dot_nn(adj, jnp.concatenate(near + far, axis=0))
        mean_ref[i] = (agg * scale[rows]).astype(BF16)
    pre = (
        dot_nn(own[...], ws_ref[...])
        + dot_nn(mean_ref[...].reshape(ROWS, D), wn_ref[...])
        + bias_ref[...]
    )
    sig = 1.0 / (1.0 + jnp.exp(-pre))
    new_ref[...] = (pre * sig).astype(BF16).reshape(GROUP, TILE, D)
    cot = cot_ref[...].reshape(ROWS, D).astype(F32)
    gp = (cot * sig * (1.0 + pre * (1.0 - sig))).astype(BF16)
    gp_ref[...] = gp.reshape(GROUP, TILE, D)
    gm = (dot_nt(gp, wn_ref[...]) * scale[...]).astype(BF16)
    gm_ref[...] = gm.reshape(GROUP, TILE, D)

    def copy(n):
        return pltpu.make_async_copy(grads.at[n], back_ref.at[block_ref[n]], sem.at[n])

    for i in range(GROUP):
        adj = jnp.concatenate([adj_ref[i, KL + k] for k in range(KH)], axis=1)
        both = dot_tn(adj, gm[i * TILE : (i + 1) * TILE]).astype(BF16)
        for part in range(2 * KH):
            n = (g * GROUP + i) * 2 * KH + part
            grads[n] = both[part * HALF : (part + 1) * HALF]
            copy(n).start()

    @pl.when(g == STEPS - 1)
    def _():
        first = TILE * (GROUP - MIG)
        tail = dot_nt(gp[first:], ws_ref[...]) + gm[first:].astype(F32)
        tail_ref[...] = tail.astype(BF16).reshape(MIG, TILE, D)
        loop(0, 2 * CL * KH, lambda n: copy(n).wait())


def middle(blocks, src, recv, home, moved, adjacency, cot, w_self, w_neigh, bias):
    def halo_block(n):
        return pl.BlockSpec((1, HALF, D), lambda g, blocks, src: (blocks[g * PARTS + n], 0, 0))

    tiles = jax.ShapeDtypeStruct((CL, TILE, D), BF16)
    return pl.pallas_call(
        middle_kernel,
        out_shape=[
            tiles, tiles, tiles, tiles,
            jax.ShapeDtypeStruct((MIG, TILE, D), BF16),
            jax.ShapeDtypeStruct(recv.shape, BF16),
        ],
        grid_spec=pltpu.PrefetchScalarGridSpec(
            num_scalar_prefetch=2,
            grid=(STEPS,),
            in_specs=[halo_block(n) for n in range(PARTS)]
            + [
                whole(CL, TILE, D),
                whole(MIG, TILE, D),
                pl.BlockSpec((GROUP, KL + KH, TILE, TILE), lambda g, *_: (g, 0, 0, 0)),
                tile_block(),
                whole(D, D),
                whole(D, D),
                whole(1, D),
            ],
            out_specs=[tile_block()] * 4 + [whole(MIG, TILE, D), ANY],
            scratch_shapes=[
                pltpu.VMEM((ROWS, D), BF16),
                pltpu.VMEM((ROWS, D), F32),
                pltpu.VMEM((2 * CL * KH, HALF, D), BF16),
                pltpu.SemaphoreType.DMA((2 * CL * KH,)),
            ],
        ),
        compiler_params=pltpu.CompilerParams(vmem_limit_bytes=VMEM_LIMIT),
    )(
        blocks, src, *([recv] * PARTS), home, moved, adjacency, cot, w_self, w_neigh, bias
    )


FOUR = 4


def final_kernel(table_ref, acc_ref, moved_ref, back_ref, passed_ref, *refs):
    extra_ref = refs[0] if len(refs) == 8 else None
    dw_ref, db_ref, out_ref, dws_ref, dwn_ref, bias_ref, acc = refs[-7:]
    g = pl.program_id(0)
    me = lax.axis_index("dom")
    core, chip = lax.rem(me, 2), me // 2
    dws_ref[...] = dw_ref[0] * FACTOR
    dwn_ref[...] = dw_ref[1] * FACTOR

    @pl.when(g == 0)
    def _():
        bias_ref[...] = db_ref[...] * FACTOR
        acc[...] = acc_ref[...]
        for j in range(MIG):
            acc[OWN + j] += moved_ref[j].astype(F32)

    for n in range(FOUR):
        c = g * FOUR + n
        first, asked = table_ref[c, me], table_ref[c, NDOM + chip]
        other = lax.rem(asked, CL)

        @pl.when(first >= 0)
        def _():
            acc[first] += back_ref[n, pl.ds(0, TILE)].astype(F32)

        @pl.when(jnp.logical_and(asked >= 0, asked // CL == core))
        def _():
            rows = pl.ds(pl.multiple_of(core * HALF, HALF), HALF)
            acc[other, rows] += back_ref[n, pl.ds(TILE, HALF)].astype(F32)
            rows = pl.ds(pl.multiple_of((1 - core) * HALF, HALF), HALF)
            acc[other, rows] += passed_ref[n].astype(F32)

        if extra_ref is not None:
            more = table_ref[c, NDOM + CHIPS + chip]

            @pl.when(jnp.logical_and(more >= 0, core == 1))
            def _():
                acc[more] += extra_ref[n].astype(F32)

    @pl.when(g == NDOM // FOUR - 1)
    def _():
        out_ref[...] = acc[...].astype(BF16)


def finish(tables, acc, moved, back, passed, extra, dw, db):
    steps = NDOM // FOUR

    def four(rows):
        return pl.BlockSpec((FOUR, rows, D), lambda g, *_: (g, 0, 0))

    extras = [] if extra is None else [extra]
    return pl.pallas_call(
        final_kernel,
        out_shape=[
            jax.ShapeDtypeStruct((CL, TILE, D), BF16),
            jax.ShapeDtypeStruct((D, D), F32),
            jax.ShapeDtypeStruct((D, D), F32),
            jax.ShapeDtypeStruct((1, D), F32),
        ],
        grid_spec=pltpu.PrefetchScalarGridSpec(
            num_scalar_prefetch=1,
            grid=(steps,),
            in_specs=[whole(CL, TILE, D), whole(MIG, TILE, D), four(WIDE), four(HALF)]
            + [four(TILE)] * len(extras)
            + [pl.BlockSpec((2, D // steps, D), lambda g, *_: (0, g, 0)), whole(1, D)],
            out_specs=[whole(CL, TILE, D)]
            + [pl.BlockSpec((D // steps, D), lambda g, *_: (g, 0))] * 2
            + [whole(1, D)],
            scratch_shapes=[pltpu.VMEM((CL, TILE, D), F32)],
        ),
        compiler_params=pltpu.CompilerParams(vmem_limit_bytes=VMEM_LIMIT),
    )(tables, acc, moved, back, passed, *extras, dw, db)


def requests(owner, local):
    entries = jnp.arange(owner.shape[0], dtype=jnp.int32)
    same = owner[:, None] == owner[None, :]
    second = jnp.any(same & (entries[None, :] < entries[:, None]), axis=1)
    partner = (owner[:, None] ^ 1) == owner[None, :]
    fourth = second & (owner % 2 == 1) & jnp.any(partner & second[None, :], axis=1)
    chip = owner // 2

    column = jnp.where(second, jnp.where(fourth, NDOM + CHIPS + chip, NDOM + chip), owner)
    value = jnp.where(second & ~fourth, (owner % 2) * CL + local, local)
    hit = column[:, None] == jnp.arange(128, dtype=jnp.int32)[None, :]
    row = jnp.sum(jnp.where(hit, value[:, None] + 1, 0), axis=0) - 1
    low = jnp.where(
        fourth, UNITS * owner + 3, jnp.where(second, 2 * UNITS * chip + 2, UNITS * owner)
    )
    high = jnp.where(second & ~fourth, low + UNITS, low + 1)
    return row, jnp.stack([low, high], axis=1).reshape(-1)


def sorted_near(src):
    entries = jnp.arange(NEAR, dtype=jnp.int32)
    ahead = (src[None, :] < src[:, None]) | (
        (src[None, :] == src[:, None]) & (entries[None, :] < entries[:, None])
    )
    rank = jnp.sum(ahead.astype(jnp.int32), axis=1)
    order = jnp.sum(jnp.where(rank[None, :] == entries[:, None], entries[None, :], 0), axis=1)
    begins = jnp.sum(
        (src[None, :] < jnp.arange(CL + 1, dtype=jnp.int32)[:, None]).astype(jnp.int32), axis=1
    )
    return jnp.concatenate([order, begins])


def body(
    features, w_self, w_neigh, out_bias, cluster_plan, local_source, halo_owner, halo_local,
    adjacency, cotangent,
):
    me = lax.axis_index("dom")
    chip = me // 2
    home = features[0].reshape(CL, TILE, D)
    cot = cotangent[0].reshape(CL, TILE, D)
    src = local_source.reshape(-1)
    bias = out_bias.reshape(1, D)
    row, blocks = requests(halo_owner.reshape(-1), halo_local.reshape(-1))
    offset = (cluster_plan[OWN:] // CL - me + NDOM) % NDOM
    few = few_ways(offset)
    recv, tables, moved = lax.cond(
        few,
        functools.partial(exchange_forward, ROOMS[0]),
        functools.partial(exchange_forward, ROOMS[1]),
        cluster_plan,
        row.reshape(1, 128),
        home,
    )
    asked = tables[:, 0, :]
    order = sorted_near(src)

    def rest_of(extra, room, recv, moved):
        if extra:
            more = lax.dynamic_slice(asked, (0, NDOM + CHIPS + chip), (NDOM, 1)).reshape(-1)
            recv = fourth_forward(more, home, recv)
        new, gp, mean, gm, tail, back = middle(
            blocks, src, recv.reshape(NDOM * UNITS, HALF, D), home, moved, adjacency, cot,
            w_self, w_neigh, bias,
        )
        back = back.reshape(NDOM, FULL, D)
        ret, passed, returned, acc, dw, db = exchange_backward(
            room, cluster_plan, order, back, tail, gp, gm, mean, home, moved, adjacency, w_self
        )
        got = fourth_backward(back) if extra else None
        return new, *finish(asked, acc, returned, ret, passed, got, dw, db)

    extra = jnp.any(asked[:, NDOM + CHIPS : NDOM + 2 * CHIPS] >= 0)
    new, grad, dws, dwn, db = lax.switch(
        2 * extra.astype(jnp.int32) + 1 - few.astype(jnp.int32),
        [functools.partial(rest_of, more, room) for more in (False, True) for room in ROOMS],
        recv,
        moved,
    )
    return (
        new.reshape(1, CL * TILE, D), grad.reshape(1, CL * TILE, D), dws, dwn, db.reshape(D)
    )


def solution(mesh):
    return jax.shard_map(
        body,
        mesh=mesh,
        in_specs=(
            P("rep", "dom", None),
            P(),
            P(),
            P(),
            P("dom"),
            P("dom", None),
            P("dom", None),
            P("dom", None),
            P("dom", None, None, None),
            P("rep", "dom", None),
        ),
        out_specs=(P("rep", "dom", None), P("rep", "dom", None), P(), P(), P()),
        check_vma=False,
    )
```

```python
import functools
import math

import jax
import jax.numpy as jnp
from jax import lax
from jax.experimental import pallas as pl
from jax.experimental.pallas import tpu as pltpu
from jax.sharding import PartitionSpec as P

D = 512
TILE = 128
CL = 16
KL = 3
KH = 2
MIG = 3
OWN = CL - MIG
NDOM = 32
NREP = 4
HALF = TILE // 2
WIDE = TILE + HALF
FULL = WIDE + TILE
UNITS = FULL // HALF
CHUNK = 16
SIDE = 4
GROUP = 4
STEPS = CL // GROUP
ROWS = GROUP * TILE
VMEM_LIMIT = 60 * 2**20
FACTOR = 1.0 / math.sqrt(NDOM * NREP * CL * TILE)
MESH = pl.DeviceIdType.MESH
F32 = jnp.float32
BF16 = jnp.bfloat16

ANY = pl.BlockSpec(memory_space=pl.ANY)
VMEM = pl.BlockSpec(memory_space=pltpu.VMEM)
SMEM = pl.BlockSpec(memory_space=pltpu.SMEM)


def dot_tn(a, b):
    return lax.dot_general(a, b, (((0,), (0,)), ((), ())), preferred_element_type=F32)


def dot_nt(a, b):
    return lax.dot_general(a, b, (((1,), (1,)), ((), ())), preferred_element_type=F32)


def dot_nn(a, b):
    return jnp.dot(a, b, preferred_element_type=F32)


ZROWS = D // NREP
CHIPS = NDOM // 2
CROWS = ZROWS // CHIPS

ORDER = [
    (1, 0), (3, 0), (0, 1), (0, 3), (1, 1), (3, 3), (1, 3), (3, 1),
    (2, 0), (0, 2), (2, 2), (1, 2), (2, 1), (3, 2), (2, 3),
]
PEERS = [(0, 0, 1)] + [(dx, dy, dc) for dx, dy in ORDER for dc in (0, 1)]
NPEER = len(PEERS)


class Place:
    def __init__(self):
        self.me, self.rep = lax.axis_index("dom"), lax.axis_index("rep")
        self.core, self.chip = lax.rem(self.me, 2), self.me // 2
        self.x, self.y = lax.rem(self.chip, SIDE), self.chip // SIDE
        self.partner = self.chip * 2 + 1 - self.core

    def at(self, dx, dy, dc):
        x, y = lax.rem(self.x + dx, SIDE), lax.rem(self.y + dy, SIDE)
        return (y * SIDE + x) * 2 + lax.rem(self.core + dc, 2)


def loop(low, high, f):
    def step(t, carry):
        f(t)
        return carry

    lax.fori_loop(low, high, step, 0)


def greet_plane(here, barrier):
    def one(t):
        dom = lax.rem(here.me + t, NDOM)
        pl.semaphore_signal(barrier, inc=1, device_id=(dom, here.rep), device_id_type=MESH)

    loop(1, NDOM, one)


def remote(src, dst, send_sem, recv_sem, dom, z):
    return pltpu.make_async_remote_copy(
        src_ref=src,
        dst_ref=dst,
        send_sem=send_sem,
        recv_sem=recv_sem,
        device_id=(dom, z),
        device_id_type=MESH,
    )


class Exchange:
    def __init__(self, here, src, dst, send_sem, recv_sem, first, last):
        self.here, self.src, self.dst = here, src, dst
        self.send_sem, self.recv_sem = send_sem, recv_sem
        self.first, self.last = first, last

    def copy(self, n, rows):
        dom = self.here.at(*PEERS[n])
        return remote(
            self.src.at[dom, rows],
            self.dst.at[self.here.me, rows],
            self.send_sem.at[n],
            self.recv_sem.at[n],
            dom,
            self.here.rep,
        )

    def start(self, low, high):
        def chunk(c):
            rows = pl.ds(pl.multiple_of(self.first + c * CHUNK, CHUNK), CHUNK)
            for n in range(NPEER):
                self.copy(n, rows).start()

        loop(low, high, chunk)

    def every(self, n):
        return self.copy(n, pl.ds(self.first, self.last - self.first))


def scalar_sum(terms):
    total = jnp.int32(0)
    for term in terms:
        total = total + term
    return total


class Ring:
    def __init__(self, here, steps, axis, sign, room, buffers, sems):
        self.here, self.axis, self.room, self.sems = here, axis, room, sems
        self.steps = steps if sign > 0 else [lax.rem(SIDE - s, SIDE) for s in steps]
        self.to = (SIDE - 1, 1, 2) if sign > 0 else (1, SIDE - 1, 2)
        self.own, self.out, self.near = buffers

    def peer(self, t):
        return self.here.at(t, 0, 0) if self.axis == "x" else self.here.at(0, t, 0)

    def ways(self):
        first = 0
        for way, step in enumerate((1, SIDE - 1, 2)):
            chosen = [(s == step).astype(jnp.int32) for s in self.steps]
            rank = [scalar_sum(chosen[:j]) for j in range(MIG)]
            yield way, first, chosen, rank
            first += self.room[way]

    def copy(self, way, first):
        room = self.room[way]
        return remote(
            self.out.at[pl.ds(first, room)],
            self.near.at[pl.ds(MIG + first, room)],
            self.sems.at[0, way],
            self.sems.at[1, way],
            self.peer(self.to[way]),
            self.here.rep,
        )

    def start(self):
        for way, first, chosen, rank in self.ways():
            for k in range(self.room[way]):
                held = scalar_sum(
                    j * chosen[j] * (rank[j] == k).astype(jnp.int32) for j in range(MIG)
                )
                self.out[first + k] = self.own[held]
            self.copy(way, first).start()
        self.near[pl.ds(0, MIG)] = self.own[...]

    def finish(self):
        for way, first, _, _ in self.ways():
            self.copy(way, first).wait()

    def result(self, j):
        at = jnp.int32(j)
        for way, first, chosen, rank in self.ways():
            slot = MIG + first + jnp.minimum(rank[j], self.room[way] - 1)
            at = at + chosen[j] * (slot - j)
        return self.near[at]


class Shift:
    def __init__(self, here, plan_ref, sign, room, scratch):
        self.here = here
        ring_x, ring_y, self.lanes, self.sems = scratch[:3], scratch[3:6], scratch[6], scratch[7]
        along_x, along_y, self.swaps = [], [], []
        for j in range(MIG):
            offset = lax.rem(plan_ref[OWN + j] // CL - here.me + NDOM, NDOM)
            if sign < 0:
                offset = lax.rem(NDOM - offset, NDOM)
            swap = lax.rem(offset, 2)
            to = lax.rem(here.core + swap, 2)
            shift = offset // 2 + to * swap
            carry = (here.x + lax.rem(shift, SIDE)) // SIDE
            along_x.append(lax.rem(shift, SIDE))
            along_y.append(lax.rem(shift // SIDE + carry, SIDE))
            self.swaps.append(swap)
        self.x = Ring(here, along_x, "x", sign, room, ring_x, self.sems.at[0])
        self.y = Ring(here, along_y, "y", sign, room, ring_y, self.sems.at[1])

    def copy_lane(self):
        slot = self.lanes.at[self.here.core]
        send_sem, recv_sem = self.sems.at[2, 0, 0], self.sems.at[2, 1, 0]
        return remote(slot, slot, send_sem, recv_sem, self.here.partner, self.here.rep)

    def turn(self):
        self.x.finish()
        for j in range(MIG):
            self.y.own[j] = self.x.result(j)
        self.y.start()

    def start_lane(self):
        self.y.finish()
        for j in range(MIG):
            self.lanes[self.here.core, j] = self.y.result(j)
        self.copy_lane().start()

    def finish(self, out_ref):
        self.copy_lane().wait()
        for j in range(MIG):
            out_ref[j] = self.lanes[lax.rem(self.here.core + self.swaps[j], 2), j]


ROOMS = [(1, 2, 2), (MIG, MIG, MIG)]


def shift_scratch(room):
    ring = [
        pltpu.VMEM((MIG, TILE, D), BF16),
        pltpu.VMEM((sum(room), TILE, D), BF16),
        pltpu.VMEM((MIG + sum(room), TILE, D), BF16),
    ]
    return ring + ring + [
        pltpu.VMEM((2, MIG, TILE, D), BF16),
        pltpu.SemaphoreType.DMA((3, 2, 3)),
    ]


def few_ways(offset):
    back = jnp.arange(2, dtype=jnp.int32)[:, None, None, None]
    core = jnp.arange(2, dtype=jnp.int32)[None, :, None, None]
    x = jnp.arange(SIDE, dtype=jnp.int32)[None, None, :, None]
    signed = jnp.where(back == 1, NDOM - offset, offset)
    swap = signed & 1
    shift = (signed >> 1) + ((core + swap) & 1) * swap
    along_x = shift & (SIDE - 1)
    along_y = ((shift >> 2) + ((x + along_x) >> 2)) & (SIDE - 1)
    axes = jnp.stack([jnp.broadcast_to(along_x, along_y.shape), along_y])
    axes = jnp.where(back == 1, (SIDE - axes) & (SIDE - 1), axes)
    crowded = jnp.zeros(axes.shape[:-1], jnp.bool_)
    for way, step in enumerate((1, SIDE - 1, 2)):
        count = sum((axes[..., j] == step).astype(jnp.int32) for j in range(MIG))
        crowded = crowded | (count > ROOMS[0][way])
    return ~jnp.any(crowded)


EXCHANGE_SEMS = pltpu.SemaphoreType.DMA((2, NPEER))


def forward_kernel(room, plan_ref, row_ref, home_ref, recv_ref, table_ref, moved_ref, *scratch):
    feat, stage, asked, table_sems, tile_sems, local_sems = scratch[:6]
    here = Place()
    me, core, rep = here.me, here.core, here.rep
    barrier = pltpu.get_barrier_semaphore()
    greet_plane(here, barrier)
    own = feat.at[pl.ds(core * CL, CL)]
    take = pltpu.make_async_copy(home_ref, own, local_sems.at[0])
    take.start()
    shift = Shift(here, plan_ref, 1, room, scratch[6:])
    mine = pltpu.make_async_copy(home_ref.at[pl.ds(OWN, MIG)], shift.x.own, local_sems.at[1])
    mine.start()
    table_ref[me] = row_ref[...]
    pl.semaphore_wait(barrier, NDOM - 1)

    def table(n):
        return remote(
            row_ref, table_ref.at[me], table_sems.at[0, n], table_sems.at[1, n],
            lax.rem(me + n, NDOM), rep,
        )

    loop(1, NDOM, lambda n: table(n).start())
    share = remote(home_ref, own, local_sems.at[2], local_sems.at[3], here.partner, rep)
    share.start()
    mine.wait()
    shift.x.start()
    loop(1, NDOM, lambda n: table(n).wait())
    read = pltpu.make_async_copy(table_ref, asked, local_sems.at[4])
    read.start()
    read.wait()
    take.wait()
    share.wait()

    def gather(p):
        first = asked[p, 0, me]
        other = asked[p, 0, NDOM + here.chip]
        stage[p, pl.ds(0, TILE)] = feat[core * CL + jnp.maximum(first, 0)]
        stage[p, pl.ds(TILE, HALF)] = feat[
            jnp.maximum(other, 0), pl.ds(pl.multiple_of(core * HALF, HALF), HALF)
        ]

    loop(0, NDOM, gather)
    keep = pltpu.make_async_copy(
        stage.at[me], recv_ref.at[me, pl.ds(0, WIDE)], local_sems.at[5]
    )
    keep.start()
    tiles = Exchange(here, stage, recv_ref, tile_sems.at[0], tile_sems.at[1], 0, WIDE)
    tiles.start(0, 4)
    shift.turn()
    tiles.start(4, 8)
    shift.start_lane()
    tiles.start(8, WIDE // CHUNK)
    keep.wait()
    for n in range(NPEER):
        tiles.every(n).wait()
    shift.finish(moved_ref)


def exchange_forward(room, plan, row, home):
    return pl.pallas_call(
        functools.partial(forward_kernel, room),
        out_shape=[
            jax.ShapeDtypeStruct((NDOM, FULL, D), BF16),
            jax.ShapeDtypeStruct((NDOM, 1, 128), jnp.int32),
            jax.ShapeDtypeStruct((MIG, TILE, D), BF16),
        ],
        in_specs=[SMEM, VMEM, ANY],
        out_specs=[ANY, VMEM, VMEM],
        scratch_shapes=[
            pltpu.VMEM((2 * CL, TILE, D), BF16),
            pltpu.VMEM((NDOM, WIDE, D), BF16),
            pltpu.SMEM((NDOM, 1, 128), jnp.int32),
            pltpu.SemaphoreType.DMA((2, NDOM)),
            EXCHANGE_SEMS,
            pltpu.SemaphoreType.DMA((6,)),
        ]
        + shift_scratch(room),
        compiler_params=pltpu.CompilerParams(
            collective_id=ROOMS.index(room), has_side_effects=True, vmem_limit_bytes=VMEM_LIMIT
        ),
    )(plan, row, home)


NEAR = CL * KL


def backward_kernel(
    room, plan_ref, order_ref, back_ref, tail_ref, gp_ref, gm_ref, mean_ref, home_ref, moved_in,
    adj_ref, w_ref, ret_ref, passed_ref, moved_ref, acc_ref, out_ref, bias_ref, *scratch
):
    r1, b1, s1, r2, b2, s2, r3, b3, sums, half_sems, tile_sems, pass_sems, local_sems = scratch[:13]
    gp, gm, mean, own, adj, w, dw, db, acc, running = scratch[13:23]
    here = Place()
    me, core, chip, rep, partner = here.me, here.core, here.chip, here.rep, here.partner
    barrier = pltpu.get_barrier_semaphore()

    def z_peer(t):
        return lax.rem(rep + t, NREP)

    def chip_peer(t):
        return lax.rem(chip + t, CHIPS)

    def greet_z(t):
        pl.semaphore_signal(barrier, inc=1, device_id=(me, z_peer(t)), device_id_type=MESH)

    greet_plane(here, barrier)
    loop(1, NREP, greet_z)
    keep = pltpu.make_async_copy(
        back_ref.at[me, pl.ds(0, WIDE)], ret_ref.at[me], local_sems.at[0]
    )
    keep.start()
    loads = [
        pltpu.make_async_copy(src, dst, local_sems.at[1 + n])
        for n, (src, dst) in enumerate(
            [
                (gp_ref, gp),
                (home_ref.at[pl.ds(0, OWN)], own.at[pl.ds(0, OWN)]),
                (moved_in, own.at[pl.ds(OWN, MIG)]),
                (mean_ref, mean),
                (gm_ref, gm),
                (w_ref, w),
                (adj_ref, adj),
            ]
        )
    ]
    for copy in loads:
        copy.start()
    shift = Shift(here, plan_ref, -1, room, scratch[23:])
    shift.x.own[...] = tail_ref[...]
    pl.semaphore_wait(barrier, NDOM - 1 + NREP - 1)

    def send(src, dst, n, dom, z):
        return remote(src, dst, sums.at[0, n], sums.at[1, n], dom, z)

    halves = Exchange(here, back_ref, ret_ref, half_sems.at[0], half_sems.at[1], TILE, WIDE)
    tiles = Exchange(here, back_ref, ret_ref, tile_sems.at[0], tile_sems.at[1], 0, TILE)
    shift.x.start()
    halves.start(0, 2)

    dw[...] = jnp.zeros_like(dw)
    db[...] = jnp.zeros_like(db)
    for copy in loads[:4]:
        copy.wait()

    def weights(g):
        rows = pl.ds(g * GROUP, GROUP)
        grad = gp[rows].reshape(ROWS, D)
        dw[0] += dot_tn(own[rows].reshape(ROWS, D), grad)
        dw[1] += dot_tn(mean[rows].reshape(ROWS, D), grad)
        db[...] += jnp.sum(grad.astype(F32), axis=0, keepdims=True)

    loop(0, STEPS, weights)

    c_dw = send(dw.at[1 - core], r1, 0, partner, rep)
    c_db = send(db, b1, 1, partner, rep)
    c_dw.start()
    c_db.start()
    halves.start(2, 4)
    c_db.wait()
    c_dw.wait()
    s1[...] = dw[core] + r1[...]
    b2[rep] = db[...] + b1[...]

    def z_dw(t):
        z = z_peer(t)
        return send(s1.at[pl.ds(z * ZROWS, ZROWS)], r2.at[rep], 2 + t, me, z)

    def z_db(t):
        return send(b2.at[rep], b2.at[rep], 6 + t, me, z_peer(t))

    loop(1, NREP, lambda t: z_dw(t).start())
    loop(1, NREP, lambda t: z_db(t).start())
    r2[rep] = s1[pl.ds(pl.multiple_of(rep * ZROWS, ZROWS), ZROWS)]
    tiles.start(0, 2)
    shift.turn()

    for copy in loads[4:]:
        copy.wait()

    def kept(g):
        rows = pl.ds(g * GROUP, GROUP)
        part = dot_nt(gp[rows].reshape(ROWS, D), w[...]) + gm[rows].reshape(ROWS, D).astype(F32)
        acc[rows] = part.astype(BF16).astype(F32).reshape(GROUP, TILE, D)

    loop(0, STEPS, kept)
    acc[pl.ds(OWN, MIG)] = jnp.zeros((MIG, TILE, D), F32)

    loop(1, NREP, lambda t: z_db(t).wait())
    loop(1, NREP, lambda t: z_dw(t).wait())
    s2[...] = (r2[0] + r2[1]) + (r2[2] + r2[3])
    b3[chip] = (b2[0] + b2[1]) + (b2[2] + b2[3])

    def p_dw(t):
        q = chip_peer(t)
        return send(s2.at[pl.ds(q * CROWS, CROWS)], r3.at[chip], 10 + t, q * 2 + core, rep)

    def p_db(t):
        return send(b3.at[chip], b3.at[chip], 26 + t, chip_peer(t) * 2 + core, rep)

    loop(1, CHIPS, lambda t: p_dw(t).start())
    loop(1, CHIPS, lambda t: p_db(t).start())
    r3[chip] = s2[pl.ds(pl.multiple_of(chip * CROWS, CROWS), CROWS)]
    tiles.start(2, 4)

    running[0] = jnp.zeros((TILE, D), F32)

    def near(n):
        e = order_ref[n]
        part = dot_tn(adj[e // KL, e % KL], gm[e // KL]).astype(BF16)
        running[n + 1] = running[n] + part.astype(F32)

    loop(0, NEAR // 2, near)
    loop(1, CHIPS, lambda t: p_dw(t).wait())
    total = r3[0]
    for q in range(1, CHIPS):
        total = total + r3[q]
    mine = out_ref.at[core, pl.ds(pl.multiple_of(rep * ZROWS + chip * CROWS, CROWS), CROWS)]
    mine[...] = total

    def p_out(t):
        return send(mine, mine, 42 + t, chip_peer(t) * 2 + core, rep)

    loop(1, CHIPS, lambda t: p_out(t).start())
    shift.start_lane()
    tiles.start(4, 6)
    loop(NEAR // 2, NEAR, near)
    loop(1, CHIPS, lambda t: p_db(t).wait())
    bias = b3[0]
    for q in range(1, CHIPS):
        bias = bias + b3[q]
    bias_ref[...] = bias
    loop(1, CHIPS, lambda t: p_out(t).wait())
    block = out_ref.at[core, pl.ds(pl.multiple_of(rep * ZROWS, ZROWS), ZROWS)]

    def z_out(t):
        return send(block, block, 58 + t, me, z_peer(t))

    loop(1, NREP, lambda t: z_out(t).start())

    def pass_on(src, n):
        rows = pl.ds(TILE, HALF)
        return remote(
            ret_ref.at[src, rows], passed_ref.at[src], pass_sems.at[0, n], pass_sems.at[1, n],
            partner, rep,
        )

    keep.wait()
    pass_on(me, NPEER).start()
    for n, (dx, dy, dc) in enumerate(PEERS):
        halves.every(n).wait()
        pass_on(here.at(SIDE - dx, SIDE - dy, dc), n).start()
    tiles.start(6, TILE // CHUNK)

    def settle(h):
        acc[h] += running[order_ref[NEAR + h + 1]] - running[order_ref[NEAR + h]]

    loop(0, CL, settle)
    store = pltpu.make_async_copy(acc, acc_ref, local_sems.at[8])
    store.start()
    shift.finish(moved_ref)
    loop(1, NREP, lambda t: z_out(t).wait())
    last = send(out_ref.at[core], out_ref.at[core], 62, partner, rep)
    last.start()
    pass_on(me, NPEER).wait()
    for n, (dx, dy, dc) in enumerate(PEERS):
        pass_on(here.at(SIDE - dx, SIDE - dy, dc), n).wait()
    for n in range(NPEER):
        tiles.every(n).wait()
    last.wait()
    store.wait()


def exchange_backward(room, plan, order, back, tail, gp, gm, mean, home, moved, adjacency, w_self):
    tiles = pltpu.VMEM((CL, TILE, D), BF16)
    return pl.pallas_call(
        functools.partial(backward_kernel, room),
        out_shape=[
            jax.ShapeDtypeStruct((NDOM, WIDE, D), BF16),
            jax.ShapeDtypeStruct((NDOM, HALF, D), BF16),
            jax.ShapeDtypeStruct((MIG, TILE, D), BF16),
            jax.ShapeDtypeStruct((CL, TILE, D), F32),
            jax.ShapeDtypeStruct((2, D, D), F32),
            jax.ShapeDtypeStruct((1, D), F32),
        ],
        in_specs=[SMEM, SMEM, ANY, VMEM] + [ANY] * 7,
        out_specs=[ANY, ANY, VMEM, ANY, VMEM, VMEM],
        scratch_shapes=[
            pltpu.VMEM((D, D), F32),
            pltpu.VMEM((1, D), F32),
            pltpu.VMEM((D, D), F32),
            pltpu.VMEM((NREP, ZROWS, D), F32),
            pltpu.VMEM((NREP, 1, D), F32),
            pltpu.VMEM((ZROWS, D), F32),
            pltpu.VMEM((CHIPS, CROWS, D), F32),
            pltpu.VMEM((CHIPS, 1, D), F32),
            pltpu.SemaphoreType.DMA((2, 64)),
            EXCHANGE_SEMS,
            EXCHANGE_SEMS,
            pltpu.SemaphoreType.DMA((2, NDOM)),
            pltpu.SemaphoreType.DMA((9,)),
            tiles,
            tiles,
            tiles,
            tiles,
            pltpu.VMEM((CL, KL + KH, TILE, TILE), BF16),
            pltpu.VMEM((D, D), BF16),
            pltpu.VMEM((2, D, D), F32),
            pltpu.VMEM((1, D), F32),
            pltpu.VMEM((CL, TILE, D), F32),
            pltpu.VMEM((NEAR + 1, TILE, D), F32),
        ]
        + shift_scratch(room),
        compiler_params=pltpu.CompilerParams(
            collective_id=2 + ROOMS.index(room), has_side_effects=True, vmem_limit_bytes=VMEM_LIMIT
        ),
    )(plan, order, back, tail, gp, gm, mean, home, moved, adjacency, w_self)


def fourth_pass(back, want_ref, home_ref, buffer_ref, out_ref, stage, sems, local_sem):
    here = Place()
    me, core = here.me, here.core
    barrier = pltpu.get_barrier_semaphore()

    def peers(which):
        return [n for n in range(NPEER) if (which + PEERS[n][2]) % 2 == 1]

    every = list(range(NPEER))
    roles = []
    for which in range(2):
        served, near = every if which == 1 else [], peers(which)
        roles.append((near, served) if back else (served, near))

    for which, (_, receives) in enumerate(roles):

        @pl.when(core == which)
        def _():
            for n in receives:
                dom = here.at(SIDE - PEERS[n][0], SIDE - PEERS[n][1], PEERS[n][2])
                pl.semaphore_signal(
                    barrier, inc=1, device_id=(dom, here.rep), device_id_type=MESH
                )

    rows = pl.ds(WIDE, TILE)
    if back:
        keep = pltpu.make_async_copy(buffer_ref.at[me, rows], out_ref.at[me], local_sem.at[0])
    else:

        def gather(p):
            stage[p] = home_ref[jnp.maximum(want_ref[p], 0)]

        loop(0, NDOM, gather)
        keep = pltpu.make_async_copy(stage.at[me], out_ref.at[me, rows], local_sem.at[0])
    keep.start()

    def copy(n, low, count):
        dom = here.at(*PEERS[n])
        if back:
            src = buffer_ref.at[dom, pl.ds(WIDE + low, count)]
            dst = out_ref.at[me, pl.ds(low, count)]
        else:
            src = stage.at[dom, pl.ds(low, count)]
            dst = out_ref.at[me, pl.ds(WIDE + low, count)]
        return remote(src, dst, sems.at[0, n], sems.at[1, n], dom, here.rep)

    def run(sends, receives):
        def chunk(c):
            for n in sends:
                copy(n, pl.multiple_of(c * CHUNK, CHUNK), CHUNK).start()

        if sends:
            pl.semaphore_wait(barrier, len(sends))
            loop(0, TILE // CHUNK, chunk)
        for n in sends:
            copy(n, 0, TILE).wait_send()
        for n in receives:
            copy(n, 0, TILE).wait_recv()

    for which, (sends, receives) in enumerate(roles):

        @pl.when(core == which)
        def _():
            run(sends, receives)

    keep.wait()


def fourth_forward(want, home, recv):
    return pl.pallas_call(
        functools.partial(fourth_pass, False),
        out_shape=jax.ShapeDtypeStruct((NDOM, FULL, D), BF16),
        in_specs=[SMEM, VMEM, ANY],
        out_specs=ANY,
        input_output_aliases={2: 0},
        scratch_shapes=[
            pltpu.VMEM((NDOM, TILE, D), BF16),
            pltpu.SemaphoreType.DMA((2, NPEER)),
            pltpu.SemaphoreType.DMA((1,)),
        ],
        compiler_params=pltpu.CompilerParams(
            collective_id=4, has_side_effects=True, vmem_limit_bytes=VMEM_LIMIT
        ),
    )(want, home, recv)


def fourth_backward(back):
    def kernel(back_ref, out_ref, sems, local_sem):
        fourth_pass(True, None, None, back_ref, out_ref, None, sems, local_sem)

    return pl.pallas_call(
        kernel,
        out_shape=jax.ShapeDtypeStruct((NDOM, TILE, D), BF16),
        in_specs=[ANY],
        out_specs=ANY,
        scratch_shapes=[pltpu.SemaphoreType.DMA((2, NPEER)), pltpu.SemaphoreType.DMA((1,))],
        compiler_params=pltpu.CompilerParams(
            collective_id=5, has_side_effects=True, vmem_limit_bytes=VMEM_LIMIT
        ),
    )(back)


def middle_kernel(
    block_ref, src_ref, recv_ref, home_ref, moved_ref, adj_ref, cot_ref, ws_ref, wn_ref, bias_ref,
    new_ref, gp_ref, mean_ref, gm_ref, tail_ref, back_ref,
    halo, home, adj, cot, ws, wn, own, scale, new, gp, mean, gm, grads, halo_sem, in_sem, out_sem, back_sem,
):
    parts = 2 * KH * GROUP

    def copy_halo(n):
        return pltpu.make_async_copy(recv_ref.at[block_ref[n]], halo.at[n], halo_sem.at[n])

    def copy_back(n):
        return pltpu.make_async_copy(grads.at[n], back_ref.at[block_ref[n]], back_sem.at[n])

    def group(g):
        return pl.ds(g * GROUP, GROUP)

    def copy_in(g, ref, held, n):
        return pltpu.make_async_copy(ref.at[group(g)], held.at[group(g)], in_sem.at[n, g])

    def copy_out(g, n):
        held, ref = ((new, new_ref), (gp, gp_ref), (mean, mean_ref), (gm, gm_ref))[n]
        return pltpu.make_async_copy(held.at[group(g)], ref.at[group(g)], out_sem.at[n, g])

    once = [
        pltpu.make_async_copy(ref, held, in_sem.at[2, n])
        for n, (ref, held) in enumerate([(home_ref, home), (ws_ref, ws), (wn_ref, wn)])
    ]
    once[0].start()

    def start(g):
        copy_in(g, adj_ref, adj, 0).start()
        loop(0, parts, lambda n: copy_halo(g * parts + n).start())
        copy_in(g, cot_ref, cot, 1).start()

    start(0)
    once[1].start()
    once[2].start()
    loop(1, STEPS, start)
    once[0].wait()

    def step(g):
        copy_in(g, adj_ref, adj, 0).wait()
        loop(0, parts, lambda n: copy_halo(g * parts + n).wait())
        for i in range(GROUP):
            slot = g * GROUP + i
            rows = pl.ds(i * TILE, TILE)
            mine = home[slot]
            if STEPS * GROUP - GROUP + i >= OWN:
                mine = jnp.where(g == STEPS - 1, moved_ref[CL - GROUP + i - OWN], mine)
            own[rows] = mine
            tiles = jnp.concatenate([adj[slot, k] for k in range(KL + KH)], axis=1)
            total = jnp.sum(tiles.astype(F32), axis=1, keepdims=True)
            scale[rows] = jnp.broadcast_to(1.0 / (1.0 + total), (TILE, D))
            near = [home[src_ref[slot * KL + k]] for k in range(KL)]
            far = halo[pl.ds(slot * 2 * KH, 2 * KH)].reshape(KH * TILE, D)
            agg = mine.astype(F32) + dot_nn(tiles, jnp.concatenate(near + [far], axis=0))
            mean[slot] = (agg * scale[rows]).astype(BF16)
        copy_out(g, 2).start()

        @pl.when(g == 0)
        def _():
            once[1].wait()
            once[2].wait()

        pre = (
            dot_nn(own[...], ws[...])
            + dot_nn(mean[group(g)].reshape(ROWS, D), wn[...])
            + bias_ref[...]
        )
        sig = 1.0 / (1.0 + jnp.exp(-pre))
        new[group(g)] = (pre * sig).astype(BF16).reshape(GROUP, TILE, D)
        copy_out(g, 0).start()
        copy_in(g, cot_ref, cot, 1).wait()
        grad_out = cot[group(g)].reshape(ROWS, D).astype(F32)
        grad = (grad_out * sig * (1.0 + pre * (1.0 - sig))).astype(BF16)
        gp[group(g)] = grad.reshape(GROUP, TILE, D)
        copy_out(g, 1).start()
        grad_mean = (dot_nt(grad, wn[...]) * scale[...]).astype(BF16)
        gm[group(g)] = grad_mean.reshape(GROUP, TILE, D)
        copy_out(g, 3).start()
        for i in range(GROUP):
            slot = g * GROUP + i
            tiles = jnp.concatenate([adj[slot, KL + k] for k in range(KH)], axis=1)
            both = dot_tn(tiles, grad_mean[i * TILE : (i + 1) * TILE]).astype(BF16)
            grads[pl.ds(slot * 2 * KH, 2 * KH)] = both.reshape(2 * KH, HALF, D)
            for part in range(2 * KH):
                copy_back(slot * 2 * KH + part).start()

    loop(0, STEPS, step)
    first = pl.ds(OWN, MIG)
    tail = dot_nt(gp[first].reshape(MIG * TILE, D), ws[...])
    tail = tail + gm[first].reshape(MIG * TILE, D).astype(F32)
    tail_ref[...] = tail.astype(BF16).reshape(MIG, TILE, D)

    def finish(g):
        for n in range(4):
            copy_out(g, n).wait()
        loop(0, parts, lambda n: copy_back(g * parts + n).wait())

    loop(0, STEPS, finish)


def middle(blocks, src, recv, home, moved, adjacency, cot, w_self, w_neigh, bias):
    tiles = jax.ShapeDtypeStruct((CL, TILE, D), BF16)
    held = pltpu.VMEM((CL, TILE, D), BF16)
    pieces = pltpu.VMEM((2 * CL * KH, HALF, D), BF16)
    return pl.pallas_call(
        middle_kernel,
        out_shape=[
            tiles, tiles, tiles, tiles,
            jax.ShapeDtypeStruct((MIG, TILE, D), BF16),
            jax.ShapeDtypeStruct(recv.shape, BF16),
        ],
        grid_spec=pltpu.PrefetchScalarGridSpec(
            num_scalar_prefetch=2,
            grid=(),
            in_specs=[ANY, ANY, VMEM, ANY, ANY, ANY, ANY, VMEM],
            out_specs=[ANY] * 4 + [VMEM, ANY],
            scratch_shapes=[
                pieces,
                held,
                pltpu.VMEM((CL, KL + KH, TILE, TILE), BF16),
                held,
                pltpu.VMEM((D, D), BF16),
                pltpu.VMEM((D, D), BF16),
                pltpu.VMEM((ROWS, D), BF16),
                pltpu.VMEM((ROWS, D), F32),
                held,
                held,
                held,
                held,
                pieces,
                pltpu.SemaphoreType.DMA((2 * CL * KH,)),
                pltpu.SemaphoreType.DMA((3, STEPS)),
                pltpu.SemaphoreType.DMA((4, STEPS)),
                pltpu.SemaphoreType.DMA((2 * CL * KH,)),
            ],
        ),
        compiler_params=pltpu.CompilerParams(vmem_limit_bytes=VMEM_LIMIT),
    )(blocks, src, recv, home, moved, adjacency, cot, w_self, w_neigh, bias)


FOUR = 4


def final_kernel(table_ref, acc_ref, moved_ref, db_ref, dw_ref, back_ref, passed_ref, *refs):
    extra_ref, more = (refs[0], refs[-1]) if len(refs) == 14 else (None, None)
    refs = refs if extra_ref is None else refs[1:]
    out_ref, dws_ref, dwn_ref, bias_ref = refs[:4]
    acc, out, dw, back, passed, in_sem, chunk_sem, out_sem = refs[4:12]
    me = lax.axis_index("dom")
    core, chip = lax.rem(me, 2), me // 2
    steps = NDOM // FOUR
    pairs = [(back_ref, back), (passed_ref, passed)]
    if extra_ref is not None:
        pairs.append((extra_ref, more))

    def chunk(q, n):
        ref, held = pairs[n]
        some = pl.ds(q * FOUR, FOUR)
        return pltpu.make_async_copy(ref.at[some], held.at[some], chunk_sem.at[n, q])

    take_acc = pltpu.make_async_copy(acc_ref, acc, in_sem.at[0])
    take_dw = pltpu.make_async_copy(dw_ref, dw, in_sem.at[1])
    take_acc.start()

    def start(q):
        for n in range(len(pairs)):
            chunk(q, n).start()

    loop(0, 1, start)
    take_dw.start()
    loop(1, steps, start)
    bias_ref[...] = db_ref[...] * FACTOR
    take_acc.wait()
    for j in range(MIG):
        acc[OWN + j] += moved_ref[j].astype(F32)

    def add(q):
        for n in range(len(pairs)):
            chunk(q, n).wait()
        for n in range(FOUR):
            c = q * FOUR + n
            first, asked = table_ref[c, me], table_ref[c, NDOM + chip]
            other = lax.rem(asked, CL)

            @pl.when(first >= 0)
            def _():
                acc[first] += back[c, pl.ds(0, TILE)].astype(F32)

            @pl.when(jnp.logical_and(asked >= 0, asked // CL == core))
            def _():
                rows = pl.ds(pl.multiple_of(core * HALF, HALF), HALF)
                acc[other, rows] += back[c, pl.ds(TILE, HALF)].astype(F32)
                rows = pl.ds(pl.multiple_of((1 - core) * HALF, HALF), HALF)
                acc[other, rows] += passed[c].astype(F32)

            if extra_ref is not None:
                fourth = table_ref[c, NDOM + CHIPS + chip]

                @pl.when(jnp.logical_and(fourth >= 0, core == 1))
                def _():
                    acc[fourth] += more[c].astype(F32)

    loop(0, steps // 2, add)
    take_dw.wait()
    give = [
        pltpu.make_async_copy(dw.at[n], ref, out_sem.at[n])
        for n, ref in enumerate((dws_ref, dwn_ref))
    ]
    for n in range(2):
        dw[n] = dw[n] * FACTOR
        give[n].start()
    loop(steps // 2, steps, add)

    def give_out(g):
        some = pl.ds(g * GROUP, GROUP)
        return pltpu.make_async_copy(out.at[some], out_ref.at[some], out_sem.at[2 + g])

    def settle(g):
        some = pl.ds(g * GROUP, GROUP)
        out[some] = acc[some].astype(BF16)
        give_out(g).start()

    loop(0, STEPS, settle)
    for copy in give:
        copy.wait()
    loop(0, STEPS, lambda g: give_out(g).wait())


def finish(tables, acc, moved, back, passed, extra, dw, db):
    extras = [] if extra is None else [extra]
    return pl.pallas_call(
        final_kernel,
        out_shape=[
            jax.ShapeDtypeStruct((CL, TILE, D), BF16),
            jax.ShapeDtypeStruct((D, D), F32),
            jax.ShapeDtypeStruct((D, D), F32),
            jax.ShapeDtypeStruct((1, D), F32),
        ],
        grid_spec=pltpu.PrefetchScalarGridSpec(
            num_scalar_prefetch=1,
            grid=(),
            in_specs=[ANY, VMEM, VMEM, ANY, ANY, ANY] + [ANY] * len(extras),
            out_specs=[ANY, ANY, ANY, VMEM],
            scratch_shapes=[
                pltpu.VMEM((CL, TILE, D), F32),
                pltpu.VMEM((CL, TILE, D), BF16),
                pltpu.VMEM((2, D, D), F32),
                pltpu.VMEM((NDOM, WIDE, D), BF16),
                pltpu.VMEM((NDOM, HALF, D), BF16),
                pltpu.SemaphoreType.DMA((2,)),
                pltpu.SemaphoreType.DMA((3, NDOM // FOUR)),
                pltpu.SemaphoreType.DMA((2 + STEPS,)),
            ]
            + [pltpu.VMEM((NDOM, TILE, D), BF16)] * len(extras),
        ),
        compiler_params=pltpu.CompilerParams(vmem_limit_bytes=VMEM_LIMIT),
    )(tables, acc, moved, db, dw, back, passed, *extras)


def requests(owner, local):
    entries = jnp.arange(owner.shape[0], dtype=jnp.int32)
    same = owner[:, None] == owner[None, :]
    second = jnp.any(same & (entries[None, :] < entries[:, None]), axis=1)
    partner = (owner[:, None] ^ 1) == owner[None, :]
    fourth = second & (owner % 2 == 1) & jnp.any(partner & second[None, :], axis=1)
    chip = owner // 2

    column = jnp.where(second, jnp.where(fourth, NDOM + CHIPS + chip, NDOM + chip), owner)
    value = jnp.where(second & ~fourth, (owner % 2) * CL + local, local)
    hit = column[:, None] == jnp.arange(128, dtype=jnp.int32)[None, :]
    row = jnp.sum(jnp.where(hit, value[:, None] + 1, 0), axis=0) - 1
    low = jnp.where(
        fourth, UNITS * owner + 3, jnp.where(second, 2 * UNITS * chip + 2, UNITS * owner)
    )
    high = jnp.where(second & ~fourth, low + UNITS, low + 1)
    return row, jnp.stack([low, high], axis=1).reshape(-1)


def sorted_near(src):
    entries = jnp.arange(NEAR, dtype=jnp.int32)
    ahead = (src[None, :] < src[:, None]) | (
        (src[None, :] == src[:, None]) & (entries[None, :] < entries[:, None])
    )
    rank = jnp.sum(ahead.astype(jnp.int32), axis=1)
    order = jnp.sum(jnp.where(rank[None, :] == entries[:, None], entries[None, :], 0), axis=1)
    begins = jnp.sum(
        (src[None, :] < jnp.arange(CL + 1, dtype=jnp.int32)[:, None]).astype(jnp.int32), axis=1
    )
    return jnp.concatenate([order, begins])


def body(
    features, w_self, w_neigh, out_bias, cluster_plan, local_source, halo_owner, halo_local,
    adjacency, cotangent,
):
    me = lax.axis_index("dom")
    chip = me // 2
    home = features[0].reshape(CL, TILE, D)
    cot = cotangent[0].reshape(CL, TILE, D)
    src = local_source.reshape(-1)
    bias = out_bias.reshape(1, D)
    row, blocks = requests(halo_owner.reshape(-1), halo_local.reshape(-1))
    offset = (cluster_plan[OWN:] // CL - me + NDOM) % NDOM
    few = few_ways(offset)
    recv, tables, moved = lax.cond(
        few,
        functools.partial(exchange_forward, ROOMS[0]),
        functools.partial(exchange_forward, ROOMS[1]),
        cluster_plan,
        row.reshape(1, 128),
        home,
    )
    asked = tables[:, 0, :]
    order = sorted_near(src)

    def rest_of(extra, room, recv, moved):
        if extra:
            more = lax.dynamic_slice(asked, (0, NDOM + CHIPS + chip), (NDOM, 1)).reshape(-1)
            recv = fourth_forward(more, home, recv)
        new, gp, mean, gm, tail, back = middle(
            blocks, src, recv.reshape(NDOM * UNITS, HALF, D), home, moved, adjacency, cot,
            w_self, w_neigh, bias,
        )
        back = back.reshape(NDOM, FULL, D)
        ret, passed, returned, acc, dw, db = exchange_backward(
            room, cluster_plan, order, back, tail, gp, gm, mean, home, moved, adjacency, w_self
        )
        got = fourth_backward(back) if extra else None
        return new, *finish(asked, acc, returned, ret, passed, got, dw, db)

    extra = jnp.any(asked[:, NDOM + CHIPS : NDOM + 2 * CHIPS] >= 0)
    new, grad, dws, dwn, db = lax.switch(
        2 * extra.astype(jnp.int32) + 1 - few.astype(jnp.int32),
        [functools.partial(rest_of, more, room) for more in (False, True) for room in ROOMS],
        recv,
        moved,
    )
    return (
        new.reshape(1, CL * TILE, D), grad.reshape(1, CL * TILE, D), dws, dwn, db.reshape(D)
    )


def solution(mesh):
    return jax.shard_map(
        body,
        mesh=mesh,
        in_specs=(
            P("rep", "dom", None),
            P(),
            P(),
            P(),
            P("dom"),
            P("dom", None),
            P("dom", None),
            P("dom", None),
            P("dom", None, None, None),
            P("rep", "dom", None),
        ),
        out_specs=(P("rep", "dom", None), P("rep", "dom", None), P(), P(), P()),
        check_vma=False,
    )
```

```python
import functools
import math

import jax
import jax.numpy as jnp
from jax import lax
from jax.experimental import pallas as pl
from jax.experimental.pallas import tpu as pltpu
from jax.sharding import PartitionSpec as P

D = 512
TILE = 128
CL = 16
KL = 3
KH = 2
MIG = 3
OWN = CL - MIG
NDOM = 32
NREP = 4
HALF = TILE // 2
WIDE = TILE + HALF
FULL = WIDE + TILE
UNITS = FULL // HALF
CHUNK = 16
SIDE = 4
GROUP = 4
STEPS = CL // GROUP
ROWS = GROUP * TILE
VMEM_LIMIT = 60 * 2**20
FACTOR = 1.0 / math.sqrt(NDOM * NREP * CL * TILE)
MESH = pl.DeviceIdType.MESH
F32 = jnp.float32
BF16 = jnp.bfloat16

ANY = pl.BlockSpec(memory_space=pl.ANY)
VMEM = pl.BlockSpec(memory_space=pltpu.VMEM)
SMEM = pl.BlockSpec(memory_space=pltpu.SMEM)


def dot_tn(a, b):
    return lax.dot_general(a, b, (((0,), (0,)), ((), ())), preferred_element_type=F32)


def dot_nt(a, b):
    return lax.dot_general(a, b, (((1,), (1,)), ((), ())), preferred_element_type=F32)


def dot_nn(a, b):
    return jnp.dot(a, b, preferred_element_type=F32)


ZROWS = D // NREP
CHIPS = NDOM // 2
CROWS = ZROWS // CHIPS

ORDER = [
    (1, 0), (3, 0), (0, 1), (0, 3), (1, 1), (3, 3), (1, 3), (3, 1),
    (2, 0), (0, 2), (2, 2), (1, 2), (2, 1), (3, 2), (2, 3),
]
PEERS = [(0, 0, 1)] + [(dx, dy, dc) for dx, dy in ORDER for dc in (0, 1)]
NPEER = len(PEERS)


class Place:
    def __init__(self):
        self.me, self.rep = lax.axis_index("dom"), lax.axis_index("rep")
        self.core, self.chip = lax.rem(self.me, 2), self.me // 2
        self.x, self.y = lax.rem(self.chip, SIDE), self.chip // SIDE
        self.partner = self.chip * 2 + 1 - self.core

    def at(self, dx, dy, dc):
        x, y = lax.rem(self.x + dx, SIDE), lax.rem(self.y + dy, SIDE)
        return (y * SIDE + x) * 2 + lax.rem(self.core + dc, 2)


def loop(low, high, f):
    def step(t, carry):
        f(t)
        return carry

    lax.fori_loop(low, high, step, 0)


def greet_plane(here, barrier):
    def one(t):
        dom = lax.rem(here.me + t, NDOM)
        pl.semaphore_signal(barrier, inc=1, device_id=(dom, here.rep), device_id_type=MESH)

    loop(1, NDOM, one)


def remote(src, dst, send_sem, recv_sem, dom, z):
    return pltpu.make_async_remote_copy(
        src_ref=src,
        dst_ref=dst,
        send_sem=send_sem,
        recv_sem=recv_sem,
        device_id=(dom, z),
        device_id_type=MESH,
    )


class Exchange:
    def __init__(self, here, src, dst, send_sem, recv_sem, first, last):
        self.here, self.src, self.dst = here, src, dst
        self.send_sem, self.recv_sem = send_sem, recv_sem
        self.first, self.last = first, last

    def copy(self, n, rows):
        dom = self.here.at(*PEERS[n])
        return remote(
            self.src.at[dom, rows],
            self.dst.at[self.here.me, rows],
            self.send_sem.at[n],
            self.recv_sem.at[n],
            dom,
            self.here.rep,
        )

    def start(self, low, high):
        def chunk(c):
            rows = pl.ds(pl.multiple_of(self.first + c * CHUNK, CHUNK), CHUNK)
            for n in range(NPEER):
                self.copy(n, rows).start()

        loop(low, high, chunk)

    def every(self, n):
        return self.copy(n, pl.ds(self.first, self.last - self.first))


def scalar_sum(terms):
    total = jnp.int32(0)
    for term in terms:
        total = total + term
    return total


class Ring:
    def __init__(self, here, steps, axis, sign, room, buffers, sems):
        self.here, self.axis, self.room, self.sems = here, axis, room, sems
        self.steps = steps if sign > 0 else [lax.rem(SIDE - s, SIDE) for s in steps]
        self.to = (SIDE - 1, 1, 2) if sign > 0 else (1, SIDE - 1, 2)
        self.own, self.out, self.near = buffers

    def peer(self, t):
        return self.here.at(t, 0, 0) if self.axis == "x" else self.here.at(0, t, 0)

    def ways(self):
        first = 0
        for way, step in enumerate((1, SIDE - 1, 2)):
            chosen = [(s == step).astype(jnp.int32) for s in self.steps]
            rank = [scalar_sum(chosen[:j]) for j in range(MIG)]
            yield way, first, chosen, rank
            first += self.room[way]

    def copy(self, way, first):
        room = self.room[way]
        return remote(
            self.out.at[pl.ds(first, room)],
            self.near.at[pl.ds(MIG + first, room)],
            self.sems.at[0, way],
            self.sems.at[1, way],
            self.peer(self.to[way]),
            self.here.rep,
        )

    def start(self):
        for way, first, chosen, rank in self.ways():
            for k in range(self.room[way]):
                held = scalar_sum(
                    j * chosen[j] * (rank[j] == k).astype(jnp.int32) for j in range(MIG)
                )
                self.out[first + k] = self.own[held]
            self.copy(way, first).start()
        self.near[pl.ds(0, MIG)] = self.own[...]

    def finish(self):
        for way, first, _, _ in self.ways():
            self.copy(way, first).wait()

    def result(self, j):
        at = jnp.int32(j)
        for way, first, chosen, rank in self.ways():
            slot = MIG + first + jnp.minimum(rank[j], self.room[way] - 1)
            at = at + chosen[j] * (slot - j)
        return self.near[at]


class Shift:
    def __init__(self, here, plan_ref, sign, room, scratch):
        self.here = here
        ring_x, ring_y, self.lanes, self.sems = scratch[:3], scratch[3:6], scratch[6], scratch[7]
        along_x, along_y, self.swaps = [], [], []
        for j in range(MIG):
            offset = lax.rem(plan_ref[OWN + j] // CL - here.me + NDOM, NDOM)
            if sign < 0:
                offset = lax.rem(NDOM - offset, NDOM)
            swap = lax.rem(offset, 2)
            to = lax.rem(here.core + swap, 2)
            shift = offset // 2 + to * swap
            carry = (here.x + lax.rem(shift, SIDE)) // SIDE
            along_x.append(lax.rem(shift, SIDE))
            along_y.append(lax.rem(shift // SIDE + carry, SIDE))
            self.swaps.append(swap)
        self.x = Ring(here, along_x, "x", sign, room[0], ring_x, self.sems.at[0])
        self.y = Ring(here, along_y, "y", sign, room[1], ring_y, self.sems.at[1])

    def copy_lane(self):
        slot = self.lanes.at[self.here.core]
        send_sem, recv_sem = self.sems.at[2, 0, 0], self.sems.at[2, 1, 0]
        return remote(slot, slot, send_sem, recv_sem, self.here.partner, self.here.rep)

    def turn(self):
        self.x.finish()
        for j in range(MIG):
            self.y.own[j] = self.x.result(j)
        self.y.start()

    def start_lane(self):
        self.y.finish()
        for j in range(MIG):
            self.lanes[self.here.core, j] = self.y.result(j)
        self.copy_lane().start()

    def finish(self, out_ref):
        self.copy_lane().wait()
        for j in range(MIG):
            out_ref[j] = self.lanes[lax.rem(self.here.core + self.swaps[j], 2), j]


ROOMS = [((1, 2, 1), (1, 2, 2)), ((MIG,) * 3,) * 2]


def shift_scratch(room):
    rings = []
    for ways in room:
        rings += [
            pltpu.VMEM((MIG, TILE, D), BF16),
            pltpu.VMEM((sum(ways), TILE, D), BF16),
            pltpu.VMEM((MIG + sum(ways), TILE, D), BF16),
        ]
    return rings + [
        pltpu.VMEM((2, MIG, TILE, D), BF16),
        pltpu.SemaphoreType.DMA((3, 2, 3)),
    ]


def few_ways(offset):
    back = jnp.arange(2, dtype=jnp.int32)[:, None, None, None]
    core = jnp.arange(2, dtype=jnp.int32)[None, :, None, None]
    x = jnp.arange(SIDE, dtype=jnp.int32)[None, None, :, None]
    signed = jnp.where(back == 1, NDOM - offset, offset)
    swap = signed & 1
    shift = (signed >> 1) + ((core + swap) & 1) * swap
    along_x = shift & (SIDE - 1)
    along_y = ((shift >> 2) + ((x + along_x) >> 2)) & (SIDE - 1)
    axes = jnp.stack([jnp.broadcast_to(along_x, along_y.shape), along_y])
    axes = jnp.where(back == 1, (SIDE - axes) & (SIDE - 1), axes)
    crowded = jnp.zeros(axes.shape[:-1], jnp.bool_)
    for way, step in enumerate((1, SIDE - 1, 2)):
        count = sum((axes[..., j] == step).astype(jnp.int32) for j in range(MIG))
        most = [[[[ways[way]]]] for ways in ROOMS[0]]
        crowded = crowded | (count > jnp.array(most, jnp.int32))
    return ~jnp.any(crowded)


EXCHANGE_SEMS = pltpu.SemaphoreType.DMA((2, NPEER))


def forward_kernel(room, plan_ref, row_ref, home_ref, recv_ref, table_ref, moved_ref, *scratch):
    feat, stage, asked, table_sems, tile_sems, local_sems = scratch[:6]
    here = Place()
    me, core, rep = here.me, here.core, here.rep
    barrier = pltpu.get_barrier_semaphore()
    greet_plane(here, barrier)
    own = feat.at[pl.ds(core * CL, CL)]
    take = pltpu.make_async_copy(home_ref, own, local_sems.at[0])
    take.start()
    shift = Shift(here, plan_ref, 1, room, scratch[6:])
    mine = pltpu.make_async_copy(home_ref.at[pl.ds(OWN, MIG)], shift.x.own, local_sems.at[1])
    mine.start()
    table_ref[me] = row_ref[...]
    pl.semaphore_wait(barrier, NDOM - 1)

    def table(n):
        return remote(
            row_ref, table_ref.at[me], table_sems.at[0, n], table_sems.at[1, n],
            lax.rem(me + n, NDOM), rep,
        )

    loop(1, NDOM, lambda n: table(n).start())
    share = remote(home_ref, own, local_sems.at[2], local_sems.at[3], here.partner, rep)
    share.start()
    mine.wait()
    shift.x.start()
    loop(1, NDOM, lambda n: table(n).wait())
    read = pltpu.make_async_copy(table_ref, asked, local_sems.at[4])
    read.start()
    read.wait()
    take.wait()
    share.wait()

    def gather_first(low):
        def one(p):
            rows = pl.ds(low, HALF)
            stage[p, rows] = feat[core * CL + jnp.maximum(asked[p, 0, me], 0), rows]

        loop(0, NDOM, one)

    def gather_other(p):
        other = jnp.maximum(asked[p, 0, NDOM + here.chip], 0)
        stage[p, pl.ds(TILE, HALF)] = feat[other, pl.ds(pl.multiple_of(core * HALF, HALF), HALF)]

    tiles = Exchange(here, stage, recv_ref, tile_sems.at[0], tile_sems.at[1], 0, WIDE)
    gather_first(0)
    tiles.start(0, 4)
    gather_first(HALF)
    shift.turn()
    tiles.start(4, 8)
    loop(0, NDOM, gather_other)
    keep = pltpu.make_async_copy(
        stage.at[me], recv_ref.at[me, pl.ds(0, WIDE)], local_sems.at[5]
    )
    keep.start()
    shift.start_lane()
    tiles.start(8, WIDE // CHUNK)
    keep.wait()
    for n in range(NPEER):
        tiles.every(n).wait()
    shift.finish(moved_ref)


def exchange_forward(room, plan, row, home):
    return pl.pallas_call(
        functools.partial(forward_kernel, room),
        out_shape=[
            jax.ShapeDtypeStruct((NDOM, FULL, D), BF16),
            jax.ShapeDtypeStruct((NDOM, 1, 128), jnp.int32),
            jax.ShapeDtypeStruct((MIG, TILE, D), BF16),
        ],
        in_specs=[SMEM, VMEM, ANY],
        out_specs=[ANY, VMEM, VMEM],
        scratch_shapes=[
            pltpu.VMEM((2 * CL, TILE, D), BF16),
            pltpu.VMEM((NDOM, WIDE, D), BF16),
            pltpu.SMEM((NDOM, 1, 128), jnp.int32),
            pltpu.SemaphoreType.DMA((2, NDOM)),
            EXCHANGE_SEMS,
            pltpu.SemaphoreType.DMA((6,)),
        ]
        + shift_scratch(room),
        compiler_params=pltpu.CompilerParams(
            collective_id=ROOMS.index(room), has_side_effects=True, vmem_limit_bytes=VMEM_LIMIT
        ),
    )(plan, row, home)


NEAR = CL * KL


def backward_kernel(
    room, plan_ref, order_ref, back_ref, tail_ref, gp_ref, gm_ref, mean_ref, home_ref, moved_in,
    adj_ref, w_ref, ret_ref, passed_ref, moved_ref, acc_ref, out_ref, bias_ref, *scratch
):
    r1, b1, s1, r2, b2, s2, r3, b3, sums, half_sems, tile_sems, pass_sems, local_sems = scratch[:13]
    gp, gm, mean, own, adj, w, dw, db, acc, running = scratch[13:23]
    here = Place()
    me, core, chip, rep, partner = here.me, here.core, here.chip, here.rep, here.partner
    barrier = pltpu.get_barrier_semaphore()

    def z_peer(t):
        return lax.rem(rep + t, NREP)

    def chip_peer(t):
        return lax.rem(chip + t, CHIPS)

    def greet_z(t):
        pl.semaphore_signal(barrier, inc=1, device_id=(me, z_peer(t)), device_id_type=MESH)

    greet_plane(here, barrier)
    loop(1, NREP, greet_z)
    keep = pltpu.make_async_copy(
        back_ref.at[me, pl.ds(0, WIDE)], ret_ref.at[me], local_sems.at[0]
    )
    keep.start()
    loads = [
        pltpu.make_async_copy(src, dst, local_sems.at[1 + n])
        for n, (src, dst) in enumerate(
            [
                (gp_ref, gp),
                (home_ref.at[pl.ds(0, OWN)], own.at[pl.ds(0, OWN)]),
                (moved_in, own.at[pl.ds(OWN, MIG)]),
                (mean_ref, mean),
                (gm_ref, gm),
                (w_ref, w),
                (adj_ref, adj),
            ]
        )
    ]
    for copy in loads:
        copy.start()
    shift = Shift(here, plan_ref, -1, room, scratch[23:])
    shift.x.own[...] = tail_ref[...]
    pl.semaphore_wait(barrier, NDOM - 1 + NREP - 1)

    def send(src, dst, n, dom, z):
        return remote(src, dst, sums.at[0, n], sums.at[1, n], dom, z)

    halves = Exchange(here, back_ref, ret_ref, half_sems.at[0], half_sems.at[1], TILE, WIDE)
    tiles = Exchange(here, back_ref, ret_ref, tile_sems.at[0], tile_sems.at[1], 0, TILE)
    shift.x.start()
    halves.start(0, 2)

    dw[...] = jnp.zeros_like(dw)
    db[...] = jnp.zeros_like(db)
    for copy in loads[:4]:
        copy.wait()

    def weights(g):
        rows = pl.ds(g * GROUP, GROUP)
        grad = gp[rows].reshape(ROWS, D)
        dw[0] += dot_tn(own[rows].reshape(ROWS, D), grad)
        dw[1] += dot_tn(mean[rows].reshape(ROWS, D), grad)
        db[...] += jnp.sum(grad.astype(F32), axis=0, keepdims=True)

    loop(0, STEPS, weights)

    c_dw = send(dw.at[1 - core], r1, 0, partner, rep)
    c_db = send(db, b1, 1, partner, rep)
    c_dw.start()
    c_db.start()
    halves.start(2, 4)
    c_db.wait()
    c_dw.wait()
    s1[...] = dw[core] + r1[...]
    b2[rep] = db[...] + b1[...]

    def z_dw(t):
        z = z_peer(t)
        return send(s1.at[pl.ds(z * ZROWS, ZROWS)], r2.at[rep], 2 + t, me, z)

    def z_db(t):
        return send(b2.at[rep], b2.at[rep], 6 + t, me, z_peer(t))

    loop(1, NREP, lambda t: z_dw(t).start())
    loop(1, NREP, lambda t: z_db(t).start())
    r2[rep] = s1[pl.ds(pl.multiple_of(rep * ZROWS, ZROWS), ZROWS)]
    tiles.start(0, 2)
    shift.turn()

    for copy in loads[4:]:
        copy.wait()

    def kept(g):
        rows = pl.ds(g * GROUP, GROUP)
        part = dot_nt(gp[rows].reshape(ROWS, D), w[...]) + gm[rows].reshape(ROWS, D).astype(F32)
        acc[rows] = part.astype(BF16).astype(F32).reshape(GROUP, TILE, D)

    loop(0, STEPS, kept)
    acc[pl.ds(OWN, MIG)] = jnp.zeros((MIG, TILE, D), F32)

    loop(1, NREP, lambda t: z_db(t).wait())
    loop(1, NREP, lambda t: z_dw(t).wait())
    s2[...] = (r2[0] + r2[1]) + (r2[2] + r2[3])
    b3[chip] = (b2[0] + b2[1]) + (b2[2] + b2[3])

    def p_dw(t):
        q = chip_peer(t)
        return send(s2.at[pl.ds(q * CROWS, CROWS)], r3.at[chip], 10 + t, q * 2 + core, rep)

    def p_db(t):
        return send(b3.at[chip], b3.at[chip], 26 + t, chip_peer(t) * 2 + core, rep)

    loop(1, CHIPS, lambda t: p_dw(t).start())
    loop(1, CHIPS, lambda t: p_db(t).start())
    r3[chip] = s2[pl.ds(pl.multiple_of(chip * CROWS, CROWS), CROWS)]
    tiles.start(2, 4)

    running[0] = jnp.zeros((TILE, D), F32)

    def near(n):
        e = order_ref[n]
        part = dot_tn(adj[e % CL, e // CL], gm[e % CL]).astype(BF16)
        running[n + 1] = running[n] + part.astype(F32)

    loop(0, NEAR // 2, near)
    loop(1, CHIPS, lambda t: p_dw(t).wait())
    total = r3[0]
    for q in range(1, CHIPS):
        total = total + r3[q]
    mine = out_ref.at[core, pl.ds(pl.multiple_of(rep * ZROWS + chip * CROWS, CROWS), CROWS)]
    mine[...] = total

    def p_out(t):
        return send(mine, mine, 42 + t, chip_peer(t) * 2 + core, rep)

    loop(1, CHIPS, lambda t: p_out(t).start())
    shift.start_lane()
    tiles.start(4, 6)
    loop(NEAR // 2, NEAR, near)
    loop(1, CHIPS, lambda t: p_db(t).wait())
    bias = b3[0]
    for q in range(1, CHIPS):
        bias = bias + b3[q]
    bias_ref[...] = bias
    loop(1, CHIPS, lambda t: p_out(t).wait())
    block = out_ref.at[core, pl.ds(pl.multiple_of(rep * ZROWS, ZROWS), ZROWS)]

    def z_out(t):
        return send(block, block, 58 + t, me, z_peer(t))

    loop(1, NREP, lambda t: z_out(t).start())

    def pass_on(src, n):
        rows = pl.ds(TILE, HALF)
        return remote(
            ret_ref.at[src, rows], passed_ref.at[src], pass_sems.at[0, n], pass_sems.at[1, n],
            partner, rep,
        )

    keep.wait()
    pass_on(me, NPEER).start()
    for n, (dx, dy, dc) in enumerate(PEERS):
        halves.every(n).wait()
        pass_on(here.at(SIDE - dx, SIDE - dy, dc), n).start()
    tiles.start(6, TILE // CHUNK)

    def settle(h):
        acc[h] += running[order_ref[NEAR + h + 1]] - running[order_ref[NEAR + h]]

    loop(0, CL, settle)
    store = pltpu.make_async_copy(acc, acc_ref, local_sems.at[8])
    store.start()
    shift.finish(moved_ref)
    loop(1, NREP, lambda t: z_out(t).wait())
    last = send(out_ref.at[core], out_ref.at[core], 62, partner, rep)
    last.start()
    pass_on(me, NPEER).wait()
    for n, (dx, dy, dc) in enumerate(PEERS):
        pass_on(here.at(SIDE - dx, SIDE - dy, dc), n).wait()
    for n in range(NPEER):
        tiles.every(n).wait()
    last.wait()
    store.wait()


def exchange_backward(room, plan, order, back, tail, gp, gm, mean, home, moved, adjacency, w_self):
    tiles = pltpu.VMEM((CL, TILE, D), BF16)
    return pl.pallas_call(
        functools.partial(backward_kernel, room),
        out_shape=[
            jax.ShapeDtypeStruct((NDOM, WIDE, D), BF16),
            jax.ShapeDtypeStruct((NDOM, HALF, D), BF16),
            jax.ShapeDtypeStruct((MIG, TILE, D), BF16),
            jax.ShapeDtypeStruct((CL, TILE, D), F32),
            jax.ShapeDtypeStruct((2, D, D), F32),
            jax.ShapeDtypeStruct((1, D), F32),
        ],
        in_specs=[SMEM, SMEM, ANY, VMEM] + [ANY] * 7,
        out_specs=[ANY, ANY, VMEM, ANY, VMEM, VMEM],
        scratch_shapes=[
            pltpu.VMEM((D, D), F32),
            pltpu.VMEM((1, D), F32),
            pltpu.VMEM((D, D), F32),
            pltpu.VMEM((NREP, ZROWS, D), F32),
            pltpu.VMEM((NREP, 1, D), F32),
            pltpu.VMEM((ZROWS, D), F32),
            pltpu.VMEM((CHIPS, CROWS, D), F32),
            pltpu.VMEM((CHIPS, 1, D), F32),
            pltpu.SemaphoreType.DMA((2, 64)),
            EXCHANGE_SEMS,
            EXCHANGE_SEMS,
            pltpu.SemaphoreType.DMA((2, NDOM)),
            pltpu.SemaphoreType.DMA((9,)),
            tiles,
            tiles,
            tiles,
            tiles,
            pltpu.VMEM((CL, KL + KH, TILE, TILE), BF16),
            pltpu.VMEM((D, D), BF16),
            pltpu.VMEM((2, D, D), F32),
            pltpu.VMEM((1, D), F32),
            pltpu.VMEM((CL, TILE, D), F32),
            pltpu.VMEM((NEAR + 1, TILE, D), F32),
        ]
        + shift_scratch(room),
        compiler_params=pltpu.CompilerParams(
            collective_id=2 + ROOMS.index(room), has_side_effects=True, vmem_limit_bytes=VMEM_LIMIT
        ),
    )(plan, order, back, tail, gp, gm, mean, home, moved, adjacency, w_self)


def fourth_pass(back, want_ref, home_ref, buffer_ref, out_ref, stage, sems, local_sem):
    here = Place()
    me, core = here.me, here.core
    barrier = pltpu.get_barrier_semaphore()

    def peers(which):
        return [n for n in range(NPEER) if (which + PEERS[n][2]) % 2 == 1]

    every = list(range(NPEER))
    roles = []
    for which in range(2):
        served, near = every if which == 1 else [], peers(which)
        roles.append((near, served) if back else (served, near))

    for which, (_, receives) in enumerate(roles):

        @pl.when(core == which)
        def _():
            for n in receives:
                dom = here.at(SIDE - PEERS[n][0], SIDE - PEERS[n][1], PEERS[n][2])
                pl.semaphore_signal(
                    barrier, inc=1, device_id=(dom, here.rep), device_id_type=MESH
                )

    rows = pl.ds(WIDE, TILE)
    if back:
        keep = pltpu.make_async_copy(buffer_ref.at[me, rows], out_ref.at[me], local_sem.at[0])
    else:

        def gather(p):
            stage[p] = home_ref[jnp.maximum(want_ref[p], 0)]

        loop(0, NDOM, gather)
        keep = pltpu.make_async_copy(stage.at[me], out_ref.at[me, rows], local_sem.at[0])
    keep.start()

    def copy(n, low, count):
        dom = here.at(*PEERS[n])
        if back:
            src = buffer_ref.at[dom, pl.ds(WIDE + low, count)]
            dst = out_ref.at[me, pl.ds(low, count)]
        else:
            src = stage.at[dom, pl.ds(low, count)]
            dst = out_ref.at[me, pl.ds(WIDE + low, count)]
        return remote(src, dst, sems.at[0, n], sems.at[1, n], dom, here.rep)

    def run(sends, receives):
        def chunk(c):
            for n in sends:
                copy(n, pl.multiple_of(c * CHUNK, CHUNK), CHUNK).start()

        if sends:
            pl.semaphore_wait(barrier, len(sends))
            loop(0, TILE // CHUNK, chunk)
        for n in sends:
            copy(n, 0, TILE).wait_send()
        for n in receives:
            copy(n, 0, TILE).wait_recv()

    for which, (sends, receives) in enumerate(roles):

        @pl.when(core == which)
        def _():
            run(sends, receives)

    keep.wait()


def fourth_forward(want, home, recv):
    return pl.pallas_call(
        functools.partial(fourth_pass, False),
        out_shape=jax.ShapeDtypeStruct((NDOM, FULL, D), BF16),
        in_specs=[SMEM, VMEM, ANY],
        out_specs=ANY,
        input_output_aliases={2: 0},
        scratch_shapes=[
            pltpu.VMEM((NDOM, TILE, D), BF16),
            pltpu.SemaphoreType.DMA((2, NPEER)),
            pltpu.SemaphoreType.DMA((1,)),
        ],
        compiler_params=pltpu.CompilerParams(
            collective_id=4, has_side_effects=True, vmem_limit_bytes=VMEM_LIMIT
        ),
    )(want, home, recv)


def fourth_backward(back):
    def kernel(back_ref, out_ref, sems, local_sem):
        fourth_pass(True, None, None, back_ref, out_ref, None, sems, local_sem)

    return pl.pallas_call(
        kernel,
        out_shape=jax.ShapeDtypeStruct((NDOM, TILE, D), BF16),
        in_specs=[ANY],
        out_specs=ANY,
        scratch_shapes=[pltpu.SemaphoreType.DMA((2, NPEER)), pltpu.SemaphoreType.DMA((1,))],
        compiler_params=pltpu.CompilerParams(
            collective_id=5, has_side_effects=True, vmem_limit_bytes=VMEM_LIMIT
        ),
    )(back)


def middle_kernel(
    block_ref, src_ref, recv_ref, home_ref, moved_ref, adj_ref, cot_ref, ws_ref, wn_ref, bias_ref,
    new_ref, gp_ref, mean_ref, gm_ref, tail_ref, back_ref,
    halo, home, adj, cot, ws, wn, own, scale, new, gp, mean, gm, grads, halo_sem, in_sem, out_sem, back_sem,
):
    parts = 2 * KH * GROUP

    def block(n):
        return block_ref[(n % 2) * CL * KH + (n // 2 % KH) * CL + n // (2 * KH)]

    def copy_halo(n):
        return pltpu.make_async_copy(recv_ref.at[block(n)], halo.at[n], halo_sem.at[n])

    def copy_back(n):
        return pltpu.make_async_copy(grads.at[n], back_ref.at[block(n)], back_sem.at[n])

    def group(g):
        return pl.ds(g * GROUP, GROUP)

    def copy_in(g, ref, held, n):
        return pltpu.make_async_copy(ref.at[group(g)], held.at[group(g)], in_sem.at[n, g])

    def copy_out(g, n):
        held, ref = ((new, new_ref), (gp, gp_ref), (mean, mean_ref), (gm, gm_ref))[n]
        return pltpu.make_async_copy(held.at[group(g)], ref.at[group(g)], out_sem.at[n, g])

    once = [
        pltpu.make_async_copy(ref, held, in_sem.at[2, n])
        for n, (ref, held) in enumerate([(home_ref, home), (ws_ref, ws), (wn_ref, wn)])
    ]
    once[0].start()

    def start(g):
        copy_in(g, adj_ref, adj, 0).start()
        loop(0, parts, lambda n: copy_halo(g * parts + n).start())
        copy_in(g, cot_ref, cot, 1).start()

    start(0)
    once[1].start()
    once[2].start()
    loop(1, STEPS, start)
    once[0].wait()

    def step(g):
        copy_in(g, adj_ref, adj, 0).wait()
        loop(0, parts, lambda n: copy_halo(g * parts + n).wait())
        for i in range(GROUP):
            slot = g * GROUP + i
            rows = pl.ds(i * TILE, TILE)
            mine = home[slot]
            if STEPS * GROUP - GROUP + i >= OWN:
                mine = jnp.where(g == STEPS - 1, moved_ref[CL - GROUP + i - OWN], mine)
            own[rows] = mine
            tiles = jnp.concatenate([adj[slot, k] for k in range(KL + KH)], axis=1)
            total = jnp.sum(tiles.astype(F32), axis=1, keepdims=True)
            scale[rows] = jnp.broadcast_to(1.0 / (1.0 + total), (TILE, D))
            near = [home[src_ref[k * CL + slot]] for k in range(KL)]
            far = halo[pl.ds(slot * 2 * KH, 2 * KH)].reshape(KH * TILE, D)
            agg = mine.astype(F32) + dot_nn(tiles, jnp.concatenate(near + [far], axis=0))
            mean[slot] = (agg * scale[rows]).astype(BF16)
        copy_out(g, 2).start()

        @pl.when(g == 0)
        def _():
            once[1].wait()
            once[2].wait()

        pre = (
            dot_nn(own[...], ws[...])
            + dot_nn(mean[group(g)].reshape(ROWS, D), wn[...])
            + bias_ref[...]
        )
        sig = 1.0 / (1.0 + jnp.exp(-pre))
        new[group(g)] = (pre * sig).astype(BF16).reshape(GROUP, TILE, D)
        copy_out(g, 0).start()
        copy_in(g, cot_ref, cot, 1).wait()
        grad_out = cot[group(g)].reshape(ROWS, D).astype(F32)
        grad = (grad_out * sig * (1.0 + pre * (1.0 - sig))).astype(BF16)
        gp[group(g)] = grad.reshape(GROUP, TILE, D)
        copy_out(g, 1).start()
        grad_mean = (dot_nt(grad, wn[...]) * scale[...]).astype(BF16)
        gm[group(g)] = grad_mean.reshape(GROUP, TILE, D)
        copy_out(g, 3).start()
        for i in range(GROUP):
            slot = g * GROUP + i
            tiles = jnp.concatenate([adj[slot, KL + k] for k in range(KH)], axis=1)
            both = dot_tn(tiles, grad_mean[i * TILE : (i + 1) * TILE]).astype(BF16)
            grads[pl.ds(slot * 2 * KH, 2 * KH)] = both.reshape(2 * KH, HALF, D)
            for part in range(2 * KH):
                copy_back(slot * 2 * KH + part).start()

    loop(0, STEPS, step)
    first = pl.ds(OWN, MIG)
    tail = dot_nt(gp[first].reshape(MIG * TILE, D), ws[...])
    tail = tail + gm[first].reshape(MIG * TILE, D).astype(F32)
    tail_ref[...] = tail.astype(BF16).reshape(MIG, TILE, D)

    def finish(g):
        for n in range(4):
            copy_out(g, n).wait()
        loop(0, parts, lambda n: copy_back(g * parts + n).wait())

    loop(0, STEPS, finish)


def middle(blocks, src, recv, home, moved, adjacency, cot, w_self, w_neigh, bias):
    tiles = jax.ShapeDtypeStruct((CL, TILE, D), BF16)
    held = pltpu.VMEM((CL, TILE, D), BF16)
    pieces = pltpu.VMEM((2 * CL * KH, HALF, D), BF16)
    return pl.pallas_call(
        middle_kernel,
        out_shape=[
            tiles, tiles, tiles, tiles,
            jax.ShapeDtypeStruct((MIG, TILE, D), BF16),
            jax.ShapeDtypeStruct(recv.shape, BF16),
        ],
        grid_spec=pltpu.PrefetchScalarGridSpec(
            num_scalar_prefetch=2,
            grid=(),
            in_specs=[ANY, ANY, VMEM, ANY, ANY, ANY, ANY, VMEM],
            out_specs=[ANY] * 4 + [VMEM, ANY],
            scratch_shapes=[
                pieces,
                held,
                pltpu.VMEM((CL, KL + KH, TILE, TILE), BF16),
                held,
                pltpu.VMEM((D, D), BF16),
                pltpu.VMEM((D, D), BF16),
                pltpu.VMEM((ROWS, D), BF16),
                pltpu.VMEM((ROWS, D), F32),
                held,
                held,
                held,
                held,
                pieces,
                pltpu.SemaphoreType.DMA((2 * CL * KH,)),
                pltpu.SemaphoreType.DMA((3, STEPS)),
                pltpu.SemaphoreType.DMA((4, STEPS)),
                pltpu.SemaphoreType.DMA((2 * CL * KH,)),
            ],
        ),
        compiler_params=pltpu.CompilerParams(vmem_limit_bytes=VMEM_LIMIT),
    )(blocks, src, recv, home, moved, adjacency, cot, w_self, w_neigh, bias)


FOUR = 4


def final_kernel(table_ref, acc_ref, moved_ref, db_ref, dw_ref, back_ref, passed_ref, *refs):
    extra_ref, more = (refs[0], refs[-1]) if len(refs) == 14 else (None, None)
    refs = refs if extra_ref is None else refs[1:]
    out_ref, dws_ref, dwn_ref, bias_ref = refs[:4]
    acc, out, dw, back, passed, in_sem, chunk_sem, out_sem = refs[4:12]
    me = lax.axis_index("dom")
    core, chip = lax.rem(me, 2), me // 2
    steps = NDOM // FOUR
    pairs = [(back_ref, back), (passed_ref, passed)]
    if extra_ref is not None:
        pairs.append((extra_ref, more))

    def chunk(q, n):
        ref, held = pairs[n]
        some = pl.ds(q * FOUR, FOUR)
        return pltpu.make_async_copy(ref.at[some], held.at[some], chunk_sem.at[n, q])

    take_acc = pltpu.make_async_copy(acc_ref, acc, in_sem.at[0])
    take_dw = pltpu.make_async_copy(dw_ref, dw, in_sem.at[1])
    take_acc.start()

    def start(q):
        for n in range(len(pairs)):
            chunk(q, n).start()

    loop(0, 1, start)
    take_dw.start()
    loop(1, steps, start)
    bias_ref[...] = db_ref[...] * FACTOR
    take_acc.wait()
    for j in range(MIG):
        acc[OWN + j] += moved_ref[j].astype(F32)

    def add(q):
        for n in range(len(pairs)):
            chunk(q, n).wait()
        for n in range(FOUR):
            c = q * FOUR + n
            first, asked = table_ref[c, 0, me], table_ref[c, 0, NDOM + chip]
            other = lax.rem(asked, CL)

            @pl.when(first >= 0)
            def _():
                acc[first] += back[c, pl.ds(0, TILE)].astype(F32)

            @pl.when(jnp.logical_and(asked >= 0, asked // CL == core))
            def _():
                rows = pl.ds(pl.multiple_of(core * HALF, HALF), HALF)
                acc[other, rows] += back[c, pl.ds(TILE, HALF)].astype(F32)
                rows = pl.ds(pl.multiple_of((1 - core) * HALF, HALF), HALF)
                acc[other, rows] += passed[c].astype(F32)

            if extra_ref is not None:
                fourth = table_ref[c, 0, NDOM + CHIPS + chip]

                @pl.when(jnp.logical_and(fourth >= 0, core == 1))
                def _():
                    acc[fourth] += more[c].astype(F32)

    loop(0, steps // 2, add)
    take_dw.wait()
    give = [
        pltpu.make_async_copy(dw.at[n], ref, out_sem.at[n])
        for n, ref in enumerate((dws_ref, dwn_ref))
    ]
    for n in range(2):
        dw[n] = dw[n] * FACTOR
        give[n].start()
    loop(steps // 2, steps, add)

    def give_out(g):
        some = pl.ds(g * GROUP, GROUP)
        return pltpu.make_async_copy(out.at[some], out_ref.at[some], out_sem.at[2 + g])

    def settle(g):
        some = pl.ds(g * GROUP, GROUP)
        out[some] = acc[some].astype(BF16)
        give_out(g).start()

    loop(0, STEPS, settle)
    for copy in give:
        copy.wait()
    loop(0, STEPS, lambda g: give_out(g).wait())


def finish(tables, acc, moved, back, passed, extra, dw, db):
    extras = [] if extra is None else [extra]
    return pl.pallas_call(
        final_kernel,
        out_shape=[
            jax.ShapeDtypeStruct((CL, TILE, D), BF16),
            jax.ShapeDtypeStruct((D, D), F32),
            jax.ShapeDtypeStruct((D, D), F32),
            jax.ShapeDtypeStruct((1, D), F32),
        ],
        grid_spec=pltpu.PrefetchScalarGridSpec(
            num_scalar_prefetch=1,
            grid=(),
            in_specs=[ANY, VMEM, VMEM, ANY, ANY, ANY] + [ANY] * len(extras),
            out_specs=[ANY, ANY, ANY, VMEM],
            scratch_shapes=[
                pltpu.VMEM((CL, TILE, D), F32),
                pltpu.VMEM((CL, TILE, D), BF16),
                pltpu.VMEM((2, D, D), F32),
                pltpu.VMEM((NDOM, WIDE, D), BF16),
                pltpu.VMEM((NDOM, HALF, D), BF16),
                pltpu.SemaphoreType.DMA((2,)),
                pltpu.SemaphoreType.DMA((3, NDOM // FOUR)),
                pltpu.SemaphoreType.DMA((2 + STEPS,)),
            ]
            + [pltpu.VMEM((NDOM, TILE, D), BF16)] * len(extras),
        ),
        compiler_params=pltpu.CompilerParams(vmem_limit_bytes=VMEM_LIMIT),
    )(tables, acc, moved, db, dw, back, passed, *extras)


def requests(owner, local):
    entries = jnp.arange(owner.shape[0], dtype=jnp.int32)
    same = owner[:, None] == owner[None, :]
    second = jnp.any(same & (entries[None, :] < entries[:, None]), axis=1)
    partner = (owner[:, None] ^ 1) == owner[None, :]
    fourth = second & (owner % 2 == 1) & jnp.any(partner & second[None, :], axis=1)
    chip = owner // 2

    column = jnp.where(second, jnp.where(fourth, NDOM + CHIPS + chip, NDOM + chip), owner)
    value = jnp.where(second & ~fourth, (owner % 2) * CL + local, local)
    hit = column[:, None] == jnp.arange(128, dtype=jnp.int32)[None, :]
    row = jnp.sum(jnp.where(hit, value[:, None] + 1, 0), axis=0) - 1
    low = jnp.where(
        fourth, UNITS * owner + 3, jnp.where(second, 2 * UNITS * chip + 2, UNITS * owner)
    )
    high = jnp.where(second & ~fourth, low + UNITS, low + 1)
    return row, jnp.concatenate([low, high])


def sorted_near(src):
    entries = jnp.arange(NEAR, dtype=jnp.int32)
    ahead = (src[None, :] < src[:, None]) | (
        (src[None, :] == src[:, None]) & (entries[None, :] < entries[:, None])
    )
    rank = jnp.sum(ahead.astype(jnp.int32), axis=1)
    order = jnp.sum(jnp.where(rank[None, :] == entries[:, None], entries[None, :], 0), axis=1)
    begins = jnp.sum(
        (src[None, :] < jnp.arange(CL + 1, dtype=jnp.int32)[:, None]).astype(jnp.int32), axis=1
    )
    return jnp.concatenate([order, begins])


def body(
    features, w_self, w_neigh, out_bias, cluster_plan, local_source, halo_owner, halo_local,
    adjacency, cotangent,
):
    me = lax.axis_index("dom")
    chip = me // 2
    home = features[0].reshape(CL, TILE, D)
    cot = cotangent[0].reshape(CL, TILE, D)
    src = local_source.T.reshape(-1)
    bias = out_bias.reshape(1, D)
    row, blocks = requests(halo_owner.T.reshape(-1), halo_local.T.reshape(-1))
    offset = (cluster_plan[OWN:] // CL - me + NDOM) % NDOM
    few = few_ways(offset)
    recv, tables, moved = lax.cond(
        few,
        functools.partial(exchange_forward, ROOMS[0]),
        functools.partial(exchange_forward, ROOMS[1]),
        cluster_plan,
        row.reshape(1, 128),
        home,
    )
    order = sorted_near(src)

    def rest_of(extra, room, recv, moved):
        if extra:
            more = lax.dynamic_slice(
                tables, (0, 0, NDOM + CHIPS + chip), (NDOM, 1, 1)
            ).reshape(-1)
            recv = fourth_forward(more, home, recv)
        new, gp, mean, gm, tail, back = middle(
            blocks, src, recv.reshape(NDOM * UNITS, HALF, D), home, moved, adjacency, cot,
            w_self, w_neigh, bias,
        )
        back = back.reshape(NDOM, FULL, D)
        ret, passed, returned, acc, dw, db = exchange_backward(
            room, cluster_plan, order, back, tail, gp, gm, mean, home, moved, adjacency, w_self
        )
        got = fourth_backward(back) if extra else None
        return new, *finish(tables, acc, returned, ret, passed, got, dw, db)

    extra = jnp.any(tables[:, :, NDOM + CHIPS : NDOM + 2 * CHIPS] >= 0)
    new, grad, dws, dwn, db = lax.switch(
        2 * extra.astype(jnp.int32) + 1 - few.astype(jnp.int32),
        [functools.partial(rest_of, more, room) for more in (False, True) for room in ROOMS],
        recv,
        moved,
    )
    return (
        new.reshape(1, CL * TILE, D), grad.reshape(1, CL * TILE, D), dws, dwn, db.reshape(D)
    )


def solution(mesh):
    return jax.shard_map(
        body,
        mesh=mesh,
        in_specs=(
            P("rep", "dom", None),
            P(),
            P(),
            P(),
            P("dom"),
            P("dom", None),
            P("dom", None),
            P("dom", None),
            P("dom", None, None, None),
            P("rep", "dom", None),
        ),
        out_specs=(P("rep", "dom", None), P("rep", "dom", None), P(), P(), P()),
        check_vma=False,
    )
```
